32 devices in a mesh: dp: 8 (over y, x, core), section: 4 (over z).
Axes of the slice: x: 2, y: 2, z: 4, core: 2. Of those that a mesh axis runs over, the one named last changes fastest.
Arguments:
- tokens: bfloat16 [32, 1024, 512], P('dp'), may hold values from -6 to 6
- resets: int32 [32, 1024], P('dp'), may hold values 0 or 1
- init_states: float32 [2, 32, 1024], P(None, 'dp'), may hold values from -6 to 6
- cotangent: bfloat16 [32, 1024, 512], P('dp'), may hold values from -6 to 6
- mix_gain: float32 [2, 512], replicated, may hold values from 0.5 to 1.5
- mix_in: bfloat16 [2, 512, 2048], replicated, may hold values from -0.25 to 0.25
- conv_weight: float32 [2, 4, 2048], replicated, may hold values from -3 to 3
- conv_bias: float32 [2, 2048], replicated, may hold values from -4.5 to 1.2
- mix_out: bfloat16 [2, 1024, 512], replicated, may hold values from -0.1875 to 0.1875
- mlp_gain: float32 [2, 512], replicated, may hold values from 0.5 to 1.5
- mlp_up: bfloat16 [2, 512, 2048], replicated, may hold values from -0.25 to 0.25
- up_bias: float32 [2, 2048], replicated, may hold values from -3 to 3
- mlp_down: bfloat16 [2, 2048, 512], replicated, may hold values from -0.125 to 0.125
- down_bias: float32 [2, 512], replicated, may hold values from -3 to 3
Outputs:
- activations: bfloat16 [4, 32, 1024, 512], P('section', 'dp')
- input_grads: bfloat16 [4, 32, 1024, 512], P('section', 'dp')
- final_states: float32 [2, 32, 1024], P(None, 'dp', 'section')
- mix_gain_grad: float32 [2, 512], P(None, ('dp', 'section'))
- mix_in_grad: float32 [2, 512, 2048], P(None, ('dp', 'section'))
- conv_weight_grad: float32 [2, 4, 2048], P(None, None, ('dp', 'section'))
- conv_bias_grad: float32 [2, 2048], P(None, ('dp', 'section'))
- mix_out_grad: float32 [2, 1024, 512], P(None, None, ('dp', 'section'))
- mlp_gain_grad: float32 [2, 512], P(None, ('dp', 'section'))
- mlp_up_grad: float32 [2, 512, 2048], P(None, ('dp', 'section'))
- up_bias_grad: float32 [2, 2048], P(None, ('dp', 'section'))
- mlp_down_grad: float32 [2, 2048, 512], P(None, None, ('dp', 'section'))
- down_bias_grad: float32 [2, 512], P(None, ('dp', 'section'))
The draws below stay inside these ranges and needn't reach their ends.
All inputs are finite; a program needn't handle non-finite values. No bound on the sum of `resets` on one device may be relied on, other than what follows from the above.
Results may differ from the reference program's by a relative error of at most 0.012.
Values may be sent and summed in bfloat16 or wider, within the bound.
A program may use at most 640 MiB of HBM per device.

```python
import jax
import jax.numpy as jnp
from jax import lax

D = 512
HID = 1024
FF = 2048
TAPS = 4
LAYERS = 2
SEQ = 1024
ROWS = 32


def draw_conv_bias(key, part):
    gate_key, cand_key = jax.random.split(key)
    gate_part = jax.random.uniform(gate_key, (LAYERS, HID), jnp.float32, -4.5, 0.5)
    candidate = jnp.clip(0.3 * jax.random.normal(cand_key, (LAYERS, HID), jnp.float32), -1.2, 1.2)
    return jnp.concatenate([gate_part, candidate], axis=1)


def place_ends(values, stream_key, low, largest):
    longest = values.shape.index(max(values.shape))
    spots = []
    for shift in (0, 1):
        where = [jax.random.randint(jax.random.fold_in(stream_key, axis), (), 0, length) for axis, length in enumerate(values.shape)]
        where[longest] = (where[longest] + shift) % values.shape[longest]
        spots.append(tuple(where))
    return values.at[spots[0]].set(low).at[spots[1]].set(largest)


def block_levels(own_key, dims, cuts, smallest, top_value):
    level = 1.0
    for axis_at, parts in cuts:
        steps = jax.random.uniform(jax.random.fold_in(jax.random.fold_in(own_key, 6), axis_at), (parts,), jnp.float32, smallest / len(cuts), top_value / len(cuts))
        level = level * jnp.repeat(jnp.exp(steps), dims[axis_at] // parts).reshape((-1,) + (1,) * (len(dims) - 1 - axis_at))
    return level


def noise(own_key, extent, width, reach, pieces=(), kind=jnp.bfloat16):
    array = width * jax.random.normal(own_key, extent, jnp.float32)
    if pieces:
        array = array * block_levels(own_key, extent, pieces, -0.22, 0.18)
    return jnp.clip(array, -reach, reach).astype(kind)


def setup_inputs(seed: int = 0) -> dict:
    arg_keys = jax.random.split(jax.random.key(seed), 15)
    tokens = noise(arg_keys[0], (ROWS, SEQ, D), 1.0, 6.0, ((0, 8),))
    resets = place_ends((jax.random.randint(arg_keys[1], (ROWS, SEQ), 0, 256) < 1).astype(jnp.int32), jax.random.fold_in(arg_keys[1], 1), 0, 1)
    init_states = noise(arg_keys[2], (LAYERS, ROWS, HID), 1.0, 6.0, ((1, 8),), jnp.float32)
    cotangent = noise(arg_keys[3], (ROWS, SEQ, D), 1.0, 6.0, ((0, 8),))
    mix_gain = jnp.clip(1.0 + 0.1 * jax.random.normal(arg_keys[4], (LAYERS, D), jnp.float32), 0.5, 1.5)
    mix_in = noise(arg_keys[5], (LAYERS, D, 2 * HID), D ** -0.5, 0.25)
    conv_weight = noise(arg_keys[6], (LAYERS, TAPS, 2 * HID), TAPS ** -0.5, 3.0, (), jnp.float32)
    conv_bias = draw_conv_bias(jax.random.fold_in(arg_keys[14], 71), 0)
    mix_out = noise(arg_keys[8], (LAYERS, HID, D), HID ** -0.5, 0.1875)
    mlp_gain = jnp.clip(1.0 + 0.1 * jax.random.normal(arg_keys[9], (LAYERS, D), jnp.float32), 0.5, 1.5)
    mlp_up = noise(arg_keys[10], (LAYERS, D, FF), D ** -0.5, 0.25)
    up_bias = noise(arg_keys[11], (LAYERS, FF), 0.5, 3.0, (), jnp.float32)
    mlp_down = noise(arg_keys[12], (LAYERS, FF, D), FF ** -0.5, 0.125)
    down_bias = noise(arg_keys[13], (LAYERS, D), 0.5, 3.0, (), jnp.float32)
    return dict(tokens=tokens, resets=resets, init_states=init_states, cotangent=cotangent, mix_gain=mix_gain, mix_in=mix_in, conv_weight=conv_weight, conv_bias=conv_bias, mix_out=mix_out, mlp_gain=mlp_gain, mlp_up=mlp_up, up_bias=up_bias, mlp_down=mlp_down, down_bias=down_bias)


EPSILON = 1e-06
HIGHEST_MODE = lax.Precision.HIGHEST

@jax.custom_vjp
def low(v):
    return lax.optimization_barrier(v.astype(jnp.bfloat16)).astype(jnp.float32)

@jax.custom_vjp
def low_back(v):
    return v

def low_keep(v):
    return (low(v), None)

def low_pass(kept, grad):
    return (grad,)

def back_keep(v):
    return (v, None)

def back_low(kept, grad):
    return (low(grad),)
low.defvjp(low_keep, low_pass)
low_back.defvjp(back_keep, back_low)

def scaled_norm(values, norm_gain):
    return values * lax.rsqrt(lax.optimization_barrier(jnp.mean(values * values, axis=-1, keepdims=True)) + EPSILON) * norm_gain

def delay(values, amount):
    return jnp.concatenate([jnp.zeros_like(values[..., :amount, :]), values[..., :-amount, :]], axis=-2)

def delay_ones(values, amount):
    return jnp.concatenate([jnp.ones_like(values[..., :amount, :]), values[..., :-amount, :]], axis=-2)

def linear_chain(earlier, latter):
    return (earlier[0] * latter[0], latter[0] * earlier[1] + latter[1])

def recurrence(projected, kernel, shift_bias, initial, continuing):
    convolved = shift_bias + kernel[0] * projected
    window = continuing
    for offset in range(1, kernel.shape[0]):
        if offset > 1:
            window = window * delay_ones(continuing, offset - 1)
        convolved = convolved + kernel[offset] * window * delay(projected, offset)
    midpoint = projected.shape[-1] // 2
    update = jax.nn.sigmoid(convolved[..., :midpoint])
    candidate = convolved[..., midpoint:]
    retain = (1.0 - update) * continuing
    inject = update * candidate
    opening = inject[..., :1, :] + retain[..., :1, :] * initial[..., None, :]
    inject = jnp.concatenate([opening, inject[..., 1:, :]], axis=-2)
    return lax.associative_scan(linear_chain, (retain, inject), axis=projected.ndim - 2)[1]

def smooth_gate(values):
    return jax.nn.gelu(values, approximate=True)

def dot_high(left, right):
    return jnp.dot(left, right, precision=HIGHEST_MODE, preferred_element_type=jnp.float32)

def mixer_layer(inputs, continuing, initial, norm_gain, weight_in, kernel, shift_bias, weight_out):
    normed = low(scaled_norm(inputs, norm_gain))
    projected = low_back(dot_high(normed, weight_in))
    hidden = recurrence(projected, kernel, shift_bias, initial, continuing)
    return (inputs + dot_high(low(hidden), weight_out), hidden[-1])

def mlp_layer(inputs, norm_gain, weight_up, bias_up, weight_down, bias_down):
    normed = low(scaled_norm(inputs, norm_gain))
    pre_act = low_back(dot_high(normed, weight_up) + bias_up)
    active = low(smooth_gate(pre_act))
    return inputs + dot_high(active, weight_down) + bias_down

def residual_block(params, first_input, continuing, initials, errors):
    gains_mix, weights_in, kernels, shift_biases, weights_out, gains_mlp, weights_up, biases_up, weights_down, biases_down = params
    current = first_input
    outputs = []
    finals = []
    for position in range(4):
        current = low_back(current + errors[position])
        layer_no = position // 2
        if position % 2 == 0:
            result, final_state = mixer_layer(current, continuing, initials[layer_no], gains_mix[layer_no], weights_in[layer_no], kernels[layer_no], shift_biases[layer_no], weights_out[layer_no])
            finals.append(final_state)
        else:
            result = mlp_layer(current, gains_mlp[layer_no], weights_up[layer_no], biases_up[layer_no], weights_down[layer_no], biases_down[layer_no])
        current = low(result)
        outputs.append(current)
    return (jnp.stack(outputs), jnp.stack(finals))

def reference(tokens, resets, init_states, cotangent, mix_gain, mix_in, conv_weight, conv_bias, mix_out, mlp_gain, mlp_up, up_bias, mlp_down, down_bias):
    params = tuple((item.astype(jnp.float32) for item in (mix_gain, mix_in, conv_weight, conv_bias, mix_out, mlp_gain, mlp_up, up_bias, mlp_down, down_bias)))
    continuing_all = (1 - resets).astype(jnp.float32)[..., None]
    initials_rows = jnp.transpose(init_states, (1, 0, 2))
    zero_grads = jax.tree.map(jnp.zeros_like, params)

    def row_step(totals, row_inputs):
        first_input, continuing, initials, row_cot = row_inputs
        errors = jnp.zeros((4,) + first_input.shape, jnp.float32)

        def forward(weights, perturb):
            return residual_block(weights, first_input, continuing, initials, perturb)
        (outputs, finals), pullback = jax.vjp(forward, params, errors)
        pull_input = jnp.concatenate([jnp.zeros_like(outputs[:3]), row_cot[None]], axis=0)
        weight_grads, error_grads = pullback((pull_input, jnp.zeros_like(finals)))
        totals = jax.tree.map(jnp.add, totals, weight_grads)
        return (totals, (outputs.astype(jnp.bfloat16), error_grads.astype(jnp.bfloat16), finals))
    totals, (outputs, error_grads, finals) = lax.scan(row_step, zero_grads, (tokens.astype(jnp.float32), continuing_all, initials_rows, cotangent.astype(jnp.float32)))
    activations = jnp.transpose(outputs, (1, 0, 2, 3))
    input_grads = jnp.transpose(error_grads, (1, 0, 2, 3))
    final_states = jnp.transpose(finals, (1, 0, 2))
    return (activations, input_grads, final_states, totals[0], totals[1], totals[2], totals[3], totals[4], totals[5], totals[6], totals[7], totals[8], totals[9])
```

```python
import functools

import jax
import jax.numpy as jnp
from jax import lax
from jax.experimental import pallas as pl
from jax.experimental.pallas import tpu as pltpu
from jax.sharding import PartitionSpec as P

EPSILON = 1e-06
LANES = 128
GROUP = 8
TILE_C = 256
TILE_F = 512
BIG = 256
F32 = jnp.float32
BF16 = jnp.bfloat16
ROOT_2_PI = 0.7978845608028654
CUBIC = 0.044715


def dot_nn(left, right):
    return jnp.dot(left, right, preferred_element_type=F32)


def dot_nt(left, right):
    return lax.dot_general(left, right, (((1,), (1,)), ((), ())), preferred_element_type=F32)


def rows_loop(total, step, fn):
    def at(index, carry):
        fn(pl.ds(pl.multiple_of(index * step, step), step))
        return carry

    lax.fori_loop(0, total // step, at, 0)


def to_chunks(natural, target):
    stride = natural.shape[1] // GROUP

    def at(index, carry):
        for tile in range(natural.shape[0]):
            first = natural[tile, pl.ds(2 * index, GROUP, stride=stride), :]
            second = natural[tile, pl.ds(2 * index + 1, GROUP, stride=stride), :]
            both = jnp.concatenate([first, second], axis=0).astype(BF16)
            target[pl.ds(pl.multiple_of(index * 16, 16), 16), pl.ds(tile * LANES, LANES)] = both
        return carry

    lax.fori_loop(0, stride // 2, at, 0)


def to_tokens(chunked, natural):
    stride = natural.shape[1] // GROUP

    def at(index, carry):
        for tile in range(natural.shape[0]):
            rows = pl.ds(pl.multiple_of(index * GROUP, GROUP), GROUP)
            natural[tile, pl.ds(index, GROUP, stride=stride), :] = chunked[rows, pl.ds(tile * LANES, LANES)]
        return carry

    lax.fori_loop(0, stride, at, 0)


def transpose_into(source, target):
    def at(index, carry):
        rows = pl.ds(pl.multiple_of(index * LANES, LANES), LANES)
        target[:, rows] = source[rows, :].astype(F32).T.astype(BF16)
        return carry

    lax.fori_loop(0, source.shape[0] // LANES, at, 0)


def inverse_rms(values):
    return lax.rsqrt(jnp.mean(values * values, axis=-1, keepdims=True) + EPSILON)


def put_tiles(natural, rows, values):
    for tile in range(natural.shape[0]):
        natural[tile, rows, :] = values[:, tile * LANES : (tile + 1) * LANES]


def get_tiles(natural, rows):
    return jnp.concatenate([natural[tile, rows, :] for tile in range(natural.shape[0])], axis=1)


def norm_into(x_ref, gain_ref, target):
    def at(rows):
        source = x_ref[rows, :].astype(F32)
        result = source * inverse_rms(source) * gain_ref[...]
        if len(target.shape) == 3:
            put_tiles(target, rows, result)
        else:
            target[rows, :] = result.astype(target.dtype)

    rows_loop(x_ref.shape[0], 128, at)


def previous_chunk(values, first_row):
    rolled = pltpu.roll(values, 1, 0)
    position = lax.broadcasted_iota(jnp.int32, values.shape, 0)
    return jnp.where(position == 0, first_row, rolled)


def following_chunk(values):
    rolled = pltpu.roll(values, GROUP - 1, 0)
    position = lax.broadcasted_iota(jnp.int32, values.shape, 0)
    return jnp.where(position == GROUP - 1, 0.0, rolled)


def sigmoid(values):
    return 0.5 * jnp.tanh(0.5 * values) + 0.5


def repeat_rows(values, rows):
    return jnp.concatenate([values] * (rows // values.shape[0]), axis=0)


STEP = 32
SPLIT = 64
HALO = 24


def mixer_forward_kernel(
    x_ref, gain_ref, wg_ref, wc_ref, kg_ref, kc_ref, bg_ref, bc_ref, wo_ref, mask_ref, init_ref,
    y_ref, p_ref, z_ref, cand_ref, h_ref, final_ref,
    normed, natural, total, proj, local, decay,
):
    step = pl.program_id(0)
    seq = x_ref.shape[0]
    width = wg_ref.shape[1]

    @pl.when(step == 0)
    def _():
        norm_into(x_ref, gain_ref, natural)
        to_chunks(natural, normed)
        total[...] = jnp.zeros_like(total)

    def project(index, carry):
        rows = pl.ds(pl.multiple_of(index * BIG, BIG), BIG)
        out_rows = pl.ds(pl.multiple_of(index * BIG + HALO, GROUP), BIG)
        block = normed[rows, :]
        for side, weight in enumerate((wg_ref, wc_ref)):
            lanes = pl.ds(side * width, width)
            piece = dot_nn(block, weight[...])
            proj[out_rows, lanes] = piece
            p_ref[0, rows, lanes] = piece.astype(BF16)
        return carry

    lax.fori_loop(0, seq // BIG, project, 0)
    for offset in range(3):
        last = proj[pl.ds(seq + GROUP * offset, GROUP), :]
        proj[pl.ds(GROUP * offset, GROUP), :] = previous_chunk(last, 0.0)

    def scan_step(index, carry):
        base = pl.multiple_of(index * STEP, STEP)
        rows = pl.ds(base, STEP)
        masks = [None] + [mask_ref[k, rows, :] for k in range(3)]
        updated = []
        for tile in range(width // LANES):
            lanes = pl.ds(tile * LANES, LANES)

            def convolve(shift, taps, bias):
                value = bias[0:1, lanes]
                for k in range(4):
                    at = pl.ds(pl.multiple_of(base + HALO - GROUP * k, GROUP), STEP)
                    term = proj[at, pl.ds(shift + tile * LANES, LANES)]
                    if k:
                        term = term * masks[k]
                    value = value + taps[k : k + 1, lanes] * term
                return value

            update = sigmoid(convolve(0, kg_ref, bg_ref))
            candidate = convolve(width, kc_ref, bc_ref)
            z_ref[rows, lanes] = update.astype(BF16)
            cand_ref[rows, lanes] = candidate.astype(BF16)
            retain = (1.0 - update) * masks[1]
            inject = update * candidate
            state, product = carry[tile]
            states, products = [], []
            for g in range(STEP // GROUP):
                here = slice(g * GROUP, (g + 1) * GROUP)
                state = retain[here] * state + inject[here]
                product = retain[here] * product
                states.append(state)
                products.append(product)
            local[rows, lanes] = jnp.concatenate(states, axis=0)
            decay[rows, lanes] = jnp.concatenate(products, axis=0)
            updated.append((state, product))
        return tuple(updated)

    zero = jnp.zeros((GROUP, LANES), F32)
    one = jnp.ones((GROUP, LANES), F32)
    ends = lax.fori_loop(0, seq // STEP, scan_step, ((zero, one),) * (width // LANES))
    entries = []
    for tile, (state, product) in enumerate(ends):
        lanes = pl.ds(tile * LANES, LANES)
        current = init_ref[0:1, lanes]
        starts = []
        for g in range(GROUP):
            starts.append(current)
            current = product[g : g + 1] * current + state[g : g + 1]
        final_ref[0:1, lanes] = current
        entries.append(jnp.concatenate(starts, axis=0))
    entry = repeat_rows(jnp.concatenate(entries, axis=1), STEP)

    def fix(index, carry):
        rows = pl.ds(pl.multiple_of(index * STEP, STEP), STEP)
        h_ref[rows, :] = (local[rows, :] + decay[rows, :] * entry).astype(BF16)
        return carry

    lax.fori_loop(0, seq // STEP, fix, 0)

    def output(rows):
        total[rows, :] += dot_nn(h_ref[rows, :], wo_ref[...])

    rows_loop(seq, BIG, output)

    @pl.when(step == pl.num_programs(0) - 1)
    def _():
        to_tokens(total, natural)

        def finish(rows):
            y_ref[rows, :] = (x_ref[rows, :].astype(F32) + get_tiles(natural, rows)).astype(BF16)

        rows_loop(seq, 128, finish)


def norm_backward(x_ref, g_ref, gain_ref, grad_normed, dx_ref, dgain_ref):
    gain = gain_ref[...]

    def at(index, carry):
        rows = pl.ds(pl.multiple_of(index * 64, 64), 64)
        source = x_ref[rows, :].astype(F32)
        upstream = g_ref[rows, :].astype(F32)
        incoming = get_tiles(grad_normed, rows) if len(grad_normed.shape) == 3 else grad_normed[rows, :]
        scale = inverse_rms(source)
        scaled = gain * incoming
        mean = jnp.mean(source * scaled, axis=-1, keepdims=True)
        result = upstream + scale * scaled - source * (scale * scale * scale * mean)
        dx_ref[rows, :] = result.astype(BF16)
        return carry + jnp.sum(incoming * source * scale, axis=0, keepdims=True)

    dgain_ref[...] = lax.fori_loop(0, x_ref.shape[0] // 64, at, jnp.zeros(gain.shape, F32))


def put_halves(keep_ref, send_ref, bit_ref, index, lanes, values):
    low = values[:SPLIT].astype(BF16)
    high = values[SPLIT:].astype(BF16)
    mine = bit_ref[0] == 1
    rows = pl.ds(pl.multiple_of(index * SPLIT, SPLIT), SPLIT)
    keep_ref[0, rows, lanes] = jnp.where(mine, high, low)
    send_ref[0, rows, lanes] = jnp.where(mine, low, high)


def mixer_backward_kernel(
    x_ref, g_ref, gain_ref, wg_ref, wc_ref, kg_ref, kc_ref, wo_ref, mask_ref, init_ref,
    p_ref, z_ref, cand_ref, h_ref, bit_ref,
    dx_ref, keep_ref, send_ref, small_ref, dgain_ref,
    normed_t, upstream, upstream_t, natural, total, local, decay, dconv, dproj,
):
    step = pl.program_id(0)
    seq = x_ref.shape[0]
    width = wg_ref.shape[1]
    tiles = width // LANES

    @pl.when(step == 0)
    def _():
        norm_into(x_ref, gain_ref, natural)
        to_chunks(natural, upstream)
        transpose_into(upstream, normed_t)

        def widen(rows):
            put_tiles(natural, rows, g_ref[rows, :].astype(F32))

        rows_loop(seq, 128, widen)
        to_chunks(natural, upstream)
        transpose_into(upstream, upstream_t)
        total[...] = jnp.zeros_like(total)

    def back_hidden(rows):
        local[rows, :] = dot_nt(upstream[rows, :], wo_ref[...])

    rows_loop(seq, BIG, back_hidden)

    def scan_step(index, carry):
        rows = pl.ds(pl.multiple_of(seq - STEP - index * STEP, STEP), STEP)
        keep = mask_ref[0, rows, :]
        updated = []
        for tile in range(tiles):
            lanes = pl.ds(tile * LANES, LANES)
            retain = (1.0 - z_ref[rows, lanes].astype(F32)) * keep
            grads = local[rows, lanes]
            chain, product = carry[tile]
            chains, products = [], []
            for g in reversed(range(STEP // GROUP)):
                here = slice(g * GROUP, (g + 1) * GROUP)
                value = grads[here] + chain
                chains.append(value)
                products.append(product)
                chain = retain[here] * value
                product = retain[here] * product
            local[rows, lanes] = jnp.concatenate(chains[::-1], axis=0)
            decay[rows, lanes] = jnp.concatenate(products[::-1], axis=0)
            updated.append((chain, product))
        return tuple(updated)

    zero = jnp.zeros((GROUP, LANES), F32)
    one = jnp.ones((GROUP, LANES), F32)
    ends = lax.fori_loop(0, seq // STEP, scan_step, ((zero, one),) * tiles)
    entries = []
    for chain, product in ends:
        current = jnp.zeros((1, LANES), F32)
        starts = [current]
        for g in reversed(range(1, GROUP)):
            current = chain[g : g + 1] + product[g : g + 1] * current
            starts.append(current)
        entries.append(jnp.concatenate(starts[::-1], axis=0))

    last_rows = h_ref[pl.ds(seq - 16, 16), :].astype(F32)[GROUP:]
    before = previous_chunk(last_rows, init_ref[0:1, :])

    def gates(index, carry):
        base = pl.multiple_of(index * STEP, STEP)
        rows = pl.ds(base, STEP)
        keep = mask_ref[0, rows, :]
        updated = []
        for tile in range(tiles):
            lanes = pl.ds(tile * LANES, LANES)
            hidden = h_ref[rows, lanes].astype(F32)
            delayed = jnp.concatenate([carry[tile], hidden[: STEP - GROUP]], axis=0)
            error = local[rows, lanes] + decay[rows, lanes] * repeat_rows(entries[tile], STEP)
            update = z_ref[rows, lanes].astype(F32)
            candidate = cand_ref[rows, lanes].astype(F32)
            slope = error * (candidate - keep * delayed)
            dconv[rows, lanes] = slope * (update * (1.0 - update))
            dconv[rows, pl.ds(width + tile * LANES, LANES)] = update * error
            updated.append(hidden[STEP - GROUP :])
        return tuple(updated)

    starting = tuple(before[:, tile * LANES : (tile + 1) * LANES] for tile in range(tiles))
    lax.fori_loop(0, seq // STEP, gates, starting)
    for offset in range(3):
        first = dconv[pl.ds(GROUP * offset, GROUP), :]
        dconv[pl.ds(seq + GROUP * offset, GROUP), :] = following_chunk(first)

    def fold(values):
        result = values[0:GROUP]
        for g in range(1, STEP // GROUP):
            result = result + values[g * GROUP : (g + 1) * GROUP]
        return result

    for side, taps in enumerate((kg_ref, kc_ref)):

        def spread(index, carry):
            base = pl.multiple_of(index * STEP, STEP)
            rows = pl.ds(base, STEP)
            updated = []
            for tile in range(tiles):
                lanes = pl.ds(side * width + tile * LANES, LANES)
                weights = pl.ds(tile * LANES, LANES)
                projected = p_ref[0, rows, lanes].astype(F32)
                sums = carry[tile]
                fresh = []
                value = None
                for k in range(4):
                    at = pl.ds(pl.multiple_of(base + GROUP * k, GROUP), STEP)
                    moved = dconv[at, lanes]
                    if k == 0:
                        bias_sum = sums[4] + fold(moved)
                    else:
                        moved = moved * mask_ref[k - 1, at, :]
                    fresh.append(sums[k] + fold(moved * projected))
                    term = taps[k : k + 1, weights] * moved
                    value = term if value is None else value + term
                fresh.append(bias_sum)
                dproj[rows, lanes] = value.astype(BF16)
                updated.append(tuple(fresh))
            return tuple(updated)

        sums = lax.fori_loop(0, seq // STEP, spread, ((zero,) * 5,) * tiles)
        for tile in range(tiles):
            lanes = pl.ds(side * width + tile * LANES, LANES)
            for k in range(5):
                small_ref[0, k : k + 1, lanes] = jnp.sum(sums[tile][k], axis=0, keepdims=True)
            small_ref[0, 5:8, lanes] = jnp.zeros((3, LANES), F32)

    def weight_grads(index, carry):
        rows = pl.ds(pl.multiple_of(index * 128, 128), 128)
        put_halves(keep_ref, send_ref, bit_ref, index, pl.ds(0, 2 * width), dot_nn(normed_t[rows, :], dproj[...]))
        put_halves(
            keep_ref, send_ref, bit_ref, index, pl.ds(2 * width, width), dot_nn(upstream_t[rows, :], h_ref[...])
        )
        return carry

    lax.fori_loop(0, normed_t.shape[0] // 128, weight_grads, 0)

    def back_normed(rows):
        total[rows, :] += dot_nt(dproj[rows, pl.ds(0, width)], wg_ref[...]) + dot_nt(
            dproj[rows, pl.ds(width, width)], wc_ref[...]
        )

    rows_loop(seq, BIG, back_normed)

    @pl.when(step == pl.num_programs(0) - 1)
    def _():
        to_tokens(total, natural)
        norm_backward(x_ref, g_ref, gain_ref, natural, dx_ref, dgain_ref)


def mlp_forward_kernel(
    x_ref, gain_ref, wu_ref, bu_ref, wd_ref, bd_ref, y_ref, u_ref, normed, total
):
    step = pl.program_id(0)
    seq = x_ref.shape[0]

    @pl.when(step == 0)
    def _():
        norm_into(x_ref, gain_ref, normed)

        def start(rows):
            total[rows, :] = x_ref[rows, :].astype(F32) + bd_ref[...]

        rows_loop(seq, 128, start)

    def at(rows):
        pre = dot_nn(normed[rows, :], wu_ref[...]) + bu_ref[...]
        u_ref[rows, :] = pre.astype(BF16)
        inner = ROOT_2_PI * (pre + CUBIC * (pre * pre * pre))
        active = (0.5 * pre * (1.0 + jnp.tanh(inner))).astype(BF16)
        total[rows, :] += dot_nn(active, wd_ref[...])

    rows_loop(seq, BIG, at)

    @pl.when(step == pl.num_programs(0) - 1)
    def _():
        def finish(rows):
            y_ref[rows, :] = total[rows, :].astype(BF16)

        rows_loop(seq, 128, finish)


def mlp_backward_kernel(
    x_ref, g_ref, gain_ref, wu_ref, wd_ref, u_ref, bit_ref,
    dx_ref, keep_ref, send_ref, dbu_ref, dbd_ref, dgain_ref,
    normed_t, upstream_t, total, active, dpre,
):
    step = pl.program_id(0)
    seq = x_ref.shape[0]
    width = wu_ref.shape[1]

    @pl.when(step == 0)
    def _():
        norm_into(x_ref, gain_ref, active)
        transpose_into(active, normed_t)
        transpose_into(g_ref, upstream_t)

        def at(index, carry):
            rows = pl.ds(pl.multiple_of(index * 64, 64), 64)
            return carry + jnp.sum(g_ref[rows, :].astype(F32), axis=0, keepdims=True)

        dbd_ref[...] = lax.fori_loop(0, seq // 64, at, jnp.zeros(dbd_ref.shape, F32))
        total[...] = jnp.zeros_like(total)

    def at(index, carry):
        rows = pl.ds(pl.multiple_of(index * BIG, BIG), BIG)
        pre = u_ref[rows, :].astype(F32)
        square = pre * pre
        bent = jnp.tanh(pre * (ROOT_2_PI + (ROOT_2_PI * CUBIC) * square))
        half = 0.5 * pre
        active[rows, :] = (half + half * bent).astype(BF16)
        slope = 0.5 + 0.5 * bent + half * (1.0 - bent * bent) * (
            ROOT_2_PI + (3.0 * ROOT_2_PI * CUBIC) * square
        )
        low = (dot_nt(g_ref[rows, :], wd_ref[...]) * slope).astype(BF16)
        dpre[rows, :] = low
        total[rows, :] += dot_nt(low, wu_ref[...])
        return carry + jnp.sum(low.astype(F32), axis=0, keepdims=True)

    dbu_ref[...] = lax.fori_loop(0, seq // BIG, at, jnp.zeros(dbu_ref.shape, F32))

    def weight_grads(index, carry):
        rows = pl.ds(pl.multiple_of(index * 128, 128), 128)
        put_halves(keep_ref, send_ref, bit_ref, index, pl.ds(0, width), dot_nn(normed_t[rows, :], dpre[...]))
        put_halves(
            keep_ref, send_ref, bit_ref, index, pl.ds(width, width), dot_nn(upstream_t[rows, :], active[...])
        )
        return carry

    lax.fori_loop(0, normed_t.shape[0] // 128, weight_grads, 0)

    @pl.when(step == pl.num_programs(0) - 1)
    def _():
        norm_backward(x_ref, g_ref, gain_ref, total, dx_ref, dgain_ref)


def shape(dims, kind):
    return jax.ShapeDtypeStruct(dims, kind)


PARAMS = pltpu.CompilerParams(
    dimension_semantics=("arbitrary",), vmem_limit_bytes=56 * 1024 * 1024
)


SCALAR = pl.BlockSpec(memory_space=pltpu.SMEM)


def cost(seq, microseconds):
    return pl.CostEstimate(
        flops=int(microseconds * 1.1e9), bytes_accessed=seq * 4096, transcendentals=0
    )


def whole(dims):
    return pl.BlockSpec(dims, lambda i: (0,) * len(dims))


def mixer_specs(layer, width, hidden, tile):
    count = hidden // tile
    return dict(
        gate=pl.BlockSpec((None, width, tile), lambda i: (layer, 0, i)),
        cand=pl.BlockSpec((None, width, tile), lambda i: (layer, 0, count + i)),
        tap_gate=pl.BlockSpec((None, 4, tile), lambda i: (layer, 0, i)),
        tap_cand=pl.BlockSpec((None, 4, tile), lambda i: (layer, 0, count + i)),
        bias_gate=pl.BlockSpec((None, 1, tile), lambda i: (layer, 0, i)),
        bias_cand=pl.BlockSpec((None, 1, tile), lambda i: (layer, 0, count + i)),
        out=pl.BlockSpec((None, tile, width), lambda i: (layer, i, 0)),
        gain=pl.BlockSpec((None, 1, width), lambda i: (layer, 0, 0)),
        init=pl.BlockSpec((None, 1, tile), lambda i: (layer, 0, i)),
    )


def mixer_forward(layer, x, masks, init, gain, weight_in, taps, bias, weight_out):
    seq, width = x.shape
    hidden = init.shape[2]
    tile = TILE_C
    count = hidden // tile
    spec = mixer_specs(layer, width, hidden, tile)
    column = pl.BlockSpec((seq, tile), lambda i: (0, i))
    return pl.pallas_call(
        mixer_forward_kernel,
        grid=(count,),
        in_specs=[
            whole(x.shape), spec["gain"], spec["gate"], spec["cand"], spec["tap_gate"], spec["tap_cand"],
            spec["bias_gate"], spec["bias_cand"], spec["out"], whole(masks.shape), spec["init"],
        ],
        out_specs=[
            whole(x.shape), pl.BlockSpec((1, seq, 2 * tile), lambda i: (i, 0, 0)), column, column, column,
            pl.BlockSpec((1, tile), lambda i: (0, i)),
        ],
        out_shape=[
            shape(x.shape, BF16), shape((count, seq, 2 * tile), BF16), shape((seq, hidden), BF16),
            shape((seq, hidden), BF16), shape((seq, hidden), BF16), shape((1, hidden), F32),
        ],
        scratch_shapes=[
            pltpu.VMEM((seq, width), BF16), pltpu.VMEM((width // LANES, seq, LANES), F32), pltpu.VMEM((seq, width), F32),
            pltpu.VMEM((seq + HALO, 2 * tile), F32), pltpu.VMEM((seq, tile), F32), pltpu.VMEM((seq, tile), F32),
        ],
        compiler_params=PARAMS,
        cost_estimate=cost(seq, 15),
        name="mixer_forward",
    )(x, gain, weight_in, weight_in, taps, taps, bias, bias, weight_out, masks, init)


def mixer_backward(layer, x, g, stash, masks, init, gain, weight_in, taps, weight_out, bit):
    seq, width = x.shape
    hidden = init.shape[2]
    tile = TILE_C
    count = hidden // tile
    spec = mixer_specs(layer, width, hidden, tile)
    column = pl.BlockSpec((seq, tile), lambda i: (0, i))
    return pl.pallas_call(
        mixer_backward_kernel,
        grid=(count,),
        in_specs=[
            whole(x.shape), whole(x.shape), spec["gain"], spec["gate"], spec["cand"], spec["tap_gate"],
            spec["tap_cand"], spec["out"], whole(masks.shape), spec["init"],
            pl.BlockSpec((1, seq, 2 * tile), lambda i: (i, 0, 0)), column, column, column, SCALAR,
        ],
        out_specs=[
            whole(x.shape), pl.BlockSpec((1, width // 2, 3 * tile), lambda i: (i, 0, 0)),
            pl.BlockSpec((1, width // 2, 3 * tile), lambda i: (i, 0, 0)),
            pl.BlockSpec((1, 8, 2 * tile), lambda i: (i, 0, 0)), whole((1, width)),
        ],
        out_shape=[
            shape(x.shape, BF16), shape((count, width // 2, 3 * tile), BF16),
            shape((count, width // 2, 3 * tile), BF16), shape((count, 8, 2 * tile), F32),
            shape((1, width), F32),
        ],
        scratch_shapes=[
            pltpu.VMEM((width, seq), BF16), pltpu.VMEM((seq, width), BF16), pltpu.VMEM((width, seq), BF16),
            pltpu.VMEM((width // LANES, seq, LANES), F32), pltpu.VMEM((seq, width), F32), pltpu.VMEM((seq, tile), F32),
            pltpu.VMEM((seq, tile), F32), pltpu.VMEM((seq + HALO, 2 * tile), F32),
            pltpu.VMEM((seq, 2 * tile), BF16),
        ],
        compiler_params=PARAMS,
        cost_estimate=cost(seq, 30),
        name="mixer_backward",
    )(x, g, gain, weight_in, weight_in, taps, taps, weight_out, masks, init, *stash, bit)


def mlp_forward(layer, x, gain, weight_up, bias_up, weight_down, bias_down):
    seq, width = x.shape
    inner = weight_up.shape[2]
    tile = TILE_F
    return pl.pallas_call(
        mlp_forward_kernel,
        grid=(inner // tile,),
        in_specs=[
            whole(x.shape), pl.BlockSpec((None, 1, width), lambda i: (layer, 0, 0)),
            pl.BlockSpec((None, width, tile), lambda i: (layer, 0, i)),
            pl.BlockSpec((None, 1, tile), lambda i: (layer, 0, i)),
            pl.BlockSpec((None, tile, width), lambda i: (layer, i, 0)),
            pl.BlockSpec((None, 1, width), lambda i: (layer, 0, 0)),
        ],
        out_specs=[whole(x.shape), pl.BlockSpec((seq, tile), lambda i: (0, i))],
        out_shape=[shape(x.shape, BF16), shape((seq, inner), BF16)],
        scratch_shapes=[pltpu.VMEM((seq, width), BF16), pltpu.VMEM((seq, width), F32)],
        compiler_params=PARAMS,
        cost_estimate=cost(seq, 10),
        name="mlp_forward",
    )(x, gain, weight_up, bias_up, weight_down, bias_down)


def mlp_backward(layer, x, g, pre, gain, weight_up, weight_down, bit):
    seq, width = x.shape
    inner = weight_up.shape[2]
    tile = TILE_F
    return pl.pallas_call(
        mlp_backward_kernel,
        grid=(inner // tile,),
        in_specs=[
            whole(x.shape), whole(x.shape), pl.BlockSpec((None, 1, width), lambda i: (layer, 0, 0)),
            pl.BlockSpec((None, width, tile), lambda i: (layer, 0, i)),
            pl.BlockSpec((None, tile, width), lambda i: (layer, i, 0)),
            pl.BlockSpec((seq, tile), lambda i: (0, i)), SCALAR,
        ],
        out_specs=[
            whole(x.shape), pl.BlockSpec((1, width // 2, 2 * tile), lambda i: (i, 0, 0)),
            pl.BlockSpec((1, width // 2, 2 * tile), lambda i: (i, 0, 0)),
            pl.BlockSpec((1, tile), lambda i: (0, i)), whole((1, width)), whole((1, width)),
        ],
        out_shape=[
            shape(x.shape, BF16), shape((inner // tile, width // 2, 2 * tile), BF16),
            shape((inner // tile, width // 2, 2 * tile), BF16), shape((1, inner), F32),
            shape((1, width), F32), shape((1, width), F32),
        ],
        scratch_shapes=[
            pltpu.VMEM((width, seq), BF16), pltpu.VMEM((width, seq), BF16), pltpu.VMEM((seq, width), F32),
            pltpu.VMEM((seq, tile), BF16), pltpu.VMEM((seq, tile), BF16),
        ],
        compiler_params=PARAMS,
        cost_estimate=cost(seq, 20),
        name="mlp_backward",
    )(x, g, gain, weight_up, weight_down, pre, bit)


def chunk_masks(resets):
    seq = resets.shape[0]
    keep = (1 - resets).astype(F32)
    windows = [keep]
    for k in (1, 2):
        windows.append(windows[-1] * jnp.concatenate([jnp.ones((k,), F32), keep[:-k]]))
    stacked = jnp.stack(windows)
    cut = stacked.reshape(3, GROUP, seq // GROUP).transpose(0, 2, 1)
    ahead = jnp.concatenate([cut[:, :4, 1:], jnp.zeros((3, 4, 1), F32)], axis=2)
    rows = jnp.concatenate([cut, ahead], axis=1).reshape(3, seq + 4 * GROUP, 1)
    return jnp.broadcast_to(rows, (3, seq + 4 * GROUP, LANES))


def permute(x, axis, pairs):
    return lax.ppermute(x, axis, pairs)


def assemble_kernel(own0, own1, own2, own3, left1, left2, left3, right1, right2, right3, out, sems):
    section = lax.axis_index("section")
    lefts = (left1, left2, left3)
    rights = (right1, right2, right3)
    for which, own in enumerate((own0, own1, own2, own3)):

        @pl.when(section == which)
        def _():
            pltpu.make_async_copy(own, out.at[which], sems.at[0]).start()

    for k in (1, 2, 3):

        @pl.when(section < 2)
        def _():
            pltpu.make_async_copy(lefts[k - 1], out.at[section ^ k], sems.at[k]).start()

        @pl.when(section >= 2)
        def _():
            pltpu.make_async_copy(rights[k - 1], out.at[section ^ k], sems.at[k]).start()

    for k in range(4):
        pltpu.make_async_copy(own0, out.at[0], sems.at[k]).wait()


def assemble(owns, lefts, rights):
    dims = owns[0].shape
    anywhere = pl.BlockSpec(memory_space=pl.ANY)
    return pl.pallas_call(
        assemble_kernel,
        in_specs=[anywhere] * 10,
        out_specs=pl.BlockSpec(memory_space=pltpu.VMEM),
        out_shape=shape((4,) + dims, owns[0].dtype),
        scratch_shapes=[pltpu.SemaphoreType.DMA((4,))],
        compiler_params=pltpu.CompilerParams(vmem_limit_bytes=32 * 1024 * 1024),
        name="assemble",
    )(*owns, *lefts, *rights)[None]


def after(value, *others):
    return lax.optimization_barrier((value,) + others)


def send_low(first, second, odd):
    one = jnp.where(odd, first, second)
    two = jnp.where(odd, second, first)
    return (
        permute(one, "section", [(0, 1), (1, 0)]),
        permute(two, "section", [(2, 0), (3, 1)]),
        permute(one, "section", [(3, 0), (2, 1)]),
    )


def send_high(third, fourth, odd):
    one = jnp.where(odd, third, fourth)
    two = jnp.where(odd, fourth, third)
    return (
        permute(one, "section", [(2, 3), (3, 2)]),
        permute(two, "section", [(0, 2), (1, 3)]),
        permute(one, "section", [(1, 2), (0, 3)]),
    )


def swap_pairs(size, step):
    return [(i, i ^ step) for i in range(size)]


def halve(addends, dim, axis, size, step):
    bit = (lax.axis_index(axis) // step) % 2

    def part(which):
        pieces = [
            lax.dynamic_index_in_dim(a, which, dim, keepdims=False).astype(F32) for a in addends
        ]
        return functools.reduce(jnp.add, pieces).astype(addends[0].dtype)

    got = permute(part(1 - bit), axis, swap_pairs(size, step))
    return [part(bit), got]


def bits_of(size):
    return [1 << k for k in range(size.bit_length() - 1)]


def first_step(dp, width):
    return SPLIT // (width // dp)


def sum_rows(keep, send, dp, sections, width, reverse=False):
    split = first_step(dp, width)
    got = permute(send, "dp", swap_pairs(dp, split))
    rest = [step for step in bits_of(dp) if step != split]
    share = width // (dp * sections)
    tiles, _, count = keep.shape
    names = [("dp", dp, step) for step in rest[::-1]]
    names += [("section", sections, step) for step in bits_of(sections)[::-1]]
    dims = (tiles,) + (2,) * len(names) + (share, count)
    addends = [keep.reshape(dims), got.reshape(dims)]
    order = [("dp", dp, step) for step in (rest[::-1] if reverse else rest)]
    order += [("section", sections, step) for step in bits_of(sections)]
    left = list(names)
    for item in order:
        addends = halve(addends, 1 + left.index(item), *item)
        left.remove(item)
    return addends[0].astype(F32) + addends[1].astype(F32)


def sum_small(packed, dp, sections):
    names = [("dp", dp, step) for step in bits_of(dp)[::-1]]
    names += [("section", sections, step) for step in bits_of(sections)[::-1]]
    addends = [packed.reshape((2,) * len(names) + packed.shape[1:])]
    order = [("dp", dp, step) for step in bits_of(dp)]
    order += [("section", sections, step) for step in bits_of(sections)]
    left = list(names)
    for item in order:
        addends = halve(addends, left.index(item), *item)
        left.remove(item)
    return addends[0] + addends[1]


def body(
    tokens, resets, init_states, cotangent, mix_gain, mix_in, conv_weight, conv_bias, mix_out,
    mlp_gain, mlp_up, up_bias, mlp_down, down_bias,
):
    dp = lax.axis_size("dp")
    sections = lax.axis_size("section")
    section = lax.axis_index("section")
    width = tokens.shape[2]
    odd = section % 2 == 1
    bit = ((lax.axis_index("dp") // first_step(dp, width)) % 2).astype(jnp.int32).reshape(1)

    def own(values, axis):
        return lax.dynamic_index_in_dim(values, section, axis, keepdims=False)

    x0 = own(tokens, 0)
    g4 = own(cotangent, 0)
    masks = chunk_masks(own(resets, 0))
    init = own(init_states, 1)[:, None, :]
    mix_gain = mix_gain[:, None, :]
    mlp_gain = mlp_gain[:, None, :]
    conv_bias = conv_bias[:, None, :]
    up_bias = up_bias[:, None, :]
    down_bias = down_bias[:, None, :]

    def mixer(layer, x):
        y, *stash, final = mixer_forward(
            layer, x, masks, init, mix_gain, mix_in, conv_weight, conv_bias, mix_out
        )
        return y, stash, final

    def mlp(layer, x):
        return mlp_forward(layer, x, mlp_gain, mlp_up, up_bias, mlp_down, down_bias)

    x1, stash0, final0 = mixer(0, x0)
    x2, pre0 = mlp(0, x1)
    act_low = send_low(x1, x2, odd)
    x3, stash1, final1 = mixer(1, x2)
    x4, pre1 = mlp(1, x3)
    act_high = send_high(x3, x4, odd)
    final = jnp.concatenate([final0, final1], axis=0)[:, None, :]
    final_states = lax.all_to_all(final, "section", split_axis=2, concat_axis=1, tiled=True)

    g3, up1_keep, up1_send, dbu1, dbd1, dgain_mlp1 = mlp_backward(
        1, x3, g4, pre1, mlp_gain, mlp_up, mlp_down, bit
    )
    mlp1 = sum_rows(up1_keep, up1_send, dp, sections, width)
    act_low = list(act_low)
    g3, act_low[0], act_low[1] = after(g3, act_low[0], act_low[1])
    g2, in1_keep, in1_send, small1, dgain_mix1 = mixer_backward(
        1, x2, g3, stash1, masks, init, mix_gain, mix_in, conv_weight, mix_out, bit
    )
    g2, act_low[2] = after(g2, act_low[2])
    dx_high = send_high(g2, g3, odd)
    mix1 = sum_rows(in1_keep, in1_send, dp, sections, width)
    g1, up0_keep, up0_send, dbu0, dbd0, dgain_mlp0 = mlp_backward(
        0, x1, g2, pre0, mlp_gain, mlp_up, mlp_down, bit
    )
    act_high = list(act_high)
    g1, act_high[0], act_high[1], act_high[2] = after(g1, *act_high)
    mlp0 = sum_rows(up0_keep, up0_send, dp, sections, width)
    g0, in0_keep, in0_send, small0, dgain_mix0 = mixer_backward(
        0, x0, g1, stash0, masks, init, mix_gain, mix_in, conv_weight, mix_out, bit
    )
    dx_high = list(dx_high)
    g0, dx_high[0], dx_high[1], mlp1 = after(g0, dx_high[0], dx_high[1], mlp1)
    dx_low = send_low(g0, g1, odd)
    half = in0_keep.shape[0] // 2
    mix0 = jnp.concatenate(
        [
            sum_rows(in0_keep[:half], in0_send[:half], dp, sections, width),
            sum_rows(in0_keep[half:], in0_send[half:], dp, sections, width, True),
        ]
    )
    activations = assemble((x1, x2, x3, x4), act_low, act_high)
    input_grads = assemble((g0, g1, g2, g3), dx_low, dx_high)

    devices = dp * sections
    mix_small = jnp.stack([small0, small1])
    count, tile = mix_small.shape[1], mix_small.shape[3] // 2
    mix_small = mix_small.reshape(2, count, 8, 2, tile).transpose(0, 2, 3, 1, 4).reshape(2, 8, -1)
    lines = [
        jnp.stack([dgain_mix0[0], dgain_mix1[0]]),
        jnp.stack([dgain_mlp0[0], dgain_mlp1[0]]),
        jnp.stack([dbd0[0], dbd1[0]]),
        jnp.stack([dbu0[0], dbu1[0]]),
        mix_small[:, :5].reshape(10, -1),
    ]
    packed = jnp.concatenate(
        [a.reshape(a.shape[0], devices, -1).transpose(1, 0, 2).reshape(devices, -1) for a in lines],
        axis=1,
    )
    summed = sum_small(packed, dp, sections)
    pieces, at = [], 0
    for a in lines:
        size = a.size // devices
        pieces.append(summed[at : at + size].reshape(a.shape[0], -1))
        at += size
    mix_gain_grad, mlp_gain_grad, down_bias_grad, up_bias_grad, conv = pieces
    conv = conv.reshape(2, 5, -1)

    mix_big = jnp.stack([mix0, mix1])
    mlp_big = jnp.stack([mlp0, mlp1])
    share = mix_big.shape[2]
    mix_in_grad = (
        mix_big[..., : 2 * tile].reshape(2, count, share, 2, tile).transpose(0, 2, 3, 1, 4)
        .reshape(2, share, -1)
    )
    mix_out_grad = mix_big[..., 2 * tile :].transpose(0, 1, 3, 2).reshape(2, -1, share)
    wide = mlp_big.shape[3] // 2
    mlp_up_grad = mlp_big[..., :wide].transpose(0, 2, 1, 3).reshape(2, share, -1)
    mlp_down_grad = mlp_big[..., wide:].transpose(0, 1, 3, 2).reshape(2, -1, share)
    return (
        activations, input_grads, final_states, mix_gain_grad, mix_in_grad, conv[:, :4], conv[:, 4],
        mix_out_grad, mlp_gain_grad, mlp_up_grad, up_bias_grad, mlp_down_grad, down_bias_grad,
    )


def solution(mesh):
    both = ("dp", "section")
    return jax.shard_map(
        body,
        mesh=mesh,
        in_specs=(
            P("dp", None, None), P("dp", None), P(None, "dp", None), P("dp", None, None),
            P(), P(), P(), P(), P(), P(), P(), P(), P(), P(),
        ),
        out_specs=(
            P("section", "dp", None, None), P("section", "dp", None, None), P(None, "dp", "section"),
            P(None, both), P(None, both, None), P(None, None, both), P(None, both), P(None, None, both),
            P(None, both), P(None, both, None), P(None, both), P(None, None, both), P(None, both),
        ),
        check_vma=False,
    )
```

```python
import functools

import jax
import jax.numpy as jnp
from jax import lax
from jax.experimental import pallas as pl
from jax.experimental.pallas import tpu as pltpu
from jax.sharding import PartitionSpec as P

EPSILON = 1e-06
LANES = 128
GROUP = 8
TILE_C = 256
TILE_F = 512
BIG = 1024
F32 = jnp.float32
BF16 = jnp.bfloat16
ROOT_2_PI = 0.7978845608028654
CUBIC = 0.044715


def dot_nn(left, right):
    return jnp.dot(left, right, preferred_element_type=F32)


def dot_nt(left, right):
    return lax.dot_general(left, right, (((1,), (1,)), ((), ())), preferred_element_type=F32)


def rows_loop(total, step, fn):
    def at(index, carry):
        fn(pl.ds(pl.multiple_of(index * step, step), step))
        return carry

    lax.fori_loop(0, total // step, at, 0)


def to_chunks(natural, target):
    stride = natural.shape[1] // GROUP

    def at(index, carry):
        for tile in range(natural.shape[0]):
            first = natural[tile, pl.ds(2 * index, GROUP, stride=stride), :]
            second = natural[tile, pl.ds(2 * index + 1, GROUP, stride=stride), :]
            both = jnp.concatenate([first, second], axis=0).astype(BF16)
            target[pl.ds(pl.multiple_of(index * 16, 16), 16), pl.ds(tile * LANES, LANES)] = both
        return carry

    lax.fori_loop(0, stride // 2, at, 0)


def to_tokens(chunked, natural):
    stride = natural.shape[1] // GROUP

    def at(index, carry):
        for tile in range(natural.shape[0]):
            rows = pl.ds(pl.multiple_of(index * GROUP, GROUP), GROUP)
            natural[tile, pl.ds(index, GROUP, stride=stride), :] = chunked[rows, pl.ds(tile * LANES, LANES)]
        return carry

    lax.fori_loop(0, stride, at, 0)


def transpose_into(source, target):
    def at(index, carry):
        rows = pl.ds(pl.multiple_of(index * LANES, LANES), LANES)
        target[:, rows] = source[rows, :].astype(F32).T.astype(BF16)
        return carry

    lax.fori_loop(0, source.shape[0] // LANES, at, 0)


def inverse_rms(values):
    return lax.rsqrt(jnp.mean(values * values, axis=-1, keepdims=True) + EPSILON)


def put_tiles(natural, rows, values):
    for tile in range(natural.shape[0]):
        natural[tile, rows, :] = values[:, tile * LANES : (tile + 1) * LANES]


def get_tiles(natural, rows):
    return jnp.concatenate([natural[tile, rows, :] for tile in range(natural.shape[0])], axis=1)


def norm_into(x_ref, gain_ref, target):
    def at(rows):
        source = x_ref[rows, :].astype(F32)
        result = source * inverse_rms(source) * gain_ref[...]
        if len(target.shape) == 3:
            put_tiles(target, rows, result)
        else:
            target[rows, :] = result.astype(target.dtype)

    rows_loop(x_ref.shape[0], 128, at)


def previous_chunk(values, first_row):
    rolled = pltpu.roll(values, 1, 0)
    position = lax.broadcasted_iota(jnp.int32, values.shape, 0)
    return jnp.where(position == 0, first_row, rolled)


def following_chunk(values):
    rolled = pltpu.roll(values, GROUP - 1, 0)
    position = lax.broadcasted_iota(jnp.int32, values.shape, 0)
    return jnp.where(position == GROUP - 1, 0.0, rolled)


def sigmoid(values):
    return 0.5 * jnp.tanh(0.5 * values) + 0.5


def repeat_rows(values, rows):
    return jnp.concatenate([values] * (rows // values.shape[0]), axis=0)


STEP = 32
SPLIT = 64
HALO = 24


def mixer_forward_kernel(
    x_ref, gain_ref, wg_ref, wc_ref, kg_ref, kc_ref, bg_ref, bc_ref, wo_ref, mask_ref, init_ref,
    y_ref, p_ref, z_ref, cand_ref, h_ref, final_ref,
    normed, natural, total, proj, local, decay,
):
    step = pl.program_id(0)
    seq = x_ref.shape[0]
    width = wg_ref.shape[1]

    @pl.when(step == 0)
    def _():
        norm_into(x_ref, gain_ref, natural)
        to_chunks(natural, normed)
        total[...] = jnp.zeros_like(total)

    def project(index, carry):
        rows = pl.ds(pl.multiple_of(index * BIG, BIG), BIG)
        out_rows = pl.ds(pl.multiple_of(index * BIG + HALO, GROUP), BIG)
        block = normed[rows, :]
        for side, weight in enumerate((wg_ref, wc_ref)):
            lanes = pl.ds(side * width, width)
            piece = dot_nn(block, weight[...])
            proj[out_rows, lanes] = piece
            p_ref[0, rows, lanes] = piece.astype(BF16)
        return carry

    lax.fori_loop(0, seq // BIG, project, 0)
    for offset in range(3):
        last = proj[pl.ds(seq + GROUP * offset, GROUP), :]
        proj[pl.ds(GROUP * offset, GROUP), :] = previous_chunk(last, 0.0)

    def scan_step(index, carry):
        base = pl.multiple_of(index * STEP, STEP)
        rows = pl.ds(base, STEP)
        masks = [None] + [mask_ref[k, rows, :] for k in range(3)]
        updated = []
        for tile in range(width // LANES):
            lanes = pl.ds(tile * LANES, LANES)

            def convolve(shift, taps, bias):
                value = bias[0:1, lanes]
                for k in range(4):
                    at = pl.ds(pl.multiple_of(base + HALO - GROUP * k, GROUP), STEP)
                    term = proj[at, pl.ds(shift + tile * LANES, LANES)]
                    if k:
                        term = term * masks[k]
                    value = value + taps[k : k + 1, lanes] * term
                return value

            update = sigmoid(convolve(0, kg_ref, bg_ref))
            candidate = convolve(width, kc_ref, bc_ref)
            z_ref[rows, lanes] = update.astype(BF16)
            cand_ref[rows, lanes] = candidate.astype(BF16)
            retain = (1.0 - update) * masks[1]
            inject = update * candidate
            state, product = carry[tile]
            states, products = [], []
            for g in range(STEP // GROUP):
                here = slice(g * GROUP, (g + 1) * GROUP)
                state = retain[here] * state + inject[here]
                product = retain[here] * product
                states.append(state)
                products.append(product)
            local[rows, lanes] = jnp.concatenate(states, axis=0)
            decay[rows, lanes] = jnp.concatenate(products, axis=0)
            updated.append((state, product))
        return tuple(updated)

    zero = jnp.zeros((GROUP, LANES), F32)
    one = jnp.ones((GROUP, LANES), F32)
    ends = lax.fori_loop(0, seq // STEP, scan_step, ((zero, one),) * (width // LANES))
    entries = []
    for tile, (state, product) in enumerate(ends):
        lanes = pl.ds(tile * LANES, LANES)
        current = init_ref[0:1, lanes]
        starts = []
        for g in range(GROUP):
            starts.append(current)
            current = product[g : g + 1] * current + state[g : g + 1]
        final_ref[0:1, lanes] = current
        entries.append(jnp.concatenate(starts, axis=0))
    entry = repeat_rows(jnp.concatenate(entries, axis=1), STEP)

    def fix(index, carry):
        rows = pl.ds(pl.multiple_of(index * STEP, STEP), STEP)
        h_ref[rows, :] = (local[rows, :] + decay[rows, :] * entry).astype(BF16)
        return carry

    lax.fori_loop(0, seq // STEP, fix, 0)

    def output(rows):
        total[rows, :] += dot_nn(h_ref[rows, :], wo_ref[...])

    rows_loop(seq, BIG, output)

    @pl.when(step == pl.num_programs(0) - 1)
    def _():
        to_tokens(total, natural)

        def finish(rows):
            y_ref[rows, :] = (x_ref[rows, :].astype(F32) + get_tiles(natural, rows)).astype(BF16)

        rows_loop(seq, 128, finish)


def norm_backward(x_ref, g_ref, gain_ref, grad_normed, dx_ref, dgain_ref):
    gain = gain_ref[...]

    def at(index, carry):
        rows = pl.ds(pl.multiple_of(index * 64, 64), 64)
        source = x_ref[rows, :].astype(F32)
        upstream = g_ref[rows, :].astype(F32)
        incoming = get_tiles(grad_normed, rows) if len(grad_normed.shape) == 3 else grad_normed[rows, :]
        scale = inverse_rms(source)
        scaled = gain * incoming
        mean = jnp.mean(source * scaled, axis=-1, keepdims=True)
        result = upstream + scale * scaled - source * (scale * scale * scale * mean)
        dx_ref[rows, :] = result.astype(BF16)
        return carry + jnp.sum(incoming * source * scale, axis=0, keepdims=True)

    dgain_ref[...] = lax.fori_loop(0, x_ref.shape[0] // 64, at, jnp.zeros(gain.shape, F32))


def put_grad(refs, bit_ref, lanes, values):
    if len(refs) == 1:
        refs[0][:, lanes] = values.astype(BF16)
        return
    mine = bit_ref[0] == 1
    for pair in range(values.shape[0] // (2 * SPLIT)):
        low = values[2 * pair * SPLIT : (2 * pair + 1) * SPLIT].astype(BF16)
        high = values[(2 * pair + 1) * SPLIT : (2 * pair + 2) * SPLIT].astype(BF16)
        rows = pl.ds(pair * SPLIT, SPLIT)
        refs[0][rows, lanes] = jnp.where(mine, high, low)
        refs[1][rows, lanes] = jnp.where(mine, low, high)


def mixer_backward_kernel(
    x_ref, g_ref, gain_ref, wg_ref, wc_ref, kg_ref, kc_ref, wo_ref, mask_ref, init_ref,
    p_ref, z_ref, cand_ref, h_ref, bit_ref, *rest,
):
    *dw, dx_ref, small_ref, dgain_ref = rest[:-9]
    (normed_t, upstream, upstream_t, natural, total, local, decay, dconv, dproj) = rest[-9:]
    step = pl.program_id(0)
    seq = x_ref.shape[0]
    width = wg_ref.shape[1]
    tiles = width // LANES

    @pl.when(step == 0)
    def _():
        norm_into(x_ref, gain_ref, natural)
        to_chunks(natural, upstream)
        transpose_into(upstream, normed_t)

        def widen(rows):
            put_tiles(natural, rows, g_ref[rows, :].astype(F32))

        rows_loop(seq, 128, widen)
        to_chunks(natural, upstream)
        transpose_into(upstream, upstream_t)
        total[...] = jnp.zeros_like(total)

    def back_hidden(rows):
        local[rows, :] = dot_nt(upstream[rows, :], wo_ref[...])

    rows_loop(seq, BIG, back_hidden)

    def scan_step(index, carry):
        rows = pl.ds(pl.multiple_of(seq - STEP - index * STEP, STEP), STEP)
        keep = mask_ref[0, rows, :]
        updated = []
        for tile in range(tiles):
            lanes = pl.ds(tile * LANES, LANES)
            retain = (1.0 - z_ref[rows, lanes].astype(F32)) * keep
            grads = local[rows, lanes]
            chain, product = carry[tile]
            chains, products = [], []
            for g in reversed(range(STEP // GROUP)):
                here = slice(g * GROUP, (g + 1) * GROUP)
                value = grads[here] + chain
                chains.append(value)
                products.append(product)
                chain = retain[here] * value
                product = retain[here] * product
            local[rows, lanes] = jnp.concatenate(chains[::-1], axis=0)
            decay[rows, lanes] = jnp.concatenate(products[::-1], axis=0)
            updated.append((chain, product))
        return tuple(updated)

    zero = jnp.zeros((GROUP, LANES), F32)
    one = jnp.ones((GROUP, LANES), F32)
    ends = lax.fori_loop(0, seq // STEP, scan_step, ((zero, one),) * tiles)
    entries = []
    for chain, product in ends:
        current = jnp.zeros((1, LANES), F32)
        starts = [current]
        for g in reversed(range(1, GROUP)):
            current = chain[g : g + 1] + product[g : g + 1] * current
            starts.append(current)
        entries.append(jnp.concatenate(starts[::-1], axis=0))

    last_rows = h_ref[pl.ds(seq - 16, 16), :].astype(F32)[GROUP:]
    before = previous_chunk(last_rows, init_ref[0:1, :])

    def gates(index, carry):
        base = pl.multiple_of(index * STEP, STEP)
        rows = pl.ds(base, STEP)
        keep = mask_ref[0, rows, :]
        updated = []
        for tile in range(tiles):
            lanes = pl.ds(tile * LANES, LANES)
            hidden = h_ref[rows, lanes].astype(F32)
            delayed = jnp.concatenate([carry[tile], hidden[: STEP - GROUP]], axis=0)
            error = local[rows, lanes] + decay[rows, lanes] * repeat_rows(entries[tile], STEP)
            update = z_ref[rows, lanes].astype(F32)
            candidate = cand_ref[rows, lanes].astype(F32)
            slope = error * (candidate - keep * delayed)
            dconv[rows, lanes] = slope * (update * (1.0 - update))
            dconv[rows, pl.ds(width + tile * LANES, LANES)] = update * error
            updated.append(hidden[STEP - GROUP :])
        return tuple(updated)

    starting = tuple(before[:, tile * LANES : (tile + 1) * LANES] for tile in range(tiles))
    lax.fori_loop(0, seq // STEP, gates, starting)
    for offset in range(3):
        first = dconv[pl.ds(GROUP * offset, GROUP), :]
        dconv[pl.ds(seq + GROUP * offset, GROUP), :] = following_chunk(first)

    def fold(values):
        result = values[0:GROUP]
        for g in range(1, STEP // GROUP):
            result = result + values[g * GROUP : (g + 1) * GROUP]
        return result

    for side, taps in enumerate((kg_ref, kc_ref)):

        def spread(index, carry):
            base = pl.multiple_of(index * STEP, STEP)
            rows = pl.ds(base, STEP)
            updated = []
            for tile in range(tiles):
                lanes = pl.ds(side * width + tile * LANES, LANES)
                weights = pl.ds(tile * LANES, LANES)
                projected = p_ref[0, rows, lanes].astype(F32)
                sums = carry[tile]
                fresh = []
                value = None
                for k in range(4):
                    at = pl.ds(pl.multiple_of(base + GROUP * k, GROUP), STEP)
                    moved = dconv[at, lanes]
                    if k == 0:
                        bias_sum = sums[4] + fold(moved)
                    else:
                        moved = moved * mask_ref[k - 1, at, :]
                    fresh.append(sums[k] + fold(moved * projected))
                    term = taps[k : k + 1, weights] * moved
                    value = term if value is None else value + term
                fresh.append(bias_sum)
                dproj[rows, lanes] = value.astype(BF16)
                updated.append(tuple(fresh))
            return tuple(updated)

        sums = lax.fori_loop(0, seq // STEP, spread, ((zero,) * 5,) * tiles)
        for tile in range(tiles):
            lanes = pl.ds(side * width + tile * LANES, LANES)
            for k in range(5):
                small_ref[0, k : k + 1, lanes] = jnp.sum(sums[tile][k], axis=0, keepdims=True)
            small_ref[0, 5:8, lanes] = jnp.zeros((3, LANES), F32)

    put_grad(dw, bit_ref, pl.ds(0, 2 * width), dot_nn(normed_t[...], dproj[...]))
    put_grad(dw, bit_ref, pl.ds(2 * width, width), dot_nn(upstream_t[...], h_ref[...]))

    def back_normed(rows):
        total[rows, :] += dot_nt(dproj[rows, pl.ds(0, width)], wg_ref[...]) + dot_nt(
            dproj[rows, pl.ds(width, width)], wc_ref[...]
        )

    rows_loop(seq, BIG, back_normed)

    @pl.when(step == pl.num_programs(0) - 1)
    def _():
        to_tokens(total, natural)
        norm_backward(x_ref, g_ref, gain_ref, natural, dx_ref, dgain_ref)


def mlp_forward_kernel(
    x_ref, gain_ref, wu_ref, bu_ref, wd_ref, bd_ref, y_ref, u_ref, normed, total
):
    step = pl.program_id(0)
    seq = x_ref.shape[0]

    @pl.when(step == 0)
    def _():
        norm_into(x_ref, gain_ref, normed)

        def start(rows):
            total[rows, :] = x_ref[rows, :].astype(F32) + bd_ref[...]

        rows_loop(seq, 128, start)

    def at(rows):
        pre = dot_nn(normed[rows, :], wu_ref[...]) + bu_ref[...]
        u_ref[rows, :] = pre.astype(BF16)
        inner = ROOT_2_PI * (pre + CUBIC * (pre * pre * pre))
        active = (0.5 * pre * (1.0 + jnp.tanh(inner))).astype(BF16)
        total[rows, :] += dot_nn(active, wd_ref[...])

    rows_loop(seq, BIG, at)

    @pl.when(step == pl.num_programs(0) - 1)
    def _():
        def finish(rows):
            y_ref[rows, :] = total[rows, :].astype(BF16)

        rows_loop(seq, 128, finish)


def mlp_backward_kernel(
    x_ref, g_ref, gain_ref, wu_ref, wd_ref, u_ref, bit_ref, *rest,
):
    *dw, dx_ref, dbu_ref, dbd_ref, dgain_ref = rest[:-5]
    normed_t, upstream_t, total, active, dpre = rest[-5:]
    step = pl.program_id(0)
    seq = x_ref.shape[0]
    width = wu_ref.shape[1]

    @pl.when(step == 0)
    def _():
        norm_into(x_ref, gain_ref, active)
        transpose_into(active, normed_t)
        transpose_into(g_ref, upstream_t)

        def at(index, carry):
            rows = pl.ds(pl.multiple_of(index * 64, 64), 64)
            return carry + jnp.sum(g_ref[rows, :].astype(F32), axis=0, keepdims=True)

        dbd_ref[...] = lax.fori_loop(0, seq // 64, at, jnp.zeros(dbd_ref.shape, F32))
        total[...] = jnp.zeros_like(total)

    def at(index, carry):
        rows = pl.ds(pl.multiple_of(index * BIG, BIG), BIG)
        pre = u_ref[rows, :].astype(F32)
        square = pre * pre
        bent = jnp.tanh(pre * (ROOT_2_PI + (ROOT_2_PI * CUBIC) * square))
        half = 0.5 * pre
        active[rows, :] = (half + half * bent).astype(BF16)
        slope = 0.5 + 0.5 * bent + half * (1.0 - bent * bent) * (
            ROOT_2_PI + (3.0 * ROOT_2_PI * CUBIC) * square
        )
        low = (dot_nt(g_ref[rows, :], wd_ref[...]) * slope).astype(BF16)
        dpre[rows, :] = low
        total[rows, :] += dot_nt(low, wu_ref[...])
        return carry + jnp.sum(low.astype(F32), axis=0, keepdims=True)

    dbu_ref[...] = lax.fori_loop(0, seq // BIG, at, jnp.zeros(dbu_ref.shape, F32))

    put_grad(dw, bit_ref, pl.ds(0, width), dot_nn(normed_t[...], dpre[...]))
    put_grad(dw, bit_ref, pl.ds(width, width), dot_nn(upstream_t[...], active[...]))

    @pl.when(step == pl.num_programs(0) - 1)
    def _():
        norm_backward(x_ref, g_ref, gain_ref, total, dx_ref, dgain_ref)


def shape(dims, kind):
    return jax.ShapeDtypeStruct(dims, kind)


PARAMS = pltpu.CompilerParams(
    dimension_semantics=("arbitrary",), vmem_limit_bytes=56 * 1024 * 1024
)


SCALAR = pl.BlockSpec(memory_space=pltpu.SMEM)
ANYWHERE = pl.BlockSpec(memory_space=pl.ANY)
MESH = pl.DeviceIdType.MESH
SECTIONS = 4


def meet_sections(section):
    barrier = pltpu.get_barrier_semaphore()
    for by in range(1, SECTIONS):
        other = (section + by) % SECTIONS
        pl.semaphore_signal(barrier, inc=1, device_id={"section": other}, device_id_type=MESH)
    pl.semaphore_wait(barrier, SECTIONS - 1)


def delivery(jobs, sources, buffers, send_sems, recv_sems):
    section = lax.axis_index("section")

    def copy(number, sender):
        source, part, first, count, buffer = jobs[number]
        rows = pl.ds(first, count)
        return pltpu.make_async_remote_copy(
            src_ref=sources[source][0].at[sources[source][1], rows] if sources[source][1] is not None
            else sources[source][0].at[rows],
            dst_ref=buffers[buffer].at[sender, rows],
            send_sem=send_sems.at[number],
            recv_sem=recv_sems.at[number, sender],
            device_id={"section": part},
            device_id_type=MESH,
        )

    def start():
        for number, job in enumerate(jobs):

            @pl.when(section != job[1])
            def _(number=number):
                copy(number, section).start()

    def wait():
        for number, job in enumerate(jobs):

            @pl.when(section != job[1])
            def _(number=number):
                copy(number, section).wait_send()

            @pl.when(section == job[1])
            def _(number=number, job=job):
                for sender in range(SECTIONS):
                    if sender != job[1]:
                        copy(number, sender).wait_recv()

    return start, wait


class Cargo:
    def __init__(self, collective_id, arrays, sources, buffers, jobs, dims):
        self.collective_id = collective_id
        self.arrays = list(arrays)
        self.sources = sources
        self.old = [b for b in buffers if b is not None]
        self.buffers = buffers
        self.jobs = jobs
        self.dims = dims


def call(kernel, cargo, *, grid, in_specs, out_specs, out_shape, scratch_shapes, cost_estimate, name, args, aliases=None):
    aliases = dict(aliases or {})
    if cargo is None:
        return pl.pallas_call(
            kernel, grid=grid, in_specs=in_specs, out_specs=out_specs, out_shape=out_shape,
            scratch_shapes=scratch_shapes, compiler_params=PARAMS, cost_estimate=cost_estimate, name=name,
            input_output_aliases=aliases,
        )(*args)
    n_in, n_out = len(in_specs), len(out_specs)
    n_array, n_old, n_buffer = len(cargo.arrays), len(cargo.old), len(cargo.buffers)

    def carrying(*refs):
        ins, refs = refs[:n_in], refs[n_in:]
        arrays, refs = refs[:n_array], refs[n_array + n_old :]
        outs, refs = refs[:n_out], refs[n_out:]
        buffers, refs = refs[:n_buffer], refs[n_buffer:]
        own, (send_sems, recv_sems) = refs[:-2], refs[-2:]
        sources = [(arrays[a], at) for a, at in cargo.sources]
        start, wait = delivery(cargo.jobs, sources, buffers, send_sems, recv_sems)
        step = pl.program_id(0)

        @pl.when(step == 0)
        def _():
            meet_sections(lax.axis_index("section"))
            start()

        kernel(*ins, *outs, *own)

        @pl.when(step == pl.num_programs(0) - 1)
        def _():
            wait()

    old = 0
    for number, buffer in enumerate(cargo.buffers):
        if buffer is not None:
            aliases[n_in + n_array + old] = n_out + number
            old += 1
    jobs = len(cargo.jobs)
    return pl.pallas_call(
        carrying,
        grid=grid,
        in_specs=list(in_specs) + [ANYWHERE] * (n_array + n_old),
        out_specs=list(out_specs) + [ANYWHERE] * n_buffer,
        out_shape=list(out_shape) + [shape(cargo.dims, BF16)] * n_buffer,
        scratch_shapes=list(scratch_shapes)
        + [pltpu.SemaphoreType.DMA((jobs,)), pltpu.SemaphoreType.DMA((jobs, SECTIONS))],
        compiler_params=pltpu.CompilerParams(
            dimension_semantics=("arbitrary",), vmem_limit_bytes=56 * 1024 * 1024,
            collective_id=cargo.collective_id, has_side_effects=True,
        ),
        cost_estimate=cost_estimate,
        name=name,
        input_output_aliases=aliases,
    )(*args, *cargo.arrays, *cargo.old)


def cost(seq, microseconds):
    return pl.CostEstimate(
        flops=int(microseconds * 1.1e9), bytes_accessed=seq * 4096, transcendentals=0
    )


def whole(dims):
    return pl.BlockSpec(dims, lambda i: (0,) * len(dims))


def source_spec(stack, at):
    if at is None:
        return whole(stack.shape)
    return pl.BlockSpec((None,) + stack.shape[1:], lambda i: (at, 0, 0))


def mixer_specs(layer, width, hidden, tile):
    count = hidden // tile
    return dict(
        gate=pl.BlockSpec((None, width, tile), lambda i: (layer, 0, i)),
        cand=pl.BlockSpec((None, width, tile), lambda i: (layer, 0, count + i)),
        tap_gate=pl.BlockSpec((None, 4, tile), lambda i: (layer, 0, i)),
        tap_cand=pl.BlockSpec((None, 4, tile), lambda i: (layer, 0, count + i)),
        bias_gate=pl.BlockSpec((None, 1, tile), lambda i: (layer, 0, i)),
        bias_cand=pl.BlockSpec((None, 1, tile), lambda i: (layer, 0, count + i)),
        out=pl.BlockSpec((None, tile, width), lambda i: (layer, i, 0)),
        gain=pl.BlockSpec((None, 1, width), lambda i: (layer, 0, 0)),
        init=pl.BlockSpec((None, 1, tile), lambda i: (layer, 0, i)),
    )


def mixer_forward(layer, stack, at, masks, init, gain, weight_in, taps, bias, weight_out):
    seq, width = stack.shape[-2:]
    hidden = init.shape[2]
    tile = TILE_C
    count = hidden // tile
    spec = mixer_specs(layer, width, hidden, tile)
    column = pl.BlockSpec((seq, tile), lambda i: (0, i))
    return pl.pallas_call(
        mixer_forward_kernel,
        grid=(count,),
        in_specs=[
            source_spec(stack, at), spec["gain"], spec["gate"], spec["cand"], spec["tap_gate"], spec["tap_cand"],
            spec["bias_gate"], spec["bias_cand"], spec["out"], whole(masks.shape), spec["init"],
        ],
        out_specs=[
            pl.BlockSpec((None, seq, width), lambda i: (2 * layer, 0, 0)), pl.BlockSpec((1, seq, 2 * tile), lambda i: (i, 0, 0)), column, column, column,
            pl.BlockSpec((1, tile), lambda i: (0, i)),
        ],
        out_shape=[
            shape((4, seq, width), BF16), shape((count, seq, 2 * tile), BF16), shape((seq, hidden), BF16),
            shape((seq, hidden), BF16), shape((seq, hidden), BF16), shape((1, hidden), F32),
        ],
        scratch_shapes=[
            pltpu.VMEM((seq, width), BF16), pltpu.VMEM((width // LANES, seq, LANES), F32), pltpu.VMEM((seq, width), F32),
            pltpu.VMEM((seq + HALO, 2 * tile), F32), pltpu.VMEM((seq, tile), F32), pltpu.VMEM((seq, tile), F32),
        ],
        compiler_params=PARAMS,
        cost_estimate=cost(seq, 15),
        input_output_aliases={} if at is None else {0: 0},
        name="mixer_forward",
    )(stack, gain, weight_in, weight_in, taps, taps, bias, bias, weight_out, masks, init)


def grad_outputs(width, tile, total, split):
    rows = width // 2 if split else width
    parts = 2 if split else 1
    return (
        [pl.BlockSpec((rows, tile), lambda i: (0, i))] * parts,
        [shape((rows, total), BF16)] * parts,
    )


def mixer_backward(layer, stack, at, g, stash, masks, init, gain, weight_in, taps, weight_out, bit, split, cargo):
    seq, width = g.shape
    hidden = init.shape[2]
    tile = TILE_C
    count = hidden // tile
    spec = mixer_specs(layer, width, hidden, tile)
    column = pl.BlockSpec((seq, tile), lambda i: (0, i))
    dw_specs, dw_shapes = grad_outputs(width, 3 * tile, 3 * hidden, split)
    return call(
        mixer_backward_kernel,
        cargo,
        grid=(count,),
        in_specs=[
            source_spec(stack, at), whole(g.shape), spec["gain"], spec["gate"], spec["cand"], spec["tap_gate"],
            spec["tap_cand"], spec["out"], whole(masks.shape), spec["init"],
            pl.BlockSpec((1, seq, 2 * tile), lambda i: (i, 0, 0)), column, column, column, SCALAR,
        ],
        out_specs=[
            *dw_specs, whole(g.shape), pl.BlockSpec((1, 8, 2 * tile), lambda i: (i, 0, 0)), whole((1, width)),
        ],
        out_shape=[
            *dw_shapes, shape(g.shape, BF16), shape((count, 8, 2 * tile), F32),
            shape((1, width), F32),
        ],
        scratch_shapes=[
            pltpu.VMEM((width, seq), BF16), pltpu.VMEM((seq, width), BF16), pltpu.VMEM((width, seq), BF16),
            pltpu.VMEM((width // LANES, seq, LANES), F32), pltpu.VMEM((seq, width), F32), pltpu.VMEM((seq, tile), F32),
            pltpu.VMEM((seq, tile), F32), pltpu.VMEM((seq + HALO, 2 * tile), F32),
            pltpu.VMEM((seq, 2 * tile), BF16),
        ],
        cost_estimate=cost(seq, 30),
        name="mixer_backward",
        args=(stack, g, gain, weight_in, weight_in, taps, taps, weight_out, masks, init, *stash, bit),
    )


def mlp_forward(layer, stack, at, gain, weight_up, bias_up, weight_down, bias_down):
    seq, width = stack.shape[-2:]
    inner = weight_up.shape[2]
    tile = TILE_F
    return pl.pallas_call(
        mlp_forward_kernel,
        grid=(inner // tile,),
        in_specs=[
            source_spec(stack, at), pl.BlockSpec((None, 1, width), lambda i: (layer, 0, 0)),
            pl.BlockSpec((None, width, tile), lambda i: (layer, 0, i)),
            pl.BlockSpec((None, 1, tile), lambda i: (layer, 0, i)),
            pl.BlockSpec((None, tile, width), lambda i: (layer, i, 0)),
            pl.BlockSpec((None, 1, width), lambda i: (layer, 0, 0)),
        ],
        out_specs=[
            pl.BlockSpec((None, seq, width), lambda i: (2 * layer + 1, 0, 0)),
            pl.BlockSpec((seq, tile), lambda i: (0, i)),
        ],
        out_shape=[shape(stack.shape, BF16), shape((seq, inner), BF16)],
        scratch_shapes=[pltpu.VMEM((seq, width), BF16), pltpu.VMEM((seq, width), F32)],
        compiler_params=PARAMS,
        cost_estimate=cost(seq, 10),
        input_output_aliases={0: 0},
        name="mlp_forward",
    )(stack, gain, weight_up, bias_up, weight_down, bias_down)


def mlp_backward(layer, stack, at, g, pre, gain, weight_up, weight_down, bit, split, cargo):
    seq, width = g.shape
    inner = weight_up.shape[2]
    tile = TILE_F
    dw_specs, dw_shapes = grad_outputs(width, 2 * tile, 2 * inner, split)
    return call(
        mlp_backward_kernel,
        cargo,
        grid=(inner // tile,),
        in_specs=[
            source_spec(stack, at), whole(g.shape), pl.BlockSpec((None, 1, width), lambda i: (layer, 0, 0)),
            pl.BlockSpec((None, width, tile), lambda i: (layer, 0, i)),
            pl.BlockSpec((None, tile, width), lambda i: (layer, i, 0)),
            pl.BlockSpec((seq, tile), lambda i: (0, i)), SCALAR,
        ],
        out_specs=[
            *dw_specs, whole(g.shape), pl.BlockSpec((1, tile), lambda i: (0, i)), whole((1, width)), whole((1, width)),
        ],
        out_shape=[
            *dw_shapes, shape(g.shape, BF16), shape((1, inner), F32),
            shape((1, width), F32), shape((1, width), F32),
        ],
        scratch_shapes=[
            pltpu.VMEM((width, seq), BF16), pltpu.VMEM((width, seq), BF16), pltpu.VMEM((seq, width), F32),
            pltpu.VMEM((seq, tile), BF16), pltpu.VMEM((seq, tile), BF16),
        ],
        cost_estimate=cost(seq, 20),
        name="mlp_backward",
        args=(stack, g, gain, weight_up, weight_down, pre, bit),
    )


def chunk_masks(resets):
    seq = resets.shape[0]
    keep = (1 - resets).astype(F32)
    windows = [keep]
    for k in (1, 2):
        windows.append(windows[-1] * jnp.concatenate([jnp.ones((k,), F32), keep[:-k]]))
    stacked = jnp.stack(windows)
    cut = stacked.reshape(3, GROUP, seq // GROUP).transpose(0, 2, 1)
    ahead = jnp.concatenate([cut[:, :4, 1:], jnp.zeros((3, 4, 1), F32)], axis=2)
    rows = jnp.concatenate([cut, ahead], axis=1).reshape(3, seq + 4 * GROUP, 1)
    return jnp.broadcast_to(rows, (3, seq + 4 * GROUP, LANES))


def permute(x, axis, pairs):
    return lax.ppermute(x, axis, pairs)


def last_kernel(jobs, split, dp, n_array, *refs):
    arrays, refs = refs[:n_array], refs[n_array:]
    (keeps, sends), refs = (refs[0:2], refs[2:4]), refs[5:]
    buffer, outs, refs = refs[0], refs[1:3], refs[3:]
    kept, got, parts, landed, sums = refs[0:2], refs[2:4], refs[4:6], refs[6:8], refs[8:10]
    send_sems, recv_sems, local_sems, core_sems, part_sems = refs[10:]
    section = lax.axis_index("section")
    where = lax.axis_index("dp")
    bit = (where // split) % 2
    partner = where + split * (1 - 2 * bit)
    top = dp // 4 if split * 4 < dp else 0
    steps = [step for step in bits_of(dp) if step != split][-2:]
    low_bit, high_bit = (where // steps[0]) % 2, (where // steps[1]) % 2
    mine = low_bit + 2 * high_bit

    def flipped(mask):
        low, high = mask % 2, mask // 2
        new_low = low_bit + low * (1 - 2 * low_bit)
        new_high = high_bit + high * (1 - 2 * high_bit)
        device = where + steps[0] * (new_low - low_bit) + steps[1] * (new_high - high_bit)
        return new_low + 2 * new_high, device

    barrier = pltpu.get_barrier_semaphore()
    for by in range(1, SECTIONS):
        other = (section + by) % SECTIONS
        pl.semaphore_signal(barrier, inc=1, device_id={"section": other}, device_id_type=MESH)
    pl.semaphore_signal(barrier, inc=1, device_id={"dp": partner}, device_id_type=MESH)
    for mask in (1, 2, 3):
        pl.semaphore_signal(barrier, inc=1, device_id={"dp": flipped(mask)[1]}, device_id_type=MESH)
    pl.semaphore_wait(barrier, SECTIONS + 3)

    start, wait = delivery(jobs, [(a, None) for a in arrays], [buffer], send_sems, recv_sems)
    swaps, loads = [], []
    for n in range(2):
        swap = pltpu.make_async_remote_copy(
            src_ref=sends[n], dst_ref=got[n], send_sem=core_sems.at[0, n], recv_sem=core_sems.at[1, n],
            device_id={"dp": partner}, device_id_type=MESH,
        )
        swap.start()
        load = pltpu.make_async_copy(keeps[n], kept[n], local_sems.at[n])
        load.start()
        swaps.append(swap)
        loads.append(load)
    start()
    moves = []
    for n in range(2):
        loads[n].wait()
        swaps[n].wait()
        rows = kept[n].shape[0] // 4
        for mask in (1, 2, 3):
            quarter, device = flipped(mask)
            taken = pl.ds(pl.multiple_of(quarter * rows, rows), rows)
            parts[n][mask - 1] = (kept[n][taken, :].astype(F32) + got[n][taken, :].astype(F32)).astype(BF16)
            move = pltpu.make_async_remote_copy(
                src_ref=parts[n].at[mask - 1], dst_ref=landed[n].at[mask - 1],
                send_sem=part_sems.at[0, n, mask - 1], recv_sem=part_sems.at[1, n, mask - 1],
                device_id={"dp": device}, device_id_type=MESH,
            )
            move.start()
            moves.append(move)
    for n in range(2):
        rows = kept[n].shape[0] // 4
        taken = pl.ds(pl.multiple_of(mine * rows, rows), rows)
        total = kept[n][taken, :].astype(F32) + got[n][taken, :].astype(F32)
        for mask in (1, 2, 3):
            moves[3 * n + mask - 1].wait()
            total = total + landed[n][mask - 1].astype(F32)
        sums[n][...] = total.astype(BF16)
        store = pltpu.make_async_copy(sums[n], outs[n], local_sems.at[n])
        store.start()
        store.wait()
    wait()


def finish(cargo, keeps, sends, dp, width):
    quarters = [(k.shape[0] // 4, k.shape[1]) for k in keeps]
    n_array = len(cargo.arrays)
    jobs = len(cargo.jobs)
    return pl.pallas_call(
        functools.partial(last_kernel, cargo.jobs, first_step(dp, width), dp, n_array),
        in_specs=[ANYWHERE] * (n_array + 5),
        out_specs=[ANYWHERE] * 3,
        out_shape=[shape(cargo.dims, BF16)] + [shape(q, BF16) for q in quarters],
        scratch_shapes=[pltpu.VMEM(k.shape, BF16) for k in keeps] * 2
        + [pltpu.VMEM((3,) + q, BF16) for q in quarters] * 2
        + [pltpu.VMEM(q, BF16) for q in quarters]
        + [
            pltpu.SemaphoreType.DMA((jobs,)), pltpu.SemaphoreType.DMA((jobs, SECTIONS)),
            pltpu.SemaphoreType.DMA((2,)), pltpu.SemaphoreType.DMA((2, 2)), pltpu.SemaphoreType.DMA((2, 2, 3)),
        ],
        compiler_params=pltpu.CompilerParams(
            vmem_limit_bytes=56 * 1024 * 1024, collective_id=cargo.collective_id, has_side_effects=True
        ),
        input_output_aliases={n_array + 4: 0},
        name="finish",
    )(*cargo.arrays, *keeps, *sends, cargo.old[0])


def add_up(pieces):
    return functools.reduce(jnp.add, [piece.astype(F32) for piece in pieces])


def exchange(addends, axis, size, steps):
    where = lax.axis_index(axis)
    own = sum(((where // step) % 2) << k for k, step in enumerate(steps))
    blocks = [a.reshape((1 << len(steps), -1) + a.shape[-1:]) for a in addends]

    def part(which):
        taken = [lax.dynamic_index_in_dim(b, which, 0, keepdims=False) for b in blocks]
        return add_up(taken).astype(BF16)

    result = [part(own)]
    for mask in range(1, 1 << len(steps)):
        flip = sum(step for k, step in enumerate(steps) if mask >> k & 1)
        result.append(permute(part(own ^ mask), axis, [(i, i ^ flip) for i in range(size)]))
    return result


def bits_of(size):
    return [1 << k for k in range(size.bit_length() - 1)]


def first_step(dp, width):
    return SPLIT // (width // dp)


def sum_rest(addends, dp, width):
    rest = [step for step in bits_of(dp) if step != first_step(dp, width)][:-2]
    while rest:
        top, rest = rest[-2:], rest[:-2]
        addends = exchange(addends, "dp", dp, top)
    return addends


def sum_section(addends, sections):
    return add_up(exchange(addends, "section", sections, bits_of(sections)))


def body(
    tokens, resets, init_states, cotangent, mix_gain, mix_in, conv_weight, conv_bias, mix_out,
    mlp_gain, mlp_up, up_bias, mlp_down, down_bias,
):
    dp = lax.axis_size("dp")
    sections = lax.axis_size("section")
    section = lax.axis_index("section")
    width = tokens.shape[2]
    bit = ((lax.axis_index("dp") // first_step(dp, width)) % 2).astype(jnp.int32).reshape(1)

    def own(values, axis):
        return lax.dynamic_index_in_dim(values, section, axis, keepdims=False)

    x0 = own(tokens, 0)
    g4 = own(cotangent, 0)
    masks = chunk_masks(own(resets, 0))
    init = own(init_states, 1)[:, None, :]
    mix_gain = mix_gain[:, None, :]
    mlp_gain = mlp_gain[:, None, :]
    conv_bias = conv_bias[:, None, :]
    up_bias = up_bias[:, None, :]
    down_bias = down_bias[:, None, :]
    mixer_weights = (mix_gain, mix_in, conv_weight, conv_bias, mix_out)
    mlp_weights = (mlp_gain, mlp_up, up_bias, mlp_down, down_bias)

    stack, *stash0, final0 = mixer_forward(0, x0, None, masks, init, *mixer_weights)
    stack, pre0 = mlp_forward(0, stack, 0, *mlp_weights)
    stack, *stash1, final1 = mixer_forward(1, stack, 1, masks, init, *mixer_weights)
    stack, pre1 = mlp_forward(1, stack, 2, *mlp_weights)

    seq = tokens.shape[1]
    dims = (sections, seq, width)
    stacked = [(0, part) for part in range(4)]

    def cuts(*shares):
        edges = [seq * share // 16 for share in shares]
        return [(a, b - a) for a, b in zip(edges, edges[1:])]

    def every(span, buffer=0):
        return [(part, part, *span, buffer) for part in range(4)]

    spans = cuts(0, 4, 10, 14, 16)
    back_mixer = (mix_gain, mix_in, conv_weight, mix_out, bit)
    back_mlp = (mlp_gain, mlp_up, mlp_down, bit)
    cargo = Cargo(1, [stack], stacked, [None], every(spans[0]), dims)
    up1, g3, dbu1, dbd1, dgain_mlp1, acts = mlp_backward(1, stack, 2, g4, pre1, *back_mlp, False, cargo)
    mlp1 = lax.psum_scatter(up1, "dp", scatter_dimension=0, tiled=True)
    cargo = Cargo(2, [stack], stacked, [acts], every(spans[1]), dims)
    in1, g2, small1, dgain_mix1, acts = mixer_backward(
        1, stack, 1, g3, stash1, masks, init, *back_mixer, False, cargo
    )
    mix1 = lax.psum_scatter(in1, "dp", scatter_dimension=0, tiled=True)
    cargo = Cargo(3, [stack], stacked, [acts], every(spans[2]), dims)
    up0_keep, up0_send, g1, dbu0, dbd0, dgain_mlp0, acts = mlp_backward(
        0, stack, 0, g2, pre0, *back_mlp, True, cargo
    )
    (early, late), (early1, late1) = cuts(0, 4, 16), cuts(0, 8, 16)
    jobs = every(spans[3]) + [(4, 3, *early, 1), (5, 2, *early, 1), (6, 1, *early1, 1)]
    cargo = Cargo(
        4, [stack, g3, g2, g1], stacked + [(1, None), (2, None), (3, None)], [acts, None], jobs, dims
    )
    in0_keep, in0_send, g0, small0, dgain_mix0, acts, dxs = mixer_backward(
        0, x0, None, g1, stash0, masks, init, *back_mixer, True, cargo
    )
    jobs = [(3, 0, 0, seq, 0), (0, 3, *late, 0), (1, 2, *late, 0), (2, 1, *late1, 0)]
    cargo = Cargo(5, [g3, g2, g1, g0], None, [dxs], jobs, dims)
    dxs, mlp0, mix0 = finish(cargo, (up0_keep, in0_keep), (up0_send, in0_send), dp, width)
    activations = lax.dynamic_update_index_in_dim(acts, own(stack, 0), section, 0)[None]
    own_dx = jnp.where(section < 2, jnp.where(section == 0, g0, g1), jnp.where(section == 2, g2, g3))
    input_grads = lax.dynamic_update_index_in_dim(dxs, own_dx, section, 0)[None]
    parts = (sum_rest([mlp0], dp, width), sum_rest([mix0], dp, width), [mlp1], [mix1])
    joined = [jnp.concatenate([add_up(part) for part in parts], axis=1).astype(BF16)]
    total = sum_section(joined, sections)
    sizes = [part[0].shape[1] for part in parts]
    mlp0, mix0, mlp1, mix1 = jnp.split(total, [sum(sizes[:k]) for k in range(1, 4)], axis=1)

    devices = dp * sections
    mix_small = jnp.stack([small0, small1])
    count, tile = mix_small.shape[1], mix_small.shape[3] // 2
    mix_small = mix_small.reshape(2, count, 8, 2, tile).transpose(0, 2, 3, 1, 4).reshape(2, 8, -1)
    lines = [
        jnp.stack([dgain_mix0[0], dgain_mix1[0]]),
        jnp.stack([dgain_mlp0[0], dgain_mlp1[0]]),
        jnp.stack([dbd0[0], dbd1[0]]),
        jnp.stack([dbu0[0], dbu1[0]]),
        mix_small[:, :5].reshape(10, -1),
    ]
    final = jnp.concatenate([final0, final1]).reshape(2, sections, -1).transpose(1, 0, 2)
    final = jnp.tile(final.reshape(sections, -1), (dp, 1))
    packed = jnp.concatenate(
        [a.reshape(a.shape[0], devices, -1).transpose(1, 0, 2).reshape(devices, -1) for a in lines]
        + [final],
        axis=1,
    )
    arrived = lax.all_to_all(packed, ("dp", "section"), split_axis=0, concat_axis=0, tiled=True)
    near = lax.dynamic_slice_in_dim(arrived, lax.axis_index("dp") * sections, sections, 0)
    final_states = near[:, -final.shape[1] :].reshape(sections, 2, -1).transpose(1, 0, 2)
    summed = jnp.sum(arrived[:, : -final.shape[1]], axis=0)
    pieces, at = [], 0
    for a in lines:
        size = a.size // devices
        pieces.append(summed[at : at + size].reshape(a.shape[0], -1))
        at += size
    mix_gain_grad, mlp_gain_grad, down_bias_grad, up_bias_grad, conv = pieces
    conv = conv.reshape(2, 5, -1)

    share = width // devices
    mix_big = jnp.stack([mix0, mix1]).reshape(2, share, count, 3 * tile)
    mix_in_grad = (
        mix_big[..., : 2 * tile].reshape(2, share, count, 2, tile).transpose(0, 1, 3, 2, 4)
        .reshape(2, share, -1)
    )
    mix_out_grad = mix_big[..., 2 * tile :].reshape(2, share, -1).transpose(0, 2, 1)
    mlp_big = jnp.stack([mlp0, mlp1]).reshape(2, share, -1, 2, TILE_F)
    mlp_up_grad = mlp_big[:, :, :, 0].reshape(2, share, -1)
    mlp_down_grad = mlp_big[:, :, :, 1].reshape(2, share, -1).transpose(0, 2, 1)
    return (
        activations, input_grads, final_states, mix_gain_grad, mix_in_grad, conv[:, :4], conv[:, 4],
        mix_out_grad, mlp_gain_grad, mlp_up_grad, up_bias_grad, mlp_down_grad, down_bias_grad,
    )


def solution(mesh):
    both = ("dp", "section")
    return jax.shard_map(
        body,
        mesh=mesh,
        in_specs=(
            P("dp", None, None), P("dp", None), P(None, "dp", None), P("dp", None, None),
            P(), P(), P(), P(), P(), P(), P(), P(), P(), P(),
        ),
        out_specs=(
            P("section", "dp", None, None), P("section", "dp", None, None), P(None, "dp", "section"),
            P(None, both), P(None, both, None), P(None, None, both), P(None, both), P(None, None, both),
            P(None, both), P(None, both, None), P(None, both), P(None, None, both), P(None, both),
        ),
        check_vma=False,
    )
```

```python
import functools

import jax
import jax.numpy as jnp
from jax import lax
from jax.experimental import pallas as pl
from jax.experimental.pallas import tpu as pltpu
from jax.sharding import PartitionSpec as P

EPSILON = 1e-06
LANES = 128
GROUP = 8
TILE_C = 512
TILE_F = 512
BIG = 1024
F32 = jnp.float32
BF16 = jnp.bfloat16
ROOT_2_PI = 0.7978845608028654
CUBIC = 0.044715


def dot_nn(left, right):
    return jnp.dot(left, right, preferred_element_type=F32)


def dot_nt(left, right):
    return lax.dot_general(left, right, (((1,), (1,)), ((), ())), preferred_element_type=F32)


def rows_loop(total, step, fn):
    def at(index, carry):
        fn(pl.ds(pl.multiple_of(index * step, step), step))
        return carry

    lax.fori_loop(0, total // step, at, 0)


def to_chunks(natural, target):
    stride = natural.shape[1] // GROUP

    def at(index, carry):
        for tile in range(natural.shape[0]):
            block = jnp.stack(
                [
                    natural[tile, pl.ds(pl.multiple_of(s * stride + index * GROUP, GROUP), GROUP), :]
                    for s in range(GROUP)
                ]
            )
            rows = pl.ds(pl.multiple_of(index * GROUP * GROUP, GROUP * GROUP), GROUP * GROUP)
            mixed = jnp.swapaxes(block, 0, 1).reshape(GROUP * GROUP, LANES)
            target[rows, pl.ds(tile * LANES, LANES)] = mixed.astype(BF16)
        return carry

    lax.fori_loop(0, stride // GROUP, at, 0)


def to_tokens(chunked, natural):
    stride = natural.shape[1] // GROUP

    def at(index, carry):
        for tile in range(natural.shape[0]):
            rows = pl.ds(pl.multiple_of(index * GROUP * GROUP, GROUP * GROUP), GROUP * GROUP)
            block = chunked[rows, pl.ds(tile * LANES, LANES)].reshape(GROUP, GROUP, LANES)
            mixed = jnp.swapaxes(block, 0, 1)
            for s in range(GROUP):
                to = pl.ds(pl.multiple_of(s * stride + index * GROUP, GROUP), GROUP)
                natural[tile, to, :] = mixed[s]
        return carry

    lax.fori_loop(0, stride // GROUP, at, 0)


def transpose_into(source, target):
    def at(index, carry):
        rows = pl.ds(pl.multiple_of(index * LANES, LANES), LANES)
        target[:, rows] = source[rows, :].astype(F32).T.astype(BF16)
        return carry

    lax.fori_loop(0, source.shape[0] // LANES, at, 0)


def inverse_rms(values):
    return lax.rsqrt(jnp.mean(values * values, axis=-1, keepdims=True) + EPSILON)


def put_tiles(natural, rows, values):
    for tile in range(natural.shape[0]):
        natural[tile, rows, :] = values[:, tile * LANES : (tile + 1) * LANES]


def get_tiles(natural, rows):
    return jnp.concatenate([natural[tile, rows, :] for tile in range(natural.shape[0])], axis=1)


def norm_into(x_ref, gain, target):
    def at(rows):
        source = x_ref[rows, :].astype(F32)
        result = source * inverse_rms(source) * gain
        if len(target.shape) == 3:
            put_tiles(target, rows, result)
        else:
            target[rows, :] = result.astype(target.dtype)

    rows_loop(x_ref.shape[0], 128, at)


def previous_chunk(values, first_row):
    rolled = pltpu.roll(values, 1, 0)
    position = lax.broadcasted_iota(jnp.int32, values.shape, 0)
    return jnp.where(position == 0, first_row, rolled)


def following_chunk(values):
    rolled = pltpu.roll(values, GROUP - 1, 0)
    position = lax.broadcasted_iota(jnp.int32, values.shape, 0)
    return jnp.where(position == GROUP - 1, 0.0, rolled)


def sigmoid(values):
    return 0.5 * jnp.tanh(0.5 * values) + 0.5


def repeat_rows(values, rows):
    return jnp.concatenate([values] * (rows // values.shape[0]), axis=0)


STEP = 32
SPLIT = 64
HALO = 24


def mixer_forward_kernel(
    layer, begin, x_ref, gain_ref, wg_ref, wc_ref, kg_ref, kc_ref, bg_ref, bc_ref, wo_ref, keep_ref, init_ref,
    y_ref, p_ref, z_ref, cand_ref, h_ref, final_ref,
    normed, natural, total, proj, local, decay, mask_ref,
):
    step = pl.program_id(0)
    seq = x_ref.shape[0]
    width = wg_ref.shape[1]

    @pl.when(step == 0)
    def _():
        windows_into(keep_ref, mask_ref)
        begin()
        norm_into(x_ref, gain_ref[layer : layer + 1, :], natural)
        to_chunks(natural, normed)
        total[...] = jnp.zeros_like(total)

    def project(index, carry):
        rows = pl.ds(pl.multiple_of(index * BIG, BIG), BIG)
        out_rows = pl.ds(pl.multiple_of(index * BIG + HALO, GROUP), BIG)
        block = normed[rows, :]
        for side, weight in enumerate((wg_ref, wc_ref)):
            lanes = pl.ds(side * width, width)
            piece = dot_nn(block, weight[...])
            proj[out_rows, lanes] = piece
            p_ref[0, rows, lanes] = piece.astype(BF16)
        return carry

    lax.fori_loop(0, seq // BIG, project, 0)
    for offset in range(3):
        last = proj[pl.ds(seq + GROUP * offset, GROUP), :]
        proj[pl.ds(GROUP * offset, GROUP), :] = previous_chunk(last, 0.0)

    def scan_step(index, carry):
        base = pl.multiple_of(index * STEP, STEP)
        rows = pl.ds(base, STEP)
        masks = [None] + [mask_ref[k, rows, :] for k in range(3)]
        updated = []
        for tile in range(width // LANES):
            lanes = pl.ds(tile * LANES, LANES)

            def convolve(shift, taps, bias):
                value = bias[layer : layer + 1, lanes]
                for k in range(4):
                    at = pl.ds(pl.multiple_of(base + HALO - GROUP * k, GROUP), STEP)
                    term = proj[at, pl.ds(shift + tile * LANES, LANES)]
                    if k:
                        term = term * masks[k]
                    value = value + taps[k : k + 1, lanes] * term
                return value

            update = sigmoid(convolve(0, kg_ref, bg_ref))
            candidate = convolve(width, kc_ref, bc_ref)
            z_ref[rows, lanes] = update.astype(BF16)
            cand_ref[rows, lanes] = candidate.astype(BF16)
            retain = (1.0 - update) * masks[1]
            inject = update * candidate
            state, product = carry[tile]
            states, products = [], []
            for g in range(STEP // GROUP):
                here = slice(g * GROUP, (g + 1) * GROUP)
                state = retain[here] * state + inject[here]
                product = retain[here] * product
                states.append(state)
                products.append(product)
            local[rows, lanes] = jnp.concatenate(states, axis=0)
            decay[rows, lanes] = jnp.concatenate(products, axis=0)
            updated.append((state, product))
        return tuple(updated)

    zero = jnp.zeros((GROUP, LANES), F32)
    one = jnp.ones((GROUP, LANES), F32)
    ends = lax.fori_loop(0, seq // STEP, scan_step, ((zero, one),) * (width // LANES))
    entries = []
    for tile, (state, product) in enumerate(ends):
        lanes = pl.ds(tile * LANES, LANES)
        current = init_ref[layer : layer + 1, lanes]
        starts = []
        for g in range(GROUP):
            starts.append(current)
            current = product[g : g + 1] * current + state[g : g + 1]
        final_ref[0:1, lanes] = current
        entries.append(jnp.concatenate(starts, axis=0))
    entry = repeat_rows(jnp.concatenate(entries, axis=1), STEP)

    def fix(index, carry):
        rows = pl.ds(pl.multiple_of(index * STEP, STEP), STEP)
        h_ref[rows, :] = (local[rows, :] + decay[rows, :] * entry).astype(BF16)
        return carry

    lax.fori_loop(0, seq // STEP, fix, 0)

    def output(rows):
        total[rows, :] += dot_nn(h_ref[rows, :], wo_ref[...])

    rows_loop(seq, BIG, output)

    @pl.when(step == pl.num_programs(0) - 1)
    def _():
        to_tokens(total, natural)

        def finish(rows):
            y_ref[rows, :] = (x_ref[rows, :].astype(F32) + get_tiles(natural, rows)).astype(BF16)

        rows_loop(seq, 128, finish)


def norm_backward(x_ref, g_ref, gain, grad_normed, dx_ref, dgain_ref):

    def at(index, carry):
        rows = pl.ds(pl.multiple_of(index * 64, 64), 64)
        source = x_ref[rows, :].astype(F32)
        upstream = g_ref[rows, :].astype(F32)
        incoming = get_tiles(grad_normed, rows) if len(grad_normed.shape) == 3 else grad_normed[rows, :]
        scale = inverse_rms(source)
        scaled = gain * incoming
        mean = jnp.mean(source * scaled, axis=-1, keepdims=True)
        result = upstream + scale * scaled - source * (scale * scale * scale * mean)
        dx_ref[rows, :] = result.astype(BF16)
        return carry + jnp.sum(incoming * source * scale, axis=0, keepdims=True)

    dgain_ref[...] = lax.fori_loop(0, x_ref.shape[0] // 64, at, jnp.zeros(gain.shape, F32))


def put_grad(refs, bit_ref, lanes, values):
    if len(refs) == 1:
        refs[0][:, lanes] = values.astype(BF16)
        return
    mine = bit_ref[0] == 1
    for pair in range(values.shape[0] // (2 * SPLIT)):
        low = values[2 * pair * SPLIT : (2 * pair + 1) * SPLIT].astype(BF16)
        high = values[(2 * pair + 1) * SPLIT : (2 * pair + 2) * SPLIT].astype(BF16)
        rows = pl.ds(pair * SPLIT, SPLIT)
        refs[0][rows, lanes] = jnp.where(mine, high, low)
        refs[1][rows, lanes] = jnp.where(mine, low, high)


def mixer_backward_kernel(
    layer, begin, x_ref, g_ref, gain_ref, wg_ref, wc_ref, kg_ref, kc_ref, wo_ref, keep_ref, init_ref,
    p_ref, z_ref, cand_ref, h_ref, bit_ref, *rest,
):
    *dw, dx_ref, small_ref, dgain_ref = rest[:-10]
    (normed_t, upstream, upstream_t, natural, total, local, decay, dconv, dproj, mask_ref) = rest[-10:]
    step = pl.program_id(0)
    seq = x_ref.shape[0]
    width = wg_ref.shape[1]
    tiles = width // LANES

    @pl.when(step == 0)
    def _():
        windows_into(keep_ref, mask_ref)
        begin()
        norm_into(x_ref, gain_ref[layer : layer + 1, :], natural)
        to_chunks(natural, upstream)
        transpose_into(upstream, normed_t)

        def widen(rows):
            put_tiles(natural, rows, g_ref[rows, :].astype(F32))

        rows_loop(seq, 128, widen)
        to_chunks(natural, upstream)
        transpose_into(upstream, upstream_t)
        total[...] = jnp.zeros_like(total)

    def back_hidden(rows):
        local[rows, :] = dot_nt(upstream[rows, :], wo_ref[...])

    rows_loop(seq, BIG, back_hidden)

    def scan_step(index, carry):
        rows = pl.ds(pl.multiple_of(seq - STEP - index * STEP, STEP), STEP)
        keep = mask_ref[0, rows, :]
        updated = []
        for tile in range(tiles):
            lanes = pl.ds(tile * LANES, LANES)
            retain = (1.0 - z_ref[rows, lanes].astype(F32)) * keep
            grads = local[rows, lanes]
            chain, product = carry[tile]
            chains, products = [], []
            for g in reversed(range(STEP // GROUP)):
                here = slice(g * GROUP, (g + 1) * GROUP)
                value = grads[here] + chain
                chains.append(value)
                products.append(product)
                chain = retain[here] * value
                product = retain[here] * product
            local[rows, lanes] = jnp.concatenate(chains[::-1], axis=0)
            decay[rows, lanes] = jnp.concatenate(products[::-1], axis=0)
            updated.append((chain, product))
        return tuple(updated)

    zero = jnp.zeros((GROUP, LANES), F32)
    one = jnp.ones((GROUP, LANES), F32)
    ends = lax.fori_loop(0, seq // STEP, scan_step, ((zero, one),) * tiles)
    entries = []
    for chain, product in ends:
        current = jnp.zeros((1, LANES), F32)
        starts = [current]
        for g in reversed(range(1, GROUP)):
            current = chain[g : g + 1] + product[g : g + 1] * current
            starts.append(current)
        entries.append(jnp.concatenate(starts[::-1], axis=0))

    last_rows = h_ref[pl.ds(seq - 16, 16), :].astype(F32)[GROUP:]
    before = previous_chunk(last_rows, init_ref[layer : layer + 1, :])

    def gates(index, carry):
        base = pl.multiple_of(index * STEP, STEP)
        rows = pl.ds(base, STEP)
        keep = mask_ref[0, rows, :]
        updated = []
        for tile in range(tiles):
            lanes = pl.ds(tile * LANES, LANES)
            hidden = h_ref[rows, lanes].astype(F32)
            delayed = jnp.concatenate([carry[tile], hidden[: STEP - GROUP]], axis=0)
            error = local[rows, lanes] + decay[rows, lanes] * repeat_rows(entries[tile], STEP)
            update = z_ref[rows, lanes].astype(F32)
            candidate = cand_ref[rows, lanes].astype(F32)
            slope = error * (candidate - keep * delayed)
            dconv[rows, lanes] = slope * (update * (1.0 - update))
            dconv[rows, pl.ds(width + tile * LANES, LANES)] = update * error
            updated.append(hidden[STEP - GROUP :])
        return tuple(updated)

    starting = tuple(before[:, tile * LANES : (tile + 1) * LANES] for tile in range(tiles))
    lax.fori_loop(0, seq // STEP, gates, starting)
    for offset in range(3):
        first = dconv[pl.ds(GROUP * offset, GROUP), :]
        dconv[pl.ds(seq + GROUP * offset, GROUP), :] = following_chunk(first)

    def fold(values):
        result = values[0:GROUP]
        for g in range(1, STEP // GROUP):
            result = result + values[g * GROUP : (g + 1) * GROUP]
        return result

    for side, taps in enumerate((kg_ref, kc_ref)):

        def spread(index, carry):
            base = pl.multiple_of(index * STEP, STEP)
            rows = pl.ds(base, STEP)
            updated = []
            for tile in range(tiles):
                lanes = pl.ds(side * width + tile * LANES, LANES)
                weights = pl.ds(tile * LANES, LANES)
                projected = p_ref[0, rows, lanes].astype(F32)
                sums = carry[tile]
                fresh = []
                value = None
                for k in range(4):
                    at = pl.ds(pl.multiple_of(base + GROUP * k, GROUP), STEP)
                    moved = dconv[at, lanes]
                    if k == 0:
                        bias_sum = sums[4] + fold(moved)
                    else:
                        moved = moved * mask_ref[k - 1, at, :]
                    fresh.append(sums[k] + fold(moved * projected))
                    term = taps[k : k + 1, weights] * moved
                    value = term if value is None else value + term
                fresh.append(bias_sum)
                dproj[rows, lanes] = value.astype(BF16)
                updated.append(tuple(fresh))
            return tuple(updated)

        sums = lax.fori_loop(0, seq // STEP, spread, ((zero,) * 5,) * tiles)
        for tile in range(tiles):
            lanes = pl.ds(side * width + tile * LANES, LANES)
            for k in range(5):
                small_ref[0, k : k + 1, lanes] = jnp.sum(sums[tile][k], axis=0, keepdims=True)
            small_ref[0, 5:8, lanes] = jnp.zeros((3, LANES), F32)

    put_grad(dw, bit_ref, pl.ds(0, 2 * width), dot_nn(normed_t[...], dproj[...]))
    put_grad(dw, bit_ref, pl.ds(2 * width, width), dot_nn(upstream_t[...], h_ref[...]))

    def back_normed(rows):
        total[rows, :] += dot_nt(dproj[rows, pl.ds(0, width)], wg_ref[...]) + dot_nt(
            dproj[rows, pl.ds(width, width)], wc_ref[...]
        )

    rows_loop(seq, BIG, back_normed)

    @pl.when(step == pl.num_programs(0) - 1)
    def _():
        to_tokens(total, natural)
        norm_backward(x_ref, g_ref, gain_ref[layer : layer + 1, :], natural, dx_ref, dgain_ref)


def mlp_forward_kernel(
    layer, begin, x_ref, gain_ref, wu_ref, bu_ref, wd_ref, bd_ref, y_ref, u_ref, normed, total
):
    step = pl.program_id(0)
    seq = x_ref.shape[0]

    @pl.when(step == 0)
    def _():
        begin()
        norm_into(x_ref, gain_ref[layer : layer + 1, :], normed)

        def start(rows):
            total[rows, :] = x_ref[rows, :].astype(F32) + bd_ref[layer : layer + 1, :]

        rows_loop(seq, 128, start)

    def at(rows):
        pre = dot_nn(normed[rows, :], wu_ref[...]) + bu_ref[layer : layer + 1, :]
        u_ref[rows, :] = pre.astype(BF16)
        inner = ROOT_2_PI * (pre + CUBIC * (pre * pre * pre))
        active = (0.5 * pre * (1.0 + jnp.tanh(inner))).astype(BF16)
        total[rows, :] += dot_nn(active, wd_ref[...])

    rows_loop(seq, BIG, at)

    @pl.when(step == pl.num_programs(0) - 1)
    def _():
        def finish(rows):
            y_ref[rows, :] = total[rows, :].astype(BF16)

        rows_loop(seq, 128, finish)


def gelu_parts(pre):
    square = pre * pre
    bent = jnp.tanh(pre * (ROOT_2_PI + (ROOT_2_PI * CUBIC) * square))
    half = 0.5 * pre
    slope = 0.5 + 0.5 * bent + half * (1.0 - bent * bent) * (
        ROOT_2_PI + (3.0 * ROOT_2_PI * CUBIC) * square
    )
    return (half + half * bent).astype(BF16), slope


def mlp_backward_kernel(
    layer, begin, x_ref, g_ref, gain_ref, wu_ref, wd_ref, u_ref, bit_ref, *rest,
):
    *dw, dx_ref, dbu_ref, dbd_ref, dgain_ref = rest[:-5]
    normed_t, upstream_t, total, active, dpre = rest[-5:]
    step = pl.program_id(0)
    seq = x_ref.shape[0]
    width = wu_ref.shape[1]

    @pl.when(step == 0)
    def _():
        begin()
        norm_into(x_ref, gain_ref[layer : layer + 1, :], active)
        transpose_into(active, normed_t)
        transpose_into(g_ref, upstream_t)

        def at(index, carry):
            rows = pl.ds(pl.multiple_of(index * 64, 64), 64)
            return carry + jnp.sum(g_ref[rows, :].astype(F32), axis=0, keepdims=True)

        dbd_ref[...] = lax.fori_loop(0, seq // 64, at, jnp.zeros(dbd_ref.shape, F32))
        total[...] = jnp.zeros_like(total)

    def at(index, carry):
        rows = pl.ds(pl.multiple_of(index * BIG, BIG), BIG)
        pre = u_ref[rows, :].astype(F32)
        active[rows, :], slope = gelu_parts(pre)
        low = (dot_nt(g_ref[rows, :], wd_ref[...]) * slope).astype(BF16)
        dpre[rows, :] = low
        total[rows, :] += dot_nt(low, wu_ref[...])
        return carry + jnp.sum(low.astype(F32), axis=0, keepdims=True)

    dbu_ref[...] = lax.fori_loop(0, seq // BIG, at, jnp.zeros(dbu_ref.shape, F32))

    put_grad(dw, bit_ref, pl.ds(0, width), dot_nn(normed_t[...], dpre[...]))
    put_grad(dw, bit_ref, pl.ds(width, width), dot_nn(upstream_t[...], active[...]))

    @pl.when(step == pl.num_programs(0) - 1)
    def _():
        norm_backward(x_ref, g_ref, gain_ref[layer : layer + 1, :], total, dx_ref, dgain_ref)


def shape(dims, kind):
    return jax.ShapeDtypeStruct(dims, kind)


PARAMS = pltpu.CompilerParams(
    dimension_semantics=("arbitrary",), vmem_limit_bytes=56 * 1024 * 1024
)


SCALAR = pl.BlockSpec(memory_space=pltpu.SMEM)
ANYWHERE = pl.BlockSpec(memory_space=pl.ANY)
MESH = pl.DeviceIdType.MESH
SECTIONS = 4
FAR = 2


def greet_sections(section):
    barrier = pltpu.get_barrier_semaphore()
    for by in range(1, SECTIONS):
        other = (section + by) % SECTIONS
        pl.semaphore_signal(barrier, inc=1, device_id={"section": other}, device_id_type=MESH)


def delivery(jobs, sources, buffers, send_sems, recv_sems):
    section = lax.axis_index("section")

    def sends(job):
        return functools.reduce(jnp.logical_or, [section == sender for sender in job[5]])

    def copy(number, sender):
        source, part, first, count, buffer, _ = jobs[number]
        rows = pl.ds(first, count)
        return pltpu.make_async_remote_copy(
            src_ref=sources[source].at[rows],
            dst_ref=buffers[buffer].at[sender, rows],
            send_sem=send_sems.at[number],
            recv_sem=recv_sems.at[number, sender],
            device_id={"section": part},
            device_id_type=MESH,
        )

    def start(first=0, last=len(jobs)):
        for number, job in list(enumerate(jobs))[first:last]:

            @pl.when(sends(job))
            def _(number=number):
                copy(number, section).start()

    def wait():
        for number, job in enumerate(jobs):

            @pl.when(sends(job))
            def _(number=number):
                copy(number, section).wait_send()

            @pl.when(section == job[1])
            def _(number=number, job=job):
                for sender in job[5]:
                    copy(number, sender).wait_recv()

    return start, wait


def after(value, *others):
    return lax.optimization_barrier((value,) + others)


class Cargo:
    def __init__(self, collective_id, arrays, buffers, jobs, dims):
        self.collective_id = collective_id
        self.arrays = list(arrays)
        self.old = [b for b in buffers if b is not None]
        self.buffers = buffers
        self.jobs = jobs
        self.dims = dims


def call(kernel, cargo, *, grid, in_specs, out_specs, out_shape, scratch_shapes, cost_estimate, name, args, aliases=None):
    aliases = dict(aliases or {})
    if cargo is None:
        return pl.pallas_call(
            functools.partial(kernel, lambda: None), grid=grid, in_specs=in_specs, out_specs=out_specs, out_shape=out_shape,
            scratch_shapes=scratch_shapes, compiler_params=PARAMS, cost_estimate=cost_estimate, name=name,
            input_output_aliases=aliases,
        )(*args)
    n_in, n_out = len(in_specs), len(out_specs)
    n_array, n_old, n_buffer = len(cargo.arrays), len(cargo.old), len(cargo.buffers)

    def carrying(*refs):
        ins, refs = refs[:n_in], refs[n_in:]
        arrays, refs = refs[:n_array], refs[n_array + n_old :]
        outs, refs = refs[:n_out], refs[n_out:]
        buffers, refs = refs[:n_buffer], refs[n_buffer:]
        own, (send_sems, recv_sems) = refs[:-2], refs[-2:]
        start, wait = delivery(cargo.jobs, arrays, buffers, send_sems, recv_sems)
        step = pl.program_id(0)

        @pl.when(step == 0)
        def _():
            greet_sections(lax.axis_index("section"))

        def begin():
            pl.semaphore_wait(pltpu.get_barrier_semaphore(), SECTIONS - 1)
            start()

        kernel(begin, *ins, *outs, *own)

        @pl.when(step == pl.num_programs(0) - 1)
        def _():
            wait()

    old = 0
    for number, buffer in enumerate(cargo.buffers):
        if buffer is not None:
            aliases[n_in + n_array + old] = n_out + number
            old += 1
    jobs = len(cargo.jobs)
    return pl.pallas_call(
        carrying,
        grid=grid,
        in_specs=list(in_specs) + [ANYWHERE] * (n_array + n_old),
        out_specs=list(out_specs) + [ANYWHERE] * n_buffer,
        out_shape=list(out_shape) + (cargo.dims if isinstance(cargo.dims, list) else [shape(cargo.dims, BF16)] * n_buffer),
        scratch_shapes=list(scratch_shapes)
        + [pltpu.SemaphoreType.DMA((jobs,)), pltpu.SemaphoreType.DMA((jobs, SECTIONS))],
        compiler_params=pltpu.CompilerParams(
            dimension_semantics=("arbitrary",), vmem_limit_bytes=56 * 1024 * 1024,
            collective_id=cargo.collective_id, has_side_effects=True,
        ),
        cost_estimate=cost_estimate,
        name=name,
        input_output_aliases=aliases,
    )(*args, *cargo.arrays, *cargo.old)


def cost(seq, microseconds):
    return pl.CostEstimate(
        flops=int(microseconds * 1.1e9), bytes_accessed=seq * 4096, transcendentals=0
    )


def whole(dims):
    return pl.BlockSpec(dims, lambda i: (0,) * len(dims))


def mixer_specs(layer, width, hidden, tile):
    count = hidden // tile
    return dict(
        gate=pl.BlockSpec((None, width, tile), lambda i: (layer, 0, i)),
        cand=pl.BlockSpec((None, width, tile), lambda i: (layer, 0, count + i)),
        tap_gate=pl.BlockSpec((None, 4, tile), lambda i: (layer, 0, i)),
        tap_cand=pl.BlockSpec((None, 4, tile), lambda i: (layer, 0, count + i)),
        bias_gate=pl.BlockSpec((2, tile), lambda i: (0, i)),
        bias_cand=pl.BlockSpec((2, tile), lambda i: (0, count + i)),
        out=pl.BlockSpec((None, tile, width), lambda i: (layer, i, 0)),
        gain=whole((2, width)),
        init=pl.BlockSpec((2, tile), lambda i: (0, i)),
    )


def mixer_forward(layer, x, masks, init, gain, weight_in, taps, bias, weight_out, cargo=None):
    seq, width = x.shape
    hidden = init.shape[1]
    tile = TILE_C
    count = hidden // tile
    spec = mixer_specs(layer, width, hidden, tile)
    column = pl.BlockSpec((seq, tile), lambda i: (0, i))
    return call(
        functools.partial(mixer_forward_kernel, layer),
        cargo,
        grid=(count,),
        in_specs=[
            whole(x.shape), spec["gain"], spec["gate"], spec["cand"], spec["tap_gate"], spec["tap_cand"],
            spec["bias_gate"], spec["bias_cand"], spec["out"], whole(masks.shape), spec["init"],
        ],
        out_specs=[
            whole(x.shape), pl.BlockSpec((1, seq, 2 * tile), lambda i: (i, 0, 0)), column, column, column,
            pl.BlockSpec((1, tile), lambda i: (0, i)),
        ],
        out_shape=[
            shape(x.shape, BF16), shape((count, seq, 2 * tile), BF16), shape((seq, hidden), BF16),
            shape((seq, hidden), BF16), shape((seq, hidden), BF16), shape((1, hidden), F32),
        ],
        scratch_shapes=[
            pltpu.VMEM((seq, width), BF16), pltpu.VMEM((width // LANES, seq, LANES), F32), pltpu.VMEM((seq, width), F32),
            pltpu.VMEM((seq + HALO, 2 * tile), F32), pltpu.VMEM((seq, tile), F32), pltpu.VMEM((seq, tile), F32),
            pltpu.VMEM((3, seq + HALO, LANES), F32),
        ],
        cost_estimate=cost(seq, 15),
        name="mixer_forward",
        args=(x, gain, weight_in, weight_in, taps, taps, bias, bias, weight_out, masks, init),
    )


def grad_outputs(width, tile, total, split):
    rows = width // 2 if split else width
    parts = 2 if split else 1
    return (
        [pl.BlockSpec((rows, tile), lambda i: (0, i))] * parts,
        [shape((rows, total), BF16)] * parts,
    )


def mixer_backward(layer, x, g, stash, masks, init, gain, weight_in, taps, weight_out, bit, split, cargo=None):
    seq, width = g.shape
    hidden = init.shape[1]
    tile = TILE_C
    count = hidden // tile
    spec = mixer_specs(layer, width, hidden, tile)
    column = pl.BlockSpec((seq, tile), lambda i: (0, i))
    dw_specs, dw_shapes = grad_outputs(width, 3 * tile, 3 * hidden, split)
    return call(
        functools.partial(mixer_backward_kernel, layer),
        cargo,
        grid=(count,),
        in_specs=[
            whole(x.shape), whole(g.shape), spec["gain"], spec["gate"], spec["cand"], spec["tap_gate"],
            spec["tap_cand"], spec["out"], whole(masks.shape), spec["init"],
            pl.BlockSpec((1, seq, 2 * tile), lambda i: (i, 0, 0)), column, column, column, SCALAR,
        ],
        out_specs=[
            *dw_specs, whole(g.shape), pl.BlockSpec((1, 8, 2 * tile), lambda i: (i, 0, 0)), whole((1, width)),
        ],
        out_shape=[
            *dw_shapes, shape(g.shape, BF16), shape((count, 8, 2 * tile), F32),
            shape((1, width), F32),
        ],
        scratch_shapes=[
            pltpu.VMEM((width, seq), BF16), pltpu.VMEM((seq, width), BF16), pltpu.VMEM((width, seq), BF16),
            pltpu.VMEM((width // LANES, seq, LANES), F32), pltpu.VMEM((seq, width), F32), pltpu.VMEM((seq, tile), F32),
            pltpu.VMEM((seq, tile), F32), pltpu.VMEM((seq + HALO, 2 * tile), F32),
            pltpu.VMEM((seq, 2 * tile), BF16), pltpu.VMEM((3, seq + HALO, LANES), F32),
        ],
        cost_estimate=cost(seq, 30),
        name="mixer_backward",
        args=(x, g, gain, weight_in, weight_in, taps, taps, weight_out, masks, init, *stash, bit),
    )


def mlp_forward(layer, x, gain, weight_up, bias_up, weight_down, bias_down, cargo=None):
    seq, width = x.shape
    inner = weight_up.shape[2]
    tile = TILE_F
    return call(
        functools.partial(mlp_forward_kernel, layer),
        cargo,
        grid=(inner // tile,),
        in_specs=[
            whole(x.shape), whole(gain.shape),
            pl.BlockSpec((None, width, tile), lambda i: (layer, 0, i)),
            pl.BlockSpec((2, tile), lambda i: (0, i)),
            pl.BlockSpec((None, tile, width), lambda i: (layer, i, 0)),
            whole(bias_down.shape),
        ],
        out_specs=[whole(x.shape), pl.BlockSpec((seq, tile), lambda i: (0, i))],
        out_shape=[shape(x.shape, BF16), shape((seq, inner), BF16)],
        scratch_shapes=[pltpu.VMEM((seq, width), BF16), pltpu.VMEM((seq, width), F32)],
        cost_estimate=cost(seq, 10),
        name="mlp_forward",
        args=(x, gain, weight_up, bias_up, weight_down, bias_down),
    )


def mlp_backward(layer, x, g, pre, gain, weight_up, weight_down, bit, split, cargo=None):
    seq, width = g.shape
    inner = weight_up.shape[2]
    tile = TILE_F
    dw_specs, dw_shapes = grad_outputs(width, 2 * tile, 2 * inner, split)
    return call(
        functools.partial(mlp_backward_kernel, layer),
        cargo,
        grid=(inner // tile,),
        in_specs=[
            whole(x.shape), whole(g.shape), whole(gain.shape),
            pl.BlockSpec((None, width, tile), lambda i: (layer, 0, i)),
            pl.BlockSpec((None, tile, width), lambda i: (layer, i, 0)),
            pl.BlockSpec((seq, tile), lambda i: (0, i)), SCALAR,
        ],
        out_specs=[
            *dw_specs, whole(g.shape), pl.BlockSpec((1, tile), lambda i: (0, i)), whole((1, width)), whole((1, width)),
        ],
        out_shape=[
            *dw_shapes, shape(g.shape, BF16), shape((1, inner), F32),
            shape((1, width), F32), shape((1, width), F32),
        ],
        scratch_shapes=[
            pltpu.VMEM((width, seq), BF16), pltpu.VMEM((width, seq), BF16), pltpu.VMEM((seq, width), F32),
            pltpu.VMEM((seq, tile), BF16), pltpu.VMEM((seq, tile), BF16),
        ],
        cost_estimate=cost(seq, 20),
        name="mlp_backward",
        args=(x, g, gain, weight_up, weight_down, pre, bit),
    )


def chunk_masks(resets):
    seq = resets.shape[0]
    cut = (1 - resets).astype(F32).reshape(GROUP, seq // GROUP).T
    ends = jnp.zeros((3, 1), F32)
    before = jnp.concatenate([ends, cut[-3:, :-1]], axis=1)
    ahead = jnp.concatenate([cut[:3, 1:], ends], axis=1)
    rows = jnp.concatenate([before, cut, ahead]).reshape(seq + 2 * HALO, 1)
    return jnp.broadcast_to(rows, (seq + 2 * HALO, LANES))


def windows_into(keep_ref, mask_ref):
    count = mask_ref.shape[1]
    first = keep_ref[pl.ds(HALO, count), :]
    second = first * keep_ref[pl.ds(HALO - GROUP, count), :]
    mask_ref[0] = first
    mask_ref[1] = second
    mask_ref[2] = second * keep_ref[pl.ds(HALO - 2 * GROUP, count), :]


def permute(x, axis, pairs):
    return lax.ppermute(x, axis, pairs)


def last_kernel(jobs, split, dp, inner, n_array, *refs):
    arrays, refs = refs[:n_array], refs[n_array:]
    keeps, sends, refs = refs[0:3], refs[3:6], refs[6:]
    if inner:
        later, refs = refs[0:2], refs[2:]
    cotangent, wu_any, wd_any, gain_ref, bu_ref, bd_ref, refs = *refs[:6], refs[6:]
    buffers, refs = refs[2:4], refs[4:]
    acts, dxs = buffers
    outs, refs = (refs[:5], refs[5:]) if inner else (refs[:3], refs[3:])
    wu, wd, x_own, g_own, normed, total, grad, y_own, d_own, dgain, redo_sems = refs[-11:]
    refs = refs[:-11]
    kept, got, parts, landed, refs = refs[0:3], refs[3:6], refs[6:9], refs[9:12], refs[12:]
    if inner:
        level, first, second, third, refs = refs[0:5], refs[5:10], refs[10:15], refs[15:20], refs[20:]
        z_sems, refs = refs[0], refs[1:]
    else:
        sums, refs = refs[0:3], refs[3:]
    send_sems, recv_sems, local_sems, core_sems, part_sems = refs
    section = lax.axis_index("section")
    where = lax.axis_index("dp")
    bit = (where // split) % 2
    partner = where + split * (1 - 2 * bit)
    steps = [step for step in bits_of(dp) if step != split][-2:]
    low_bit, high_bit = (where // steps[0]) % 2, (where // steps[1]) % 2
    mine = low_bit + 2 * high_bit
    near_bit, far_bit = section % 2, section // 2

    def flipped(mask):
        low, high = mask % 2, mask // 2
        new_low = low_bit + low * (1 - 2 * low_bit)
        new_high = high_bit + high * (1 - 2 * high_bit)
        device = where + steps[0] * (new_low - low_bit) + steps[1] * (new_high - high_bit)
        return new_low + 2 * new_high, device

    def near_copy(n):
        return pltpu.make_async_remote_copy(
            src_ref=level[n].at[:, 1 - near_bit], dst_ref=first[n], send_sem=z_sems.at[0, n], recv_sem=z_sems.at[1, n],
            device_id={"section": section + 1 - 2 * near_bit}, device_id_type=MESH,
        )

    def far_copy(n):
        return pltpu.make_async_remote_copy(
            src_ref=second[n].at[1 - far_bit], dst_ref=third[n], send_sem=z_sems.at[2, n], recv_sem=z_sems.at[3, n],
            device_id={"section": section + 2 - 4 * far_bit}, device_id_type=MESH,
        )

    def near_sum(n):
        for half in range(2):
            both = level[n][half, near_bit].astype(F32) + first[n][half].astype(F32)
            second[n][half] = both.astype(second[n].dtype)

    barrier = pltpu.get_barrier_semaphore()
    for by in range(1, SECTIONS):
        other = (section + by) % SECTIONS
        pl.semaphore_signal(barrier, inc=1, device_id={"section": other}, device_id_type=MESH)
    pl.semaphore_signal(barrier, inc=1, device_id={"dp": partner}, device_id_type=MESH)
    for mask in (1, 2, 3):
        pl.semaphore_signal(barrier, inc=1, device_id={"dp": flipped(mask)[1]}, device_id_type=MESH)
    loads = [pltpu.make_async_copy(keeps[n], kept[n], local_sems.at[n]) for n in range(3)]
    if inner:
        loads += [pltpu.make_async_copy(later[n], level[3 + n], local_sems.at[3 + n]) for n in range(2)]
    for load in loads:
        load.start()
    pl.semaphore_wait(barrier, SECTIONS + 3)

    start, wait = delivery(jobs, arrays, buffers, send_sems, recv_sems)
    redoes = section == SECTIONS - 1

    def fetch(row):
        return (
            pltpu.make_async_copy(acts.at[row], x_own, redo_sems.at[0]),
            pltpu.make_async_copy(cotangent.at[row], g_own, redo_sems.at[1]),
        )

    def fetch_weights():
        return (
            pltpu.make_async_copy(wu_any.at[1], wu, redo_sems.at[2]),
            pltpu.make_async_copy(wd_any.at[1], wd, redo_sems.at[3]),
        )

    def put(row):
        return (
            pltpu.make_async_copy(y_own, acts.at[row], redo_sems.at[4]),
            pltpu.make_async_copy(d_own, dxs.at[row], redo_sems.at[5]),
        )

    @pl.when(redoes)
    def _():
        for one in fetch(0) + fetch_weights():
            one.start()

    def redo(row):
        for one in fetch(row) + (fetch_weights() if row == 0 else put(row - 1)):
            one.wait()
        gain = gain_ref[1:2, :]
        norm_into(x_own, gain, normed)

        def begin_total(rows):
            total[rows, :] = x_own[rows, :].astype(F32) + bd_ref[1:2, :]

        rows_loop(total.shape[0], 128, begin_total)
        grad[...] = jnp.zeros_like(grad)

        def tile(index, carry):
            cut = pl.ds(pl.multiple_of(index * TILE_F, TILE_F), TILE_F)
            up, down = wu[:, cut], wd[cut, :]
            pre = dot_nn(normed[...], up) + bu_ref[1:2, cut]
            active, slope = gelu_parts(pre)
            total[...] += dot_nn(active, down)
            low = (dot_nt(g_own[...], down) * slope).astype(BF16)
            grad[...] += dot_nt(low, up)
            return carry

        lax.fori_loop(0, wu.shape[1] // TILE_F, tile, 0)

        def end_total(rows):
            y_own[rows, :] = total[rows, :].astype(BF16)

        rows_loop(total.shape[0], 128, end_total)
        norm_backward(x_own, g_own, gain, grad, d_own, dgain)
        for one in put(row) + (fetch(row + 1) if row + 1 < FAR else ()):
            one.start()

    swaps = []
    for n in range(3):
        swap = pltpu.make_async_remote_copy(
            src_ref=sends[n], dst_ref=got[n], send_sem=core_sems.at[0, n], recv_sem=core_sems.at[1, n],
            device_id={"dp": partner}, device_id_type=MESH,
        )
        swap.start()
        swaps.append(swap)
    start(0, -1)
    for load in loads:
        load.wait()
    near = {}
    if inner:
        for n in (3, 4):
            near[n] = near_copy(n)
            near[n].start()
    moves = []
    for n in range(3):
        swaps[n].wait()
        rows = kept[n].shape[0] // 4
        for mask in (1, 2, 3):
            quarter, device = flipped(mask)
            taken = pl.ds(pl.multiple_of(quarter * rows, rows), rows)
            pair = kept[n][taken, :].astype(F32) + got[n][taken, :].astype(F32)
            parts[n][mask - 1] = pair.astype(parts[n].dtype)
            move = pltpu.make_async_remote_copy(
                src_ref=parts[n].at[mask - 1], dst_ref=landed[n].at[mask - 1],
                send_sem=part_sems.at[0, n, mask - 1], recv_sem=part_sems.at[1, n, mask - 1],
                device_id={"dp": device}, device_id_type=MESH,
            )
            move.start()
            moves.append(move)
    pl.when(redoes)(functools.partial(redo, 0))
    for n in range(3):
        rows = kept[n].shape[0] // 4
        taken = pl.ds(pl.multiple_of(mine * rows, rows), rows)
        summed = kept[n][taken, :].astype(F32) + got[n][taken, :].astype(F32)
        for mask in (1, 2, 3):
            moves[3 * n + mask - 1].wait()
            summed = summed + landed[n][mask - 1].astype(F32)
        if inner:
            share = rows // SECTIONS
            for part in range(SECTIONS):
                level[n][part // 2, part % 2] = summed[part * share : (part + 1) * share].astype(level[n].dtype)
            near[n] = near_copy(n)
            near[n].start()
        else:
            sums[n][...] = summed.astype(sums[n].dtype)
            store = pltpu.make_async_copy(sums[n], outs[n], local_sems.at[n])
            store.start()
            store.wait()
    if not inner:
        start(len(jobs) - 1)
    pl.when(redoes)(functools.partial(redo, 1))
    if inner:
        far = {}
        for n in (3, 4, 0, 1, 2):
            near[n].wait()
            near_sum(n)
            far[n] = far_copy(n)
            far[n].start()
        start(len(jobs) - 1)
        for n in (3, 4, 0, 1, 2):
            far[n].wait()
            block = n // 3
            final = second[n][far_bit].astype(F32) + third[n][...].astype(F32)
            if n == 2:
                outs[4][...] = final
            elif n in (1, 4):
                cand = outs[0].shape[2] // 2
                for at in range(0, final.shape[1], 3 * TILE_C):
                    to = at // 3
                    outs[0][block, :, pl.ds(to, TILE_C)] = final[:, at : at + TILE_C]
                    outs[0][block, :, pl.ds(cand + to, TILE_C)] = final[:, at + TILE_C : at + 2 * TILE_C]
                    outs[1][block, :, pl.ds(to, TILE_C)] = final[:, at + 2 * TILE_C : at + 3 * TILE_C]
            else:
                for at in range(0, final.shape[1], 2 * TILE_F):
                    outs[2][block, :, pl.ds(at // 2, TILE_F)] = final[:, at : at + TILE_F]
                    outs[3][block, :, pl.ds(at // 2, TILE_F)] = final[:, at + TILE_F : at + 2 * TILE_F]

    @pl.when(redoes)
    def _():
        for one in put(1):
            one.wait()

    wait()


def finish(cargo, keeps, sends, later, redo, dp, width):
    inner = later is not None
    columns = [k.shape[1] for k in keeps]
    kinds = [k.dtype for k in keeps]
    rows = keeps[0].shape[0] // 4
    share = rows // SECTIONS
    n_array = len(cargo.arrays)
    jobs = len(cargo.jobs)
    lots = list(zip(columns + columns[:2], kinds + kinds[:2]))
    if inner:
        later = [a.reshape(2, 2, share, -1) for a in later]
        wide = columns[1] // 3
        outs = [shape((2, share, c), F32) for c in (2 * wide, wide, columns[0] // 2, columns[0] // 2)]
        outs += [shape((share, columns[2]), F32)]
        out_specs = [pl.BlockSpec(memory_space=pltpu.VMEM)] * 5
        extra = [pltpu.VMEM((2, 2, share, c), kind) for c, kind in lots]
        extra += [pltpu.VMEM((2, share, c), kind) for c, kind in lots] * 2
        extra += [pltpu.VMEM((share, c), kind) for c, kind in lots]
        extra += [pltpu.SemaphoreType.DMA((4, 5))]
    else:
        later = []
        outs = [shape((rows, c), kind) for c, kind in zip(columns, kinds)]
        out_specs = [ANYWHERE] * 3
        extra = [pltpu.VMEM((rows, c), kind) for c, kind in zip(columns, kinds)]
    n_in = n_array + 6 + len(later)
    return pl.pallas_call(
        functools.partial(last_kernel, cargo.jobs, first_step(dp, width), dp, inner, n_array),
        in_specs=[ANYWHERE] * (n_in + 3) + [pl.BlockSpec(memory_space=pltpu.VMEM)] * 3 + [ANYWHERE] * 2,
        out_specs=[ANYWHERE] * 2 + out_specs,
        out_shape=[shape(cargo.dims, BF16)] * 2 + outs,
        scratch_shapes=[pltpu.VMEM(k.shape, k.dtype) for k in keeps] * 2
        + [pltpu.VMEM((3, rows, c), kind) for c, kind in zip(columns, kinds)] * 2
        + extra
        + [
            pltpu.SemaphoreType.DMA((jobs,)), pltpu.SemaphoreType.DMA((jobs, SECTIONS)),
            pltpu.SemaphoreType.DMA((5,)), pltpu.SemaphoreType.DMA((2, 3)), pltpu.SemaphoreType.DMA((2, 3, 3)),
        ]
        + [pltpu.VMEM(redo[1].shape[1:], BF16), pltpu.VMEM(redo[2].shape[1:], BF16)]
        + [pltpu.VMEM(cargo.dims[1:], BF16)] * 3 + [pltpu.VMEM(cargo.dims[1:], F32)] * 2
        + [pltpu.VMEM(cargo.dims[1:], BF16)] * 2
        + [pltpu.VMEM((1, width), F32), pltpu.SemaphoreType.DMA((6,))],
        compiler_params=pltpu.CompilerParams(
            vmem_limit_bytes=56 * 1024 * 1024, collective_id=cargo.collective_id, has_side_effects=True
        ),
        input_output_aliases={n_in + 6: 0, n_in + 7: 1},
        cost_estimate=cost(1024, 100),
        name="finish",
    )(*cargo.arrays, *keeps, *sends, *later, *redo, *cargo.old)


def add_up(pieces):
    return functools.reduce(jnp.add, [piece.astype(F32) for piece in pieces])


def exchange(addends, axis, size, steps):
    where = lax.axis_index(axis)
    own = sum(((where // step) % 2) << k for k, step in enumerate(steps))
    blocks = [a.reshape((1 << len(steps), -1) + a.shape[-1:]) for a in addends]

    def part(which):
        taken = [lax.dynamic_index_in_dim(b, which, 0, keepdims=False) for b in blocks]
        return add_up(taken).astype(addends[0].dtype)

    result = [part(own)]
    for mask in range(1, 1 << len(steps)):
        flip = sum(step for k, step in enumerate(steps) if mask >> k & 1)
        result.append(permute(part(own ^ mask), axis, [(i, i ^ flip) for i in range(size)]))
    return result


def bits_of(size):
    return [1 << k for k in range(size.bit_length() - 1)]


def first_step(dp, width):
    return SPLIT // (width // dp)


def sum_rest(addends, dp, width):
    rest = [step for step in bits_of(dp) if step != first_step(dp, width)][:-2]
    while rest:
        top, rest = rest[-2:], rest[:-2]
        addends = exchange(addends, "dp", dp, top)
    return addends


def sum_section(addends, sections):
    return add_up(exchange(addends, "section", sections, bits_of(sections)))


def body(
    tokens, resets, init_states, cotangent, mix_gain, mix_in, conv_weight, conv_bias, mix_out,
    mlp_gain, mlp_up, up_bias, mlp_down, down_bias,
):
    dp = lax.axis_size("dp")
    sections = lax.axis_size("section")
    section = lax.axis_index("section")
    width = tokens.shape[2]
    bit = ((lax.axis_index("dp") // first_step(dp, width)) % 2).astype(jnp.int32).reshape(1)

    def own(values, axis):
        return lax.dynamic_index_in_dim(values, section, axis, keepdims=False)

    x0 = own(tokens, 0)
    g4 = own(cotangent, 0)
    masks = chunk_masks(own(resets, 0))
    init = own(init_states, 1)
    mixer_weights = (mix_gain, mix_in, conv_weight, conv_bias, mix_out)
    mlp_weights = (mlp_gain, mlp_up, up_bias, mlp_down, down_bias)
    seq = tokens.shape[1]
    dims = (sections, seq, width)
    sent = {}

    def some(source, part, share, buffer=0, senders=None):
        if senders is None:
            senders = tuple(k for k in range(sections) if k != part)
        kind = (buffer, part, senders)
        first = sent.get(kind, 0)
        sent[kind] = first + share
        return (source, part, seq * first // 32, seq * share // 32, buffer, senders)

    distant, close = tuple(range(FAR)), tuple(range(FAR, sections - 1))

    x1, *stash0, final0 = mixer_forward(0, x0, masks, init, *mixer_weights)
    x2, pre0 = mlp_forward(0, x1, *mlp_weights)
    cargo = Cargo(1, [x1, x2], [None], [some(0, 0, 5), some(1, 1, 5)], dims)
    x3, *stash1, final1, acts = mixer_forward(1, x2, masks, init, *mixer_weights, cargo)
    cargo = Cargo(2, [x1, x2, x3], [acts], [some(0, 0, 2), some(1, 1, 2), some(2, 2, 6)], dims)
    x4, pre1, acts = mlp_forward(1, x3, *mlp_weights, cargo)

    back_mixer = (mix_gain, mix_in, conv_weight, mix_out, bit)
    back_mlp = (mlp_gain, mlp_up, mlp_down, bit)
    xs = [x1, x2, x3, x4]
    jobs = [some(0, 0, 7), some(1, 1, 7), some(2, 2, 7), some(2, 3, 7, 0, distant), some(3, 3, 7, 0, close)]
    quarters = jnp.concatenate([final0, final1, jnp.zeros((GROUP - 2, final0.shape[1]), F32)])
    quarters = jnp.split(quarters, sections, axis=1)
    jobs += [some(4 + part, part, 32, 2)[:2] + (0, GROUP, 1) + some(4 + part, part, 32, 3)[5:] for part in range(sections)]
    shapes = [shape(dims, BF16), shape((sections,) + quarters[0].shape, F32)]
    up1, g3, dbu1, dbd1, dgain_mlp1, acts, ends = mlp_backward(
        1, x3, g4, pre1, *back_mlp, False, Cargo(3, xs + quarters, [acts, None], jobs, shapes)
    )
    here = lax.broadcasted_iota(jnp.int32, (sections, 1, 1), 0) == section
    ends = jnp.where(here, lax.dynamic_index_in_dim(jnp.stack(quarters), section, 0), ends)
    final_states = ends[:, :2].transpose(1, 0, 2)
    mlp1 = lax.psum_scatter(up1, "dp", scatter_dimension=0, tiled=True)
    jobs = [some(0, 0, 9), some(1, 1, 9), some(2, 2, 9), some(2, 3, 9, 0, distant), some(3, 3, 9, 0, close)]
    in1, g2, small1, dgain_mix1, acts = mixer_backward(
        1, x2, g3, stash1, masks, init, *back_mixer, False, Cargo(4, xs, [acts], jobs, dims)
    )
    mix1 = lax.psum_scatter(in1, "dp", scatter_dimension=0, tiled=True)
    jobs = [some(0, 0, 7), some(1, 1, 7), some(2, 2, 7), some(2, 3, 7, 0, distant), some(3, 3, 8, 0, close)]
    up0_keep, up0_send, g1, dbu0, dbd0, dgain_mlp0, acts = mlp_backward(
        0, x1, g2, pre0, *back_mlp, True, Cargo(5, xs, [acts], jobs, dims)
    )
    jobs = [some(0, 0, 2), some(1, 1, 2), some(2, 2, 3), some(2, 3, 9, 0, distant), some(3, 3, 8, 0, close)]
    jobs += [some(4, 3, 16, 1, close), some(5, 2, 6, 1), some(6, 1, 14, 1)]
    cargo = Cargo(6, xs + [g3, g2, g1], [acts, None], jobs, dims)
    g1, mlp1 = after(g1, mlp1)
    in0_keep, in0_send, g0, small0, dgain_mix0, acts, dxs = mixer_backward(
        0, x0, g1, stash0, masks, init, *back_mixer, True, cargo
    )
    jobs = [some(3, 0, 32, 1, (2, 3)), some(3, 0, 16, 1, (1,)), some(2, 1, 18, 1), some(0, 3, 16, 1, close), some(1, 2, 26, 1)]
    jobs += [some(3, 0, 16, 1, (1,))]
    cargo = Cargo(7, [g3, g2, g1, g0], [acts, dxs], jobs, dims)
    redo = (cotangent, mlp_up, mlp_down, mlp_gain, up_bias, down_bias)
    devices = dp * sections
    mix_small = jnp.stack([small0, small1])
    count, tile = mix_small.shape[1], mix_small.shape[3] // 2
    mix_small = mix_small.reshape(2, count, 8, 2, tile).transpose(0, 2, 3, 1, 4).reshape(2, 8, -1)
    lines = [
        jnp.stack([dgain_mix0[0], dgain_mix1[0]]),
        jnp.stack([dgain_mlp0[0], dgain_mlp1[0]]),
        jnp.stack([dbd0[0], dbd1[0]]),
        jnp.stack([dbu0[0], dbu1[0]]),
        mix_small[:, :5].reshape(10, -1),
    ]
    packed = jnp.concatenate(
        [a.reshape(a.shape[0], devices, -1).transpose(1, 0, 2).reshape(devices, -1) for a in lines], axis=1
    )
    share = width // devices
    length = packed.shape[1]
    packed = jnp.pad(packed, ((0, 0), (0, share * LANES - length))).reshape(-1, 2, SPLIT, LANES)

    def half(which):
        return lax.dynamic_index_in_dim(packed, which, 1, keepdims=False).reshape(-1, LANES)

    halves = ((up0_keep, in0_keep, half(bit[0])), (up0_send, in0_send, half(1 - bit[0])))
    inner = dp == 8 and first_step(dp, width) == 1
    if inner:
        acts, dxs, mix_in_grad, mix_out_grad, mlp_up_grad, mlp_down_grad, summed = finish(
            cargo, *halves, (mlp1, mix1), redo, dp, width
        )
    else:
        acts, dxs, mlp0, mix0, summed = finish(cargo, *halves, None, redo, dp, width)
        parts = [sum_rest([part], dp, width) for part in (mlp0, mix0, summed)] + [[mlp1], [mix1]]
        mlp0, mix0, summed, mlp1, mix1 = [
            sum_section([add_up(part).astype(part[0].dtype)], sections) for part in parts
        ]
        mix_big = jnp.stack([mix0, mix1]).reshape(2, share, -1, 3, TILE_C)
        mix_in_grad = mix_big[:, :, :, :2].transpose(0, 1, 3, 2, 4).reshape(2, share, -1)
        mix_out_grad = mix_big[:, :, :, 2].reshape(2, share, -1)
        mlp_big = jnp.stack([mlp0, mlp1]).reshape(2, share, -1, 2, TILE_F)
        mlp_up_grad = mlp_big[:, :, :, 0].reshape(2, share, -1)
        mlp_down_grad = mlp_big[:, :, :, 1].reshape(2, share, -1)
    mix_out_grad = mix_out_grad.transpose(0, 2, 1)
    mlp_down_grad = mlp_down_grad.transpose(0, 2, 1)

    def with_own(buffer, parts):
        mine = jnp.where(
            section < 2, jnp.where(section == 0, parts[0], parts[1]), jnp.where(section == 2, parts[2], parts[3])
        )
        here = lax.broadcasted_iota(jnp.int32, (sections, 1, 1), 0) == section
        return jnp.where(here, mine[None], buffer)[None]

    activations = with_own(acts, xs)
    input_grads = with_own(dxs, [g0, g1, g2, g3])

    summed = summed.reshape(-1)[:length]
    pieces, at = [], 0
    for a in lines:
        size = a.size // devices
        pieces.append(summed[at : at + size].reshape(a.shape[0], -1))
        at += size
    mix_gain_grad, mlp_gain_grad, down_bias_grad, up_bias_grad, conv = pieces
    conv = conv.reshape(2, 5, -1)

    return (
        activations, input_grads, final_states, mix_gain_grad, mix_in_grad, conv[:, :4], conv[:, 4],
        mix_out_grad, mlp_gain_grad, mlp_up_grad, up_bias_grad, mlp_down_grad, down_bias_grad,
    )


def solution(mesh):
    both = ("dp", "section")
    return jax.shard_map(
        body,
        mesh=mesh,
        in_specs=(
            P("dp", None, None), P("dp", None), P(None, "dp", None), P("dp", None, None),
            P(), P(), P(), P(), P(), P(), P(), P(), P(), P(),
        ),
        out_specs=(
            P("section", "dp", None, None), P("section", "dp", None, None), P(None, "dp", "section"),
            P(None, both), P(None, both, None), P(None, None, both), P(None, both), P(None, None, both),
            P(None, both), P(None, both, None), P(None, both), P(None, None, both), P(None, both),
        ),
        check_vma=False,
    )
```

```python
import functools

import jax
import jax.numpy as jnp
from jax import lax
from jax.experimental import pallas as pl
from jax.experimental.pallas import tpu as pltpu
from jax.sharding import PartitionSpec as P

EPSILON = 1e-06
LANES = 128
GROUP = 8
TILE_C = 512
TILE_F = 512
BIG = 1024
F32 = jnp.float32
BF16 = jnp.bfloat16
ROOT_2_PI = 0.7978845608028654
CUBIC = 0.044715


def dot_nn(left, right):
    return jnp.dot(left, right, preferred_element_type=F32)


def dot_nt(left, right):
    return lax.dot_general(left, right, (((1,), (1,)), ((), ())), preferred_element_type=F32)


def rows_loop(total, step, fn):
    def at(index, carry):
        fn(pl.ds(pl.multiple_of(index * step, step), step))
        return carry

    lax.fori_loop(0, total // step, at, 0)


def to_chunks(natural, target):
    stride = natural.shape[1] // GROUP

    def at(index, carry):
        for tile in range(natural.shape[0]):
            block = jnp.stack(
                [
                    natural[tile, pl.ds(pl.multiple_of(s * stride + index * GROUP, GROUP), GROUP), :]
                    for s in range(GROUP)
                ]
            )
            rows = pl.ds(pl.multiple_of(index * GROUP * GROUP, GROUP * GROUP), GROUP * GROUP)
            mixed = jnp.swapaxes(block, 0, 1).reshape(GROUP * GROUP, LANES)
            target[rows, pl.ds(tile * LANES, LANES)] = mixed.astype(BF16)
        return carry

    lax.fori_loop(0, stride // GROUP, at, 0, unroll=16)


def to_tokens(chunked, natural):
    stride = natural.shape[1] // GROUP

    def at(index, carry):
        for tile in range(natural.shape[0]):
            rows = pl.ds(pl.multiple_of(index * GROUP * GROUP, GROUP * GROUP), GROUP * GROUP)
            block = chunked[rows, pl.ds(tile * LANES, LANES)].reshape(GROUP, GROUP, LANES)
            mixed = jnp.swapaxes(block, 0, 1)
            for s in range(GROUP):
                to = pl.ds(pl.multiple_of(s * stride + index * GROUP, GROUP), GROUP)
                natural[tile, to, :] = mixed[s]
        return carry

    lax.fori_loop(0, stride // GROUP, at, 0, unroll=16)


def transpose_into(source, target):
    def at(index, carry):
        rows = pl.ds(pl.multiple_of(index * LANES, LANES), LANES)
        target[:, rows] = source[rows, :].astype(F32).T.astype(BF16)
        return carry

    lax.fori_loop(0, source.shape[0] // LANES, at, 0, unroll=8)


def inverse_rms(values):
    return lax.rsqrt(jnp.mean(values * values, axis=-1, keepdims=True) + EPSILON)


def put_tiles(natural, rows, values):
    for tile in range(natural.shape[0]):
        natural[tile, rows, :] = values[:, tile * LANES : (tile + 1) * LANES]


def get_tiles(natural, rows):
    return jnp.concatenate([natural[tile, rows, :] for tile in range(natural.shape[0])], axis=1)


def norm_into(x_ref, gain, target):
    def at(rows):
        source = x_ref[rows, :].astype(F32)
        result = source * inverse_rms(source) * gain
        if len(target.shape) == 3:
            put_tiles(target, rows, result)
        else:
            target[rows, :] = result.astype(target.dtype)

    rows_loop(x_ref.shape[0], 1024, at)


def previous_chunk(values, first_row):
    rolled = pltpu.roll(values, 1, 0)
    position = lax.broadcasted_iota(jnp.int32, values.shape, 0)
    return jnp.where(position == 0, first_row, rolled)


def following_chunk(values):
    rolled = pltpu.roll(values, GROUP - 1, 0)
    position = lax.broadcasted_iota(jnp.int32, values.shape, 0)
    return jnp.where(position == GROUP - 1, 0.0, rolled)


def sigmoid(values):
    return 0.5 * jnp.tanh(0.5 * values) + 0.5


def repeat_rows(values, rows):
    return jnp.concatenate([values] * (rows // values.shape[0]), axis=0)


STEP = 64
SPLIT = 64
HALO = 24


def mixer_forward_kernel(
    layer, begin, x_ref, gain_ref, wg_ref, wc_ref, kg_ref, kc_ref, bg_ref, bc_ref, wo_ref, keep_ref, init_ref,
    y_ref, p_ref, z_ref, cand_ref, h_ref, final_ref,
    normed, natural, total, proj, local, decay, mask_ref,
):
    step = pl.program_id(0)
    seq = x_ref.shape[0]
    width = wg_ref.shape[1]

    @pl.when(step == 0)
    def _():
        windows_into(keep_ref, mask_ref)
        begin()
        norm_into(x_ref, gain_ref[layer : layer + 1, :], natural)
        to_chunks(natural, normed)
        total[...] = jnp.zeros_like(total)

    def project(index, carry):
        rows = pl.ds(pl.multiple_of(index * BIG, BIG), BIG)
        out_rows = pl.ds(pl.multiple_of(index * BIG + HALO, GROUP), BIG)
        block = normed[rows, :]
        for side, weight in enumerate((wg_ref, wc_ref)):
            lanes = pl.ds(side * width, width)
            piece = dot_nn(block, weight[...])
            proj[out_rows, lanes] = piece
            p_ref[0, rows, lanes] = piece.astype(BF16)
        return carry

    lax.fori_loop(0, seq // BIG, project, 0)
    for offset in range(3):
        last = proj[pl.ds(seq + GROUP * offset, GROUP), :]
        proj[pl.ds(GROUP * offset, GROUP), :] = previous_chunk(last, 0.0)

    def scan_step(index, carry):
        base = pl.multiple_of(index * STEP, STEP)
        rows = pl.ds(base, STEP)
        masks = [None] + [mask_ref[k, rows, :] for k in range(3)]
        updated = []
        for tile in range(width // LANES):
            lanes = pl.ds(tile * LANES, LANES)

            def convolve(shift, taps, bias):
                value = bias[layer : layer + 1, lanes]
                for k in range(4):
                    at = pl.ds(pl.multiple_of(base + HALO - GROUP * k, GROUP), STEP)
                    term = proj[at, pl.ds(shift + tile * LANES, LANES)]
                    if k:
                        term = term * masks[k]
                    value = value + taps[k : k + 1, lanes] * term
                return value

            update = sigmoid(convolve(0, kg_ref, bg_ref))
            candidate = convolve(width, kc_ref, bc_ref)
            z_ref[rows, lanes] = update.astype(BF16)
            cand_ref[rows, lanes] = candidate.astype(BF16)
            retain = (1.0 - update) * masks[1]
            inject = update * candidate
            state, product = carry[tile]
            states, products = [], []
            for g in range(STEP // GROUP):
                here = slice(g * GROUP, (g + 1) * GROUP)
                state = retain[here] * state + inject[here]
                product = retain[here] * product
                states.append(state)
                products.append(product)
            local[rows, lanes] = jnp.concatenate(states, axis=0)
            decay[rows, lanes] = jnp.concatenate(products, axis=0)
            updated.append((state, product))
        return tuple(updated)

    zero = jnp.zeros((GROUP, LANES), F32)
    one = jnp.ones((GROUP, LANES), F32)
    ends = lax.fori_loop(0, seq // STEP, scan_step, ((zero, one),) * (width // LANES))
    entries = []
    for tile, (state, product) in enumerate(ends):
        lanes = pl.ds(tile * LANES, LANES)
        current = init_ref[layer : layer + 1, lanes]
        starts = []
        for g in range(GROUP):
            starts.append(current)
            current = product[g : g + 1] * current + state[g : g + 1]
        final_ref[0:1, lanes] = current
        entries.append(jnp.concatenate(starts, axis=0))
    entry = repeat_rows(jnp.concatenate(entries, axis=1), STEP)

    def fix(index, carry):
        rows = pl.ds(pl.multiple_of(index * STEP, STEP), STEP)
        h_ref[rows, :] = (local[rows, :] + decay[rows, :] * entry).astype(BF16)
        return carry

    lax.fori_loop(0, seq // STEP, fix, 0)

    def output(rows):
        total[rows, :] += dot_nn(h_ref[rows, :], wo_ref[...])

    rows_loop(seq, BIG, output)

    @pl.when(step == pl.num_programs(0) - 1)
    def _():
        to_tokens(total, natural)

        def finish(rows):
            y_ref[rows, :] = (x_ref[rows, :].astype(F32) + get_tiles(natural, rows)).astype(BF16)

        rows_loop(seq, 1024, finish)


def norm_backward(x_ref, g_ref, gain, grad_normed, dx_ref, dgain_ref):

    def at(index, carry):
        rows = pl.ds(pl.multiple_of(index * 1024, 1024), 1024)
        source = x_ref[rows, :].astype(F32)
        upstream = g_ref[rows, :].astype(F32)
        incoming = get_tiles(grad_normed, rows) if len(grad_normed.shape) == 3 else grad_normed[rows, :]
        scale = inverse_rms(source)
        scaled = gain * incoming
        mean = jnp.mean(source * scaled, axis=-1, keepdims=True)
        result = upstream + scale * scaled - source * (scale * scale * scale * mean)
        dx_ref[rows, :] = result.astype(BF16)
        return carry + jnp.sum(incoming * source * scale, axis=0, keepdims=True)

    dgain_ref[...] = lax.fori_loop(0, x_ref.shape[0] // 1024, at, jnp.zeros(gain.shape, F32))


def put_grad(refs, bit_ref, lanes, values):
    if len(refs) == 1:
        refs[0][:, lanes] = values.astype(BF16)
        return
    mine = bit_ref[0] == 1
    for pair in range(values.shape[0] // (2 * SPLIT)):
        low = values[2 * pair * SPLIT : (2 * pair + 1) * SPLIT].astype(BF16)
        high = values[(2 * pair + 1) * SPLIT : (2 * pair + 2) * SPLIT].astype(BF16)
        rows = pl.ds(pair * SPLIT, SPLIT)
        refs[0][rows, lanes] = jnp.where(mine, high, low)
        refs[1][rows, lanes] = jnp.where(mine, low, high)


def mixer_backward_kernel(
    layer, begin, x_ref, g_ref, gain_ref, wg_ref, wc_ref, kg_ref, kc_ref, wo_ref, keep_ref, init_ref,
    p_ref, z_ref, cand_ref, h_ref, bit_ref, *rest,
):
    *dw, dx_ref, small_ref, dgain_ref = rest[:-10]
    (normed_t, upstream, upstream_t, natural, total, local, decay, dconv, dproj, mask_ref) = rest[-10:]
    step = pl.program_id(0)
    seq = x_ref.shape[0]
    width = wg_ref.shape[1]
    tiles = width // LANES

    @pl.when(step == 0)
    def _():
        windows_into(keep_ref, mask_ref)
        begin()
        norm_into(x_ref, gain_ref[layer : layer + 1, :], natural)
        to_chunks(natural, upstream)
        transpose_into(upstream, normed_t)

        def widen(rows):
            put_tiles(natural, rows, g_ref[rows, :].astype(F32))

        rows_loop(seq, 1024, widen)
        to_chunks(natural, upstream)
        transpose_into(upstream, upstream_t)
        total[...] = jnp.zeros_like(total)

    def back_hidden(rows):
        local[rows, :] = dot_nt(upstream[rows, :], wo_ref[...])

    rows_loop(seq, BIG, back_hidden)

    def scan_step(index, carry):
        rows = pl.ds(pl.multiple_of(seq - STEP - index * STEP, STEP), STEP)
        keep = mask_ref[0, rows, :]
        updated = []
        for tile in range(tiles):
            lanes = pl.ds(tile * LANES, LANES)
            retain = (1.0 - z_ref[rows, lanes].astype(F32)) * keep
            grads = local[rows, lanes]
            chain, product = carry[tile]
            chains, products = [], []
            for g in reversed(range(STEP // GROUP)):
                here = slice(g * GROUP, (g + 1) * GROUP)
                value = grads[here] + chain
                chains.append(value)
                products.append(product)
                chain = retain[here] * value
                product = retain[here] * product
            local[rows, lanes] = jnp.concatenate(chains[::-1], axis=0)
            decay[rows, lanes] = jnp.concatenate(products[::-1], axis=0)
            updated.append((chain, product))
        return tuple(updated)

    zero = jnp.zeros((GROUP, LANES), F32)
    one = jnp.ones((GROUP, LANES), F32)
    ends = lax.fori_loop(0, seq // STEP, scan_step, ((zero, one),) * tiles)
    entries = []
    for chain, product in ends:
        current = jnp.zeros((1, LANES), F32)
        starts = [current]
        for g in reversed(range(1, GROUP)):
            current = chain[g : g + 1] + product[g : g + 1] * current
            starts.append(current)
        entries.append(jnp.concatenate(starts[::-1], axis=0))

    last_rows = h_ref[pl.ds(seq - 16, 16), :].astype(F32)[GROUP:]
    before = previous_chunk(last_rows, init_ref[layer : layer + 1, :])

    def gates(index, carry):
        base = pl.multiple_of(index * STEP, STEP)
        rows = pl.ds(base, STEP)
        keep = mask_ref[0, rows, :]
        updated = []
        for tile in range(tiles):
            lanes = pl.ds(tile * LANES, LANES)
            hidden = h_ref[rows, lanes].astype(F32)
            delayed = jnp.concatenate([carry[tile], hidden[: STEP - GROUP]], axis=0)
            error = local[rows, lanes] + decay[rows, lanes] * repeat_rows(entries[tile], STEP)
            update = z_ref[rows, lanes].astype(F32)
            candidate = cand_ref[rows, lanes].astype(F32)
            slope = error * (candidate - keep * delayed)
            dconv[rows, lanes] = slope * (update * (1.0 - update))
            dconv[rows, pl.ds(width + tile * LANES, LANES)] = update * error
            updated.append(hidden[STEP - GROUP :])
        return tuple(updated)

    starting = tuple(before[:, tile * LANES : (tile + 1) * LANES] for tile in range(tiles))
    lax.fori_loop(0, seq // STEP, gates, starting)
    for offset in range(3):
        first = dconv[pl.ds(GROUP * offset, GROUP), :]
        dconv[pl.ds(seq + GROUP * offset, GROUP), :] = following_chunk(first)

    def fold(values):
        result = values[0:GROUP]
        for g in range(1, STEP // GROUP):
            result = result + values[g * GROUP : (g + 1) * GROUP]
        return result

    for side, taps in enumerate((kg_ref, kc_ref)):

        def spread(index, carry):
            base = pl.multiple_of(index * STEP, STEP)
            rows = pl.ds(base, STEP)
            updated = []
            for tile in range(tiles):
                lanes = pl.ds(side * width + tile * LANES, LANES)
                weights = pl.ds(tile * LANES, LANES)
                projected = p_ref[0, rows, lanes].astype(F32)
                sums = carry[tile]
                fresh = []
                value = None
                for k in range(4):
                    at = pl.ds(pl.multiple_of(base + GROUP * k, GROUP), STEP)
                    moved = dconv[at, lanes]
                    if k == 0:
                        bias_sum = sums[4] + fold(moved)
                    else:
                        moved = moved * mask_ref[k - 1, at, :]
                    fresh.append(sums[k] + fold(moved * projected))
                    term = taps[k : k + 1, weights] * moved
                    value = term if value is None else value + term
                fresh.append(bias_sum)
                dproj[rows, lanes] = value.astype(BF16)
                updated.append(tuple(fresh))
            return tuple(updated)

        sums = lax.fori_loop(0, seq // STEP, spread, ((zero,) * 5,) * tiles)
        for tile in range(tiles):
            lanes = pl.ds(side * width + tile * LANES, LANES)
            for k in range(5):
                small_ref[0, k : k + 1, lanes] = jnp.sum(sums[tile][k], axis=0, keepdims=True)
            small_ref[0, 5:8, lanes] = jnp.zeros((3, LANES), F32)

    put_grad(dw, bit_ref, pl.ds(0, 2 * width), dot_nn(normed_t[...], dproj[...]))
    put_grad(dw, bit_ref, pl.ds(2 * width, width), dot_nn(upstream_t[...], h_ref[...]))

    def back_normed(rows):
        total[rows, :] += dot_nt(dproj[rows, pl.ds(0, width)], wg_ref[...]) + dot_nt(
            dproj[rows, pl.ds(width, width)], wc_ref[...]
        )

    rows_loop(seq, BIG, back_normed)

    @pl.when(step == pl.num_programs(0) - 1)
    def _():
        to_tokens(total, natural)
        norm_backward(x_ref, g_ref, gain_ref[layer : layer + 1, :], natural, dx_ref, dgain_ref)


def mlp_forward_kernel(
    layer, begin, x_ref, gain_ref, wu_ref, bu_ref, wd_ref, bd_ref, y_ref, u_ref, normed, total
):
    step = pl.program_id(0)
    seq = x_ref.shape[0]

    @pl.when(step == 0)
    def _():
        begin()
        norm_into(x_ref, gain_ref[layer : layer + 1, :], normed)

        def start(rows):
            total[rows, :] = x_ref[rows, :].astype(F32) + bd_ref[layer : layer + 1, :]

        rows_loop(seq, 1024, start)

    def at(rows):
        pre = dot_nn(normed[rows, :], wu_ref[...]) + bu_ref[layer : layer + 1, :]
        u_ref[rows, :] = pre.astype(BF16)
        inner = ROOT_2_PI * (pre + CUBIC * (pre * pre * pre))
        active = (0.5 * pre * (1.0 + jnp.tanh(inner))).astype(BF16)
        total[rows, :] += dot_nn(active, wd_ref[...])

    rows_loop(seq, BIG, at)

    @pl.when(step == pl.num_programs(0) - 1)
    def _():
        def finish(rows):
            y_ref[rows, :] = total[rows, :].astype(BF16)

        rows_loop(seq, 1024, finish)


def gelu_parts(pre):
    square = pre * pre
    bent = jnp.tanh(pre * (ROOT_2_PI + (ROOT_2_PI * CUBIC) * square))
    half = 0.5 * pre
    slope = 0.5 + 0.5 * bent + half * (1.0 - bent * bent) * (
        ROOT_2_PI + (3.0 * ROOT_2_PI * CUBIC) * square
    )
    return (half + half * bent).astype(BF16), slope


def mlp_backward_kernel(
    layer, begin, x_ref, g_ref, gain_ref, wu_ref, wd_ref, u_ref, bit_ref, *rest,
):
    *dw, dx_ref, dbu_ref, dbd_ref, dgain_ref = rest[:-5]
    normed_t, upstream_t, total, active, dpre = rest[-5:]
    step = pl.program_id(0)
    seq = x_ref.shape[0]
    width = wu_ref.shape[1]

    @pl.when(step == 0)
    def _():
        begin()
        norm_into(x_ref, gain_ref[layer : layer + 1, :], active)
        transpose_into(active, normed_t)
        transpose_into(g_ref, upstream_t)

        def at(index, carry):
            rows = pl.ds(pl.multiple_of(index * 1024, 1024), 1024)
            return carry + jnp.sum(g_ref[rows, :].astype(F32), axis=0, keepdims=True)

        dbd_ref[...] = lax.fori_loop(0, seq // 1024, at, jnp.zeros(dbd_ref.shape, F32))
        total[...] = jnp.zeros_like(total)

    def at(index, carry):
        rows = pl.ds(pl.multiple_of(index * BIG, BIG), BIG)
        pre = u_ref[rows, :].astype(F32)
        active[rows, :], slope = gelu_parts(pre)
        low = (dot_nt(g_ref[rows, :], wd_ref[...]) * slope).astype(BF16)
        dpre[rows, :] = low
        total[rows, :] += dot_nt(low, wu_ref[...])
        return carry + jnp.sum(low.astype(F32), axis=0, keepdims=True)

    dbu_ref[...] = lax.fori_loop(0, seq // BIG, at, jnp.zeros(dbu_ref.shape, F32))

    put_grad(dw, bit_ref, pl.ds(0, width), dot_nn(normed_t[...], dpre[...]))
    put_grad(dw, bit_ref, pl.ds(width, width), dot_nn(upstream_t[...], active[...]))

    @pl.when(step == pl.num_programs(0) - 1)
    def _():
        norm_backward(x_ref, g_ref, gain_ref[layer : layer + 1, :], total, dx_ref, dgain_ref)


def shape(dims, kind):
    return jax.ShapeDtypeStruct(dims, kind)


PARAMS = pltpu.CompilerParams(
    dimension_semantics=("arbitrary",), vmem_limit_bytes=56 * 1024 * 1024
)


SCALAR = pl.BlockSpec(memory_space=pltpu.SMEM)
ANYWHERE = pl.BlockSpec(memory_space=pl.ANY)
MESH = pl.DeviceIdType.MESH
SECTIONS = 4
FAR = 2


def greet_sections(section):
    barrier = pltpu.get_barrier_semaphore()
    for by in range(1, SECTIONS):
        other = (section + by) % SECTIONS
        pl.semaphore_signal(barrier, inc=1, device_id={"section": other}, device_id_type=MESH)


def delivery(jobs, sources, buffers, send_sems, recv_sems, relay_sems=None):
    section = lax.axis_index("section")
    near_bit = section % 2

    def near(number):
        _, source, buffer = jobs[number]
        return pltpu.make_async_remote_copy(
            src_ref=sources[source].at[:, 1 - near_bit],
            dst_ref=buffers[buffer],
            send_sem=send_sems.at[number],
            recv_sem=recv_sems.at[number, 0],
            device_id={"section": section + 1 - 2 * near_bit},
            device_id_type=MESH,
        )

    def relay(number, row):
        _, part, first, count, buffer, _ = jobs[number]
        rows = pl.ds(first, count)
        return pltpu.make_async_remote_copy(
            src_ref=buffers[buffer].at[row, rows],
            dst_ref=buffers[buffer].at[row, rows],
            send_sem=relay_sems.at[0, number, row],
            recv_sem=recv_sems.at[number, row],
            device_id={"section": part},
            device_id_type=MESH,
        )

    def sends(job):
        return functools.reduce(jnp.logical_or, [section == sender for sender in job[5]])

    def copy(number, sender):
        source, part, first, count, buffer, _ = jobs[number]
        rows = pl.ds(first, count)
        return pltpu.make_async_remote_copy(
            src_ref=sources[source].at[rows],
            dst_ref=buffers[buffer].at[sender, rows],
            send_sem=send_sems.at[number],
            recv_sem=recv_sems.at[number, sender],
            device_id={"section": part},
            device_id_type=MESH,
        )

    def start(first=0, last=len(jobs)):
        for number, job in list(enumerate(jobs))[first:last]:
            if job[0] is None:
                near(number).start()
                continue
            if job[0] == "relay":

                @pl.when(section == job[1] + 1)
                def _(number=number, job=job):
                    for row in job[5]:
                        relay(number, row).start()

                continue

            @pl.when(sends(job))
            def _(number=number):
                copy(number, section).start()

    def wait():
        for number, job in enumerate(jobs):
            if job[0] is None:
                near(number).wait()
                continue
            if job[0] == "relay":

                @pl.when(section == job[1] + 1)
                def _(number=number, job=job):
                    for row in job[5]:
                        relay(number, row).wait_send()

                @pl.when(section == job[1])
                def _(number=number, job=job):
                    for row in job[5]:
                        relay(number, row).wait_recv()

                continue

            @pl.when(sends(job))
            def _(number=number):
                copy(number, section).wait_send()

            @pl.when(section == job[1])
            def _(number=number, job=job):
                for sender in job[5]:
                    copy(number, sender).wait_recv()

    return start, wait


def after(value, *others):
    return lax.optimization_barrier((value,) + others)


class Cargo:
    def __init__(self, collective_id, arrays, buffers, jobs, dims):
        self.collective_id = collective_id
        self.arrays = list(arrays)
        self.old = [b for b in buffers if b is not None]
        self.buffers = buffers
        self.jobs = jobs
        self.dims = dims


def call(kernel, cargo, *, grid, in_specs, out_specs, out_shape, scratch_shapes, cost_estimate, name, args, aliases=None):
    aliases = dict(aliases or {})
    if cargo is None:
        return pl.pallas_call(
            functools.partial(kernel, lambda: None), grid=grid, in_specs=in_specs, out_specs=out_specs, out_shape=out_shape,
            scratch_shapes=scratch_shapes, compiler_params=PARAMS, cost_estimate=cost_estimate, name=name,
            input_output_aliases=aliases,
        )(*args)
    n_in, n_out = len(in_specs), len(out_specs)
    n_array, n_old, n_buffer = len(cargo.arrays), len(cargo.old), len(cargo.buffers)

    def carrying(*refs):
        ins, refs = refs[:n_in], refs[n_in:]
        arrays, refs = refs[:n_array], refs[n_array + n_old :]
        outs, refs = refs[:n_out], refs[n_out:]
        buffers, refs = refs[:n_buffer], refs[n_buffer:]
        own, (send_sems, recv_sems, relay_sems) = refs[:-3], refs[-3:]
        start, wait = delivery(cargo.jobs, arrays, buffers, send_sems, recv_sems, relay_sems)
        step = pl.program_id(0)

        @pl.when(step == 0)
        def _():
            greet_sections(lax.axis_index("section"))

        def begin():
            pl.semaphore_wait(pltpu.get_barrier_semaphore(), SECTIONS - 1)
            start()

        kernel(begin, *ins, *outs, *own)

        @pl.when(step == pl.num_programs(0) - 1)
        def _():
            wait()

    old = 0
    for number, buffer in enumerate(cargo.buffers):
        if buffer is not None:
            aliases[n_in + n_array + old] = n_out + number
            old += 1
    jobs = len(cargo.jobs)
    return pl.pallas_call(
        carrying,
        grid=grid,
        in_specs=list(in_specs) + [ANYWHERE] * (n_array + n_old),
        out_specs=list(out_specs) + [ANYWHERE] * n_buffer,
        out_shape=list(out_shape) + (cargo.dims if isinstance(cargo.dims, list) else [shape(cargo.dims, BF16)] * n_buffer),
        scratch_shapes=list(scratch_shapes)
        + [pltpu.SemaphoreType.DMA((jobs,)), pltpu.SemaphoreType.DMA((jobs, SECTIONS))]
        + [pltpu.SemaphoreType.DMA((1, jobs, SECTIONS))],
        compiler_params=pltpu.CompilerParams(
            dimension_semantics=("arbitrary",), vmem_limit_bytes=56 * 1024 * 1024,
            collective_id=cargo.collective_id, has_side_effects=True,
        ),
        cost_estimate=cost_estimate,
        name=name,
        input_output_aliases=aliases,
    )(*args, *cargo.arrays, *cargo.old)


def cost(seq, microseconds):
    return pl.CostEstimate(
        flops=int(microseconds * 1.1e9), bytes_accessed=seq * 4096, transcendentals=0
    )


def whole(dims):
    return pl.BlockSpec(dims, lambda i: (0,) * len(dims))


def mixer_specs(layer, width, hidden, tile):
    count = hidden // tile
    return dict(
        gate=pl.BlockSpec((None, width, tile), lambda i: (layer, 0, i)),
        cand=pl.BlockSpec((None, width, tile), lambda i: (layer, 0, count + i)),
        tap_gate=pl.BlockSpec((None, 4, tile), lambda i: (layer, 0, i)),
        tap_cand=pl.BlockSpec((None, 4, tile), lambda i: (layer, 0, count + i)),
        bias_gate=pl.BlockSpec((2, tile), lambda i: (0, i)),
        bias_cand=pl.BlockSpec((2, tile), lambda i: (0, count + i)),
        out=pl.BlockSpec((None, tile, width), lambda i: (layer, i, 0)),
        gain=whole((2, width)),
        init=pl.BlockSpec((2, tile), lambda i: (0, i)),
    )


def mixer_forward(layer, x, masks, init, gain, weight_in, taps, bias, weight_out, cargo=None):
    seq, width = x.shape
    hidden = init.shape[1]
    tile = TILE_C
    count = hidden // tile
    spec = mixer_specs(layer, width, hidden, tile)
    column = pl.BlockSpec((seq, tile), lambda i: (0, i))
    return call(
        functools.partial(mixer_forward_kernel, layer),
        cargo,
        grid=(count,),
        in_specs=[
            whole(x.shape), spec["gain"], spec["gate"], spec["cand"], spec["tap_gate"], spec["tap_cand"],
            spec["bias_gate"], spec["bias_cand"], spec["out"], whole(masks.shape), spec["init"],
        ],
        out_specs=[
            whole(x.shape), pl.BlockSpec((1, seq, 2 * tile), lambda i: (i, 0, 0)), column, column, column,
            pl.BlockSpec((1, tile), lambda i: (0, i)),
        ],
        out_shape=[
            shape(x.shape, BF16), shape((count, seq, 2 * tile), BF16), shape((seq, hidden), BF16),
            shape((seq, hidden), BF16), shape((seq, hidden), BF16), shape((1, hidden), F32),
        ],
        scratch_shapes=[
            pltpu.VMEM((seq, width), BF16), pltpu.VMEM((width // LANES, seq, LANES), F32), pltpu.VMEM((seq, width), F32),
            pltpu.VMEM((seq + HALO, 2 * tile), F32), pltpu.VMEM((seq, tile), F32), pltpu.VMEM((seq, tile), F32),
            pltpu.VMEM((3, seq + HALO, LANES), F32),
        ],
        cost_estimate=cost(seq, 15),
        name="mixer_forward",
        args=(x, gain, weight_in, weight_in, taps, taps, bias, bias, weight_out, masks, init),
    )


def grad_outputs(width, tile, total, split):
    rows = width // 2 if split else width
    parts = 2 if split else 1
    return (
        [pl.BlockSpec((rows, tile), lambda i: (0, i))] * parts,
        [shape((rows, total), BF16)] * parts,
    )


def mixer_backward(layer, x, g, stash, masks, init, gain, weight_in, taps, weight_out, bit, split, cargo=None):
    seq, width = g.shape
    hidden = init.shape[1]
    tile = TILE_C
    count = hidden // tile
    spec = mixer_specs(layer, width, hidden, tile)
    column = pl.BlockSpec((seq, tile), lambda i: (0, i))
    dw_specs, dw_shapes = grad_outputs(width, 3 * tile, 3 * hidden, split)
    return call(
        functools.partial(mixer_backward_kernel, layer),
        cargo,
        grid=(count,),
        in_specs=[
            whole(x.shape), whole(g.shape), spec["gain"], spec["gate"], spec["cand"], spec["tap_gate"],
            spec["tap_cand"], spec["out"], whole(masks.shape), spec["init"],
            pl.BlockSpec((1, seq, 2 * tile), lambda i: (i, 0, 0)), column, column, column, SCALAR,
        ],
        out_specs=[
            *dw_specs, whole(g.shape), pl.BlockSpec((1, 8, 2 * tile), lambda i: (i, 0, 0)), whole((1, width)),
        ],
        out_shape=[
            *dw_shapes, shape(g.shape, BF16), shape((count, 8, 2 * tile), F32),
            shape((1, width), F32),
        ],
        scratch_shapes=[
            pltpu.VMEM((width, seq), BF16), pltpu.VMEM((seq, width), BF16), pltpu.VMEM((width, seq), BF16),
            pltpu.VMEM((width // LANES, seq, LANES), F32), pltpu.VMEM((seq, width), F32), pltpu.VMEM((seq, tile), F32),
            pltpu.VMEM((seq, tile), F32), pltpu.VMEM((seq + HALO, 2 * tile), F32),
            pltpu.VMEM((seq, 2 * tile), BF16), pltpu.VMEM((3, seq + HALO, LANES), F32),
        ],
        cost_estimate=cost(seq, 30),
        name="mixer_backward",
        args=(x, g, gain, weight_in, weight_in, taps, taps, weight_out, masks, init, *stash, bit),
    )


def mlp_forward(layer, x, gain, weight_up, bias_up, weight_down, bias_down, cargo=None):
    seq, width = x.shape
    inner = weight_up.shape[2]
    tile = 2 * TILE_F
    return call(
        functools.partial(mlp_forward_kernel, layer),
        cargo,
        grid=(inner // tile,),
        in_specs=[
            whole(x.shape), whole(gain.shape),
            pl.BlockSpec((None, width, tile), lambda i: (layer, 0, i)),
            pl.BlockSpec((2, tile), lambda i: (0, i)),
            pl.BlockSpec((None, tile, width), lambda i: (layer, i, 0)),
            whole(bias_down.shape),
        ],
        out_specs=[whole(x.shape), pl.BlockSpec((seq, tile), lambda i: (0, i))],
        out_shape=[shape(x.shape, BF16), shape((seq, inner), BF16)],
        scratch_shapes=[pltpu.VMEM((seq, width), BF16), pltpu.VMEM((seq, width), F32)],
        cost_estimate=cost(seq, 10),
        name="mlp_forward",
        args=(x, gain, weight_up, bias_up, weight_down, bias_down),
    )


def mlp_backward(layer, x, g, pre, gain, weight_up, weight_down, bit, split, cargo=None):
    seq, width = g.shape
    inner = weight_up.shape[2]
    tile = TILE_F
    dw_specs, dw_shapes = grad_outputs(width, 2 * tile, 2 * inner, split)
    return call(
        functools.partial(mlp_backward_kernel, layer),
        cargo,
        grid=(inner // tile,),
        in_specs=[
            whole(x.shape), whole(g.shape), whole(gain.shape),
            pl.BlockSpec((None, width, tile), lambda i: (layer, 0, i)),
            pl.BlockSpec((None, tile, width), lambda i: (layer, i, 0)),
            pl.BlockSpec((seq, tile), lambda i: (0, i)), SCALAR,
        ],
        out_specs=[
            *dw_specs, whole(g.shape), pl.BlockSpec((1, tile), lambda i: (0, i)), whole((1, width)), whole((1, width)),
        ],
        out_shape=[
            *dw_shapes, shape(g.shape, BF16), shape((1, inner), F32),
            shape((1, width), F32), shape((1, width), F32),
        ],
        scratch_shapes=[
            pltpu.VMEM((width, seq), BF16), pltpu.VMEM((width, seq), BF16), pltpu.VMEM((seq, width), F32),
            pltpu.VMEM((seq, tile), BF16), pltpu.VMEM((seq, tile), BF16),
        ],
        cost_estimate=cost(seq, 20),
        name="mlp_backward",
        args=(x, g, gain, weight_up, weight_down, pre, bit),
    )


def chunk_masks(resets):
    seq = resets.shape[0]
    cut = (1 - resets).astype(F32).reshape(GROUP, seq // GROUP).T
    ends = jnp.zeros((3, 1), F32)
    before = jnp.concatenate([ends, cut[-3:, :-1]], axis=1)
    ahead = jnp.concatenate([cut[:3, 1:], ends], axis=1)
    rows = jnp.concatenate([before, cut, ahead]).reshape(seq + 2 * HALO, 1)
    return jnp.broadcast_to(rows, (seq + 2 * HALO, LANES))


def windows_into(keep_ref, mask_ref):
    count = mask_ref.shape[1]
    first = keep_ref[pl.ds(HALO, count), :]
    second = first * keep_ref[pl.ds(HALO - GROUP, count), :]
    mask_ref[0] = first
    mask_ref[1] = second
    mask_ref[2] = second * keep_ref[pl.ds(HALO - 2 * GROUP, count), :]


def permute(x, axis, pairs):
    return lax.ppermute(x, axis, pairs)


def last_kernel(jobs, split, dp, inner, n_array, *refs):
    arrays, refs = refs[:n_array], refs[n_array:]
    keeps, sends, refs = refs[0:3], refs[3:6], refs[6:]
    if inner:
        later, refs = refs[0:2], refs[2:]
    cotangent, wu_any, wd_any, gain_ref, bu_ref, bd_ref, refs = *refs[:6], refs[6:]
    if inner:
        near_any, refs = refs[0], refs[1:]
    buffers, refs = refs[2:4], refs[4:]
    acts, dxs = buffers
    outs, refs = (refs[:5], refs[5:]) if inner else (refs[:3], refs[3:])
    wu, wd, x_own, g_own, normed, total, grad, y_own, d_own, dgain, redo_sems, own_sems = refs[-12:]
    refs = refs[:-12]
    kept, got, parts, landed, refs = refs[0:3], refs[3:6], refs[6:9], refs[9:12], refs[12:]
    if inner:
        level, first, second, third, refs = refs[0:5], refs[5:10], refs[10:15], refs[15:20], refs[20:]
        z_sems, refs = refs[0], refs[1:]
    else:
        sums, refs = refs[0:3], refs[3:]
    send_sems, recv_sems, local_sems, core_sems, part_sems = refs
    section = lax.axis_index("section")
    where = lax.axis_index("dp")
    bit = (where // split) % 2
    partner = where + split * (1 - 2 * bit)
    steps = [step for step in bits_of(dp) if step != split][-2:]
    low_bit, high_bit = (where // steps[0]) % 2, (where // steps[1]) % 2
    mine = low_bit + 2 * high_bit
    near_bit, far_bit = section % 2, section // 2

    def flipped(mask):
        low, high = mask % 2, mask // 2
        new_low = low_bit + low * (1 - 2 * low_bit)
        new_high = high_bit + high * (1 - 2 * high_bit)
        device = where + steps[0] * (new_low - low_bit) + steps[1] * (new_high - high_bit)
        return new_low + 2 * new_high, device

    def near_copy(n):
        return pltpu.make_async_remote_copy(
            src_ref=level[n].at[:, 1 - near_bit], dst_ref=first[n], send_sem=z_sems.at[0, n], recv_sem=z_sems.at[1, n],
            device_id={"section": section + 1 - 2 * near_bit}, device_id_type=MESH,
        )

    def far_copy(n):
        return pltpu.make_async_remote_copy(
            src_ref=second[n].at[1 - far_bit], dst_ref=third[n], send_sem=z_sems.at[2, n], recv_sem=z_sems.at[3, n],
            device_id={"section": section + 2 - 4 * far_bit}, device_id_type=MESH,
        )

    def near_sum(n):
        for half in range(2):
            both = level[n][half, near_bit].astype(F32) + first[n][half].astype(F32)
            second[n][half] = both.astype(second[n].dtype)

    barrier = pltpu.get_barrier_semaphore()
    for by in range(1, SECTIONS):
        other = (section + by) % SECTIONS
        pl.semaphore_signal(barrier, inc=1, device_id={"section": other}, device_id_type=MESH)
    pl.semaphore_signal(barrier, inc=1, device_id={"dp": partner}, device_id_type=MESH)
    for mask in (1, 2, 3):
        pl.semaphore_signal(barrier, inc=1, device_id={"dp": flipped(mask)[1]}, device_id_type=MESH)
    loads = [pltpu.make_async_copy(keeps[n], kept[n], local_sems.at[n]) for n in range(3)]
    if inner:
        loads += [pltpu.make_async_copy(later[n], level[3 + n], local_sems.at[3 + n]) for n in range(2)]
    for load in loads:
        load.start()
    pl.semaphore_wait(barrier, SECTIONS + 3)

    start, wait = delivery(jobs, arrays, buffers, send_sems, recv_sems)
    redoes = (section == SECTIONS - 1) | (section == 1)
    full = section == SECTIONS - 1
    block = section // 2
    base = SECTIONS - 2 - 2 * block

    def own_copies(part):
        return (
            pltpu.make_async_copy(arrays[SECTIONS + part], acts.at[part], own_sems.at[0]),
            pltpu.make_async_copy(arrays[SECTIONS - 1 - part], dxs.at[part], own_sems.at[1]),
        )

    for part in range(SECTIONS):

        @pl.when(section == part)
        def _(part=part):
            for one in own_copies(part):
                one.start()

    def fetch(row):
        return (
            pltpu.make_async_copy(acts.at[base + row], x_own, redo_sems.at[0]),
            pltpu.make_async_copy(cotangent.at[base + row], g_own, redo_sems.at[1]),
        )

    def fetch_weights():
        return (
            pltpu.make_async_copy(wu_any.at[block], wu, redo_sems.at[2]),
            pltpu.make_async_copy(wd_any.at[block], wd, redo_sems.at[3]),
        )

    def put(row):
        return pltpu.make_async_copy(y_own, acts.at[base + row], redo_sems.at[4])

    def put_grad_rows(row):
        return pltpu.make_async_copy(d_own, dxs.at[base + row], redo_sems.at[5])

    @pl.when(redoes)
    def _():
        for one in fetch(0) + fetch_weights():
            one.start()

    def redo(row):
        for one in fetch(row) + (fetch_weights() if row == 0 else (put(row - 1),)):
            one.wait()

        if row:

            @pl.when(full)
            def _():
                put_grad_rows(row - 1).wait()

        gain = gain_ref[pl.ds(block, 1), :]
        norm_into(x_own, gain, normed)

        def begin_total(rows):
            total[rows, :] = x_own[rows, :].astype(F32) + bd_ref[pl.ds(block, 1), :]

        rows_loop(total.shape[0], 128, begin_total)
        grad[...] = jnp.zeros_like(grad)

        def tile(index, carry):
            cut = pl.ds(pl.multiple_of(index * TILE_F, TILE_F), TILE_F)
            up, down = wu[:, cut], wd[cut, :]
            pre = dot_nn(normed[...], up) + bu_ref[pl.ds(block, 1), cut]
            active, slope = gelu_parts(pre)
            total[...] += dot_nn(active, down)

            @pl.when(full)
            def _():
                low = (dot_nt(g_own[...], down) * slope).astype(BF16)
                grad[...] += dot_nt(low, up)

            return carry

        lax.fori_loop(0, wu.shape[1] // TILE_F, tile, 0)

        def end_total(rows):
            y_own[rows, :] = total[rows, :].astype(BF16)

        rows_loop(total.shape[0], 128, end_total)
        put(row).start()

        @pl.when(full)
        def _():
            norm_backward(x_own, g_own, gain, grad, d_own, dgain)
            put_grad_rows(row).start()

        if row + 1 < FAR:
            for one in fetch(row + 1):
                one.start()

    swaps = []
    for n in range(3):
        swap = pltpu.make_async_remote_copy(
            src_ref=sends[n], dst_ref=got[n], send_sem=core_sems.at[0, n], recv_sem=core_sems.at[1, n],
            device_id={"dp": partner}, device_id_type=MESH,
        )
        swap.start()
        swaps.append(swap)
    start(0, -1)
    for load in loads:
        load.wait()
    near = {}
    if inner:
        near[3] = pltpu.make_async_copy(near_any, first[3], local_sems.at[5])
        near[4] = near_copy(4)
        near[3].start()
        near[4].start()
    moves = []
    for n in range(3):
        swaps[n].wait()
        rows = kept[n].shape[0] // 4
        for mask in (1, 2, 3):
            quarter, device = flipped(mask)
            taken = pl.ds(pl.multiple_of(quarter * rows, rows), rows)
            pair = kept[n][taken, :].astype(F32) + got[n][taken, :].astype(F32)
            parts[n][mask - 1] = pair.astype(parts[n].dtype)
            move = pltpu.make_async_remote_copy(
                src_ref=parts[n].at[mask - 1], dst_ref=landed[n].at[mask - 1],
                send_sem=part_sems.at[0, n, mask - 1], recv_sem=part_sems.at[1, n, mask - 1],
                device_id={"dp": device}, device_id_type=MESH,
            )
            move.start()
            moves.append(move)
    pl.when(redoes)(functools.partial(redo, 0))
    for n in range(3):
        rows = kept[n].shape[0] // 4
        taken = pl.ds(pl.multiple_of(mine * rows, rows), rows)
        summed = kept[n][taken, :].astype(F32) + got[n][taken, :].astype(F32)
        for mask in (1, 2, 3):
            moves[3 * n + mask - 1].wait()
            summed = summed + landed[n][mask - 1].astype(F32)
        if inner:
            share = rows // SECTIONS
            for part in range(SECTIONS):
                level[n][part // 2, part % 2] = summed[part * share : (part + 1) * share].astype(level[n].dtype)
            near[n] = near_copy(n)
            near[n].start()
        else:
            sums[n][...] = summed.astype(sums[n].dtype)
            store = pltpu.make_async_copy(sums[n], outs[n], local_sems.at[n])
            store.start()
            store.wait()
    if not inner:
        start(len(jobs) - 1)
    pl.when(redoes)(functools.partial(redo, 1))
    if inner:
        far = {}
        for n in (3, 4, 0, 1, 2):
            near[n].wait()
            near_sum(n)
            far[n] = far_copy(n)
            far[n].start()
        start(len(jobs) - 1)
        for n in (3, 4, 0, 1, 2):
            far[n].wait()
            block = n // 3
            final = second[n][far_bit].astype(F32) + third[n][...].astype(F32)
            if n == 2:
                outs[4][...] = final
            elif n in (1, 4):
                cand = outs[0].shape[2] // 2
                for at in range(0, final.shape[1], 3 * TILE_C):
                    to = at // 3
                    outs[0][block, :, pl.ds(to, TILE_C)] = final[:, at : at + TILE_C]
                    outs[0][block, :, pl.ds(cand + to, TILE_C)] = final[:, at + TILE_C : at + 2 * TILE_C]
                    outs[1][block, :, pl.ds(to, TILE_C)] = final[:, at + 2 * TILE_C : at + 3 * TILE_C]
            else:
                for at in range(0, final.shape[1], 2 * TILE_F):
                    outs[2][block, :, pl.ds(at // 2, TILE_F)] = final[:, at : at + TILE_F]
                    outs[3][block, :, pl.ds(at // 2, TILE_F)] = final[:, at + TILE_F : at + 2 * TILE_F]

    @pl.when(redoes)
    def _():
        put(1).wait()

    @pl.when(full)
    def _():
        put_grad_rows(1).wait()

    for one in own_copies(0):
        one.wait()
    wait()


def finish(cargo, keeps, sends, later, redo, dp, width):
    inner = later is not None
    columns = [k.shape[1] for k in keeps]
    kinds = [k.dtype for k in keeps]
    rows = keeps[0].shape[0] // 4
    share = rows // SECTIONS
    n_array = len(cargo.arrays)
    jobs = len(cargo.jobs)
    lots = list(zip(columns + columns[:2], kinds + kinds[:2]))
    if inner:
        later = [a.reshape(2, 2, share, -1) for a in later]
        wide = columns[1] // 3
        outs = [shape((2, share, c), F32) for c in (2 * wide, wide, columns[0] // 2, columns[0] // 2)]
        outs += [shape((share, columns[2]), F32)]
        out_specs = [pl.BlockSpec(memory_space=pltpu.VMEM)] * 5
        extra = [pltpu.VMEM((2, 2, share, c), kind) for c, kind in lots]
        extra += [pltpu.VMEM((2, share, c), kind) for c, kind in lots] * 2
        extra += [pltpu.VMEM((share, c), kind) for c, kind in lots]
        extra += [pltpu.SemaphoreType.DMA((4, 5))]
    else:
        later = []
        outs = [shape((rows, c), kind) for c, kind in zip(columns, kinds)]
        out_specs = [ANYWHERE] * 3
        extra = [pltpu.VMEM((rows, c), kind) for c, kind in zip(columns, kinds)]
    n_in = n_array + 6 + len(later)
    return pl.pallas_call(
        functools.partial(last_kernel, cargo.jobs, first_step(dp, width), dp, inner, n_array),
        in_specs=[ANYWHERE] * (n_in + 3) + [pl.BlockSpec(memory_space=pltpu.VMEM)] * 3 + [ANYWHERE] * (2 + inner),
        out_specs=[ANYWHERE] * 2 + out_specs,
        out_shape=[shape(cargo.dims, BF16)] * 2 + outs,
        scratch_shapes=[pltpu.VMEM(k.shape, k.dtype) for k in keeps] * 2
        + [pltpu.VMEM((3, rows, c), kind) for c, kind in zip(columns, kinds)] * 2
        + extra
        + [
            pltpu.SemaphoreType.DMA((jobs,)), pltpu.SemaphoreType.DMA((jobs, SECTIONS)),
            pltpu.SemaphoreType.DMA((6,)), pltpu.SemaphoreType.DMA((2, 3)), pltpu.SemaphoreType.DMA((2, 3, 3)),
        ]
        + [pltpu.VMEM(redo[1].shape[1:], BF16), pltpu.VMEM(redo[2].shape[1:], BF16)]
        + [pltpu.VMEM(cargo.dims[1:], BF16)] * 3 + [pltpu.VMEM(cargo.dims[1:], F32)] * 2
        + [pltpu.VMEM(cargo.dims[1:], BF16)] * 2
        + [pltpu.VMEM((1, width), F32), pltpu.SemaphoreType.DMA((6,)), pltpu.SemaphoreType.DMA((2,))],
        compiler_params=pltpu.CompilerParams(
            vmem_limit_bytes=56 * 1024 * 1024, collective_id=cargo.collective_id, has_side_effects=True
        ),
        input_output_aliases={n_in + 6 + inner: 0, n_in + 7 + inner: 1},
        cost_estimate=cost(1024, 100),
        name="finish",
    )(*cargo.arrays, *keeps, *sends, *later, *redo, *cargo.old)


def add_up(pieces):
    return functools.reduce(jnp.add, [piece.astype(F32) for piece in pieces])


def exchange(addends, axis, size, steps):
    where = lax.axis_index(axis)
    own = sum(((where // step) % 2) << k for k, step in enumerate(steps))
    blocks = [a.reshape((1 << len(steps), -1) + a.shape[-1:]) for a in addends]

    def part(which):
        taken = [lax.dynamic_index_in_dim(b, which, 0, keepdims=False) for b in blocks]
        return add_up(taken).astype(addends[0].dtype)

    result = [part(own)]
    for mask in range(1, 1 << len(steps)):
        flip = sum(step for k, step in enumerate(steps) if mask >> k & 1)
        result.append(permute(part(own ^ mask), axis, [(i, i ^ flip) for i in range(size)]))
    return result


def bits_of(size):
    return [1 << k for k in range(size.bit_length() - 1)]


def first_step(dp, width):
    return SPLIT // (width // dp)


def sum_rest(addends, dp, width):
    rest = [step for step in bits_of(dp) if step != first_step(dp, width)][:-2]
    while rest:
        top, rest = rest[-2:], rest[:-2]
        addends = exchange(addends, "dp", dp, top)
    return addends


def sum_section(addends, sections):
    return add_up(exchange(addends, "section", sections, bits_of(sections)))


def body(
    tokens, resets, init_states, cotangent, mix_gain, mix_in, conv_weight, conv_bias, mix_out,
    mlp_gain, mlp_up, up_bias, mlp_down, down_bias,
):
    dp = lax.axis_size("dp")
    sections = lax.axis_size("section")
    section = lax.axis_index("section")
    width = tokens.shape[2]
    bit = ((lax.axis_index("dp") // first_step(dp, width)) % 2).astype(jnp.int32).reshape(1)

    def own(values, axis):
        return lax.dynamic_index_in_dim(values, section, axis, keepdims=False)

    x0 = own(tokens, 0)
    g4 = own(cotangent, 0)
    masks = chunk_masks(own(resets, 0))
    init = own(init_states, 1)
    mixer_weights = (mix_gain, mix_in, conv_weight, conv_bias, mix_out)
    mlp_weights = (mlp_gain, mlp_up, up_bias, mlp_down, down_bias)
    seq = tokens.shape[1]
    dims = (sections, seq, width)
    sent = {}

    def some(source, part, share, buffer=0, senders=None):
        if senders is None:
            senders = tuple(k for k in range(sections) if k != part)
        kind = (buffer, part, senders)
        first = sent.get(kind, 0)
        sent[kind] = first + share
        return (source, part, seq * first // 32, seq * share // 32, buffer, senders)

    distant, close = tuple(range(FAR)), tuple(range(FAR, sections - 1))
    across = tuple(range(FAR, sections))

    def relay(share):
        first = sent.get("relay", 0)
        sent["relay"] = first + share
        return ("relay", 0, seq * first // 32, seq * share // 32, 0, across)

    def early(cross, near, up):
        jobs = []
        if cross:
            jobs.append(some(0, 1, cross, 0, across))
        if near:
            jobs.append(some(0, 0, near, 0, (1,)))
        if up:
            jobs.append(some(1, 1, up, 0, (0,)))
        return jobs

    x1, *stash0, final0 = mixer_forward(0, x0, masks, init, *mixer_weights)
    x2, pre0 = mlp_forward(0, x1, *mlp_weights)
    cargo = Cargo(1, [x1, x2], [None], early(9, 16, 8), dims)
    x3, *stash1, final1, acts = mixer_forward(1, x2, masks, init, *mixer_weights, cargo)
    cargo = Cargo(2, [x1, x2, x3], [acts], early(5, 4, 4) + [some(2, 3, 5, 0, distant)], dims)
    x4, pre1, acts = mlp_forward(1, x3, *mlp_weights, cargo)

    back_mixer = (mix_gain, mix_in, conv_weight, mix_out, bit)
    back_mlp = (mlp_gain, mlp_up, mlp_down, bit)
    xs = [x1, x2, x3, x4]
    jobs = early(10, 6, 10)
    jobs += [relay(6), some(2, 3, 10, 0, distant), some(3, 3, 4, 0, close)]
    quarters = jnp.concatenate([final0, final1, jnp.zeros((GROUP - 2, final0.shape[1]), F32)])
    quarters = jnp.split(quarters, sections, axis=1)
    jobs += [some(4 + part, part, 32, 2)[:2] + (0, GROUP, 1) + some(4 + part, part, 32, 3)[5:] for part in range(sections)]
    shapes = [shape(dims, BF16), shape((sections,) + quarters[0].shape, F32)]
    up1, g3, dbu1, dbd1, dgain_mlp1, acts, ends = mlp_backward(
        1, x3, g4, pre1, *back_mlp, False, Cargo(3, xs + quarters, [acts, None], jobs, shapes)
    )
    here = lax.broadcasted_iota(jnp.int32, (sections, 1, 1), 0) == section
    ends = jnp.where(here, lax.dynamic_index_in_dim(jnp.stack(quarters), section, 0), ends)
    final_states = ends[:, :2].transpose(1, 0, 2)
    mlp1 = lax.psum_scatter(up1, "dp", scatter_dimension=0, tiled=True)
    jobs = early(8, 6, 10)
    jobs += [relay(14), some(2, 3, 17, 0, distant), some(3, 3, 4, 0, close)]
    in1, g2, small1, dgain_mix1, acts = mixer_backward(
        1, x2, g3, stash1, masks, init, *back_mixer, False, Cargo(4, xs, [acts], jobs, dims)
    )
    mix1 = lax.psum_scatter(in1, "dp", scatter_dimension=0, tiled=True)
    jobs = [relay(10), some(2, 2, 10), some(3, 3, 12, 0, close)]
    up0_keep, up0_send, g1, dbu0, dbd0, dgain_mlp0, acts = mlp_backward(
        0, x1, g2, pre0, *back_mlp, True, Cargo(5, xs, [acts], jobs, dims)
    )
    jobs = [relay(2), some(2, 2, 15), some(3, 3, 12, 0, close)]
    jobs += [some(4, 3, 10, 1, close), some(6, 1, 17, 1)]
    inner = dp == 8 and first_step(dp, width) == 1
    share = width // (dp * sections)
    g1, mlp1 = after(g1, mlp1)
    sources, buffers, shapes = xs + [g3, g2, g1], [acts, None], [shape(dims, BF16)] * 2
    if inner:
        halved = (2, share, mlp1.shape[1])
        sources.append(mlp1.reshape((2,) + halved))
        buffers.append(None)
        shapes.append(shape(halved, BF16))
        jobs.append((None, 7, 2))
    in0_keep, in0_send, g0, small0, dgain_mix0, acts, dxs, *near1 = mixer_backward(
        0, x0, g1, stash0, masks, init, *back_mixer, True, Cargo(6, sources, buffers, jobs, shapes)
    )
    jobs = [some(3, 0, 32, 1, (2, 3)), some(3, 0, 16, 1, (1,)), some(2, 1, 15, 1), some(0, 3, 22, 1, close), some(1, 2, 32, 1), some(6, 2, 7)]
    jobs += [some(3, 0, 16, 1, (1,))]
    cargo = Cargo(7, [g3, g2, g1, g0] + xs, [acts, dxs], jobs, dims)
    redo = (cotangent, mlp_up, mlp_down, mlp_gain, up_bias, down_bias)
    devices = dp * sections
    mix_small = jnp.stack([small0, small1])
    count, tile = mix_small.shape[1], mix_small.shape[3] // 2
    mix_small = mix_small.reshape(2, count, 8, 2, tile).transpose(0, 2, 3, 1, 4).reshape(2, 8, -1)
    lines = [
        jnp.stack([dgain_mix0[0], dgain_mix1[0]]),
        jnp.stack([dgain_mlp0[0], dgain_mlp1[0]]),
        jnp.stack([dbd0[0], dbd1[0]]),
        jnp.stack([dbu0[0], dbu1[0]]),
        mix_small[:, :5].reshape(10, -1),
    ]
    packed = jnp.concatenate(
        [a.reshape(a.shape[0], devices, -1).transpose(1, 0, 2).reshape(devices, -1) for a in lines], axis=1
    )
    share = width // devices
    length = packed.shape[1]
    packed = jnp.pad(packed, ((0, 0), (0, share * LANES - length))).reshape(-1, 2, SPLIT, LANES)

    def half(which):
        return lax.dynamic_index_in_dim(packed, which, 1, keepdims=False).reshape(-1, LANES)

    halves = ((up0_keep, in0_keep, half(bit[0])), (up0_send, in0_send, half(1 - bit[0])))
    if inner:
        acts, dxs, mix_in_grad, mix_out_grad, mlp_up_grad, mlp_down_grad, summed = finish(
            cargo, *halves, (mlp1, mix1), redo + tuple(near1), dp, width
        )
    else:
        acts, dxs, mlp0, mix0, summed = finish(cargo, *halves, None, redo, dp, width)
        parts = [sum_rest([part], dp, width) for part in (mlp0, mix0, summed)] + [[mlp1], [mix1]]
        mlp0, mix0, summed, mlp1, mix1 = [
            sum_section([add_up(part).astype(part[0].dtype)], sections) for part in parts
        ]
        mix_big = jnp.stack([mix0, mix1]).reshape(2, share, -1, 3, TILE_C)
        mix_in_grad = mix_big[:, :, :, :2].transpose(0, 1, 3, 2, 4).reshape(2, share, -1)
        mix_out_grad = mix_big[:, :, :, 2].reshape(2, share, -1)
        mlp_big = jnp.stack([mlp0, mlp1]).reshape(2, share, -1, 2, TILE_F)
        mlp_up_grad = mlp_big[:, :, :, 0].reshape(2, share, -1)
        mlp_down_grad = mlp_big[:, :, :, 1].reshape(2, share, -1)
    mix_out_grad = mix_out_grad.transpose(0, 2, 1)
    mlp_down_grad = mlp_down_grad.transpose(0, 2, 1)

    activations, input_grads = acts[None], dxs[None]

    summed = summed.reshape(-1)[:length]
    pieces, at = [], 0
    for a in lines:
        size = a.size // devices
        pieces.append(summed[at : at + size].reshape(a.shape[0], -1))
        at += size
    mix_gain_grad, mlp_gain_grad, down_bias_grad, up_bias_grad, conv = pieces
    conv = conv.reshape(2, 5, -1)

    return (
        activations, input_grads, final_states, mix_gain_grad, mix_in_grad, conv[:, :4], conv[:, 4],
        mix_out_grad, mlp_gain_grad, mlp_up_grad, up_bias_grad, mlp_down_grad, down_bias_grad,
    )


def solution(mesh):
    both = ("dp", "section")
    return jax.shard_map(
        body,
        mesh=mesh,
        in_specs=(
            P("dp", None, None), P("dp", None), P(None, "dp", None), P("dp", None, None),
            P(), P(), P(), P(), P(), P(), P(), P(), P(), P(),
        ),
        out_specs=(
            P("section", "dp", None, None), P("section", "dp", None, None), P(None, "dp", "section"),
            P(None, both), P(None, both, None), P(None, None, both), P(None, both), P(None, None, both),
            P(None, both), P(None, both, None), P(None, both), P(None, None, both), P(None, both),
        ),
        check_vma=False,
    )
```

```python
import functools

import jax
import jax.numpy as jnp
from jax import lax
from jax.experimental import pallas as pl
from jax.experimental.pallas import tpu as pltpu
from jax.sharding import PartitionSpec as P

EPSILON = 1e-06
LANES = 128
GROUP = 8
TILE_C = 512
TILE_F = 512
BIG = 1024
F32 = jnp.float32
BF16 = jnp.bfloat16
ROOT_2_PI = 0.7978845608028654
CUBIC = 0.044715


def dot_nn(left, right):
    return jnp.dot(left, right, preferred_element_type=F32)


def dot_nt(left, right):
    return lax.dot_general(left, right, (((1,), (1,)), ((), ())), preferred_element_type=F32)


def rows_loop(total, step, fn):
    def at(index, carry):
        fn(pl.ds(pl.multiple_of(index * step, step), step))
        return carry

    lax.fori_loop(0, total // step, at, 0)


def to_chunks(natural, target):
    stride = natural.shape[1] // GROUP

    def at(index, carry):
        for tile in range(natural.shape[0]):
            block = jnp.stack(
                [
                    natural[tile, pl.ds(pl.multiple_of(s * stride + index * GROUP, GROUP), GROUP), :]
                    for s in range(GROUP)
                ]
            )
            rows = pl.ds(pl.multiple_of(index * GROUP * GROUP, GROUP * GROUP), GROUP * GROUP)
            mixed = jnp.swapaxes(block, 0, 1).reshape(GROUP * GROUP, LANES)
            target[rows, pl.ds(tile * LANES, LANES)] = mixed.astype(BF16)
        return carry

    lax.fori_loop(0, stride // GROUP, at, 0, unroll=16)


def to_tokens(chunked, natural):
    stride = natural.shape[1] // GROUP

    def at(index, carry):
        for tile in range(natural.shape[0]):
            rows = pl.ds(pl.multiple_of(index * GROUP * GROUP, GROUP * GROUP), GROUP * GROUP)
            block = chunked[rows, pl.ds(tile * LANES, LANES)].reshape(GROUP, GROUP, LANES)
            mixed = jnp.swapaxes(block, 0, 1)
            for s in range(GROUP):
                to = pl.ds(pl.multiple_of(s * stride + index * GROUP, GROUP), GROUP)
                natural[tile, to, :] = mixed[s]
        return carry

    lax.fori_loop(0, stride // GROUP, at, 0, unroll=16)


def transpose_into(source, target):
    def at(index, carry):
        rows = pl.ds(pl.multiple_of(index * LANES, LANES), LANES)
        target[:, rows] = source[rows, :].astype(F32).T.astype(BF16)
        return carry

    lax.fori_loop(0, source.shape[0] // LANES, at, 0, unroll=8)


def inverse_rms(values):
    return lax.rsqrt(jnp.mean(values * values, axis=-1, keepdims=True) + EPSILON)


def put_tiles(natural, rows, values):
    for tile in range(natural.shape[0]):
        natural[tile, rows, :] = values[:, tile * LANES : (tile + 1) * LANES]


def get_tiles(natural, rows):
    return jnp.concatenate([natural[tile, rows, :] for tile in range(natural.shape[0])], axis=1)


def norm_into(x_ref, gain, target):
    def at(rows):
        source = x_ref[rows, :].astype(F32)
        result = source * inverse_rms(source) * gain
        if len(target.shape) == 3:
            put_tiles(target, rows, result)
        else:
            target[rows, :] = result.astype(target.dtype)

    rows_loop(x_ref.shape[0], 1024, at)


def previous_chunk(values, first_row):
    rolled = pltpu.roll(values, 1, 0)
    position = lax.broadcasted_iota(jnp.int32, values.shape, 0)
    return jnp.where(position == 0, first_row, rolled)


def following_chunk(values):
    rolled = pltpu.roll(values, GROUP - 1, 0)
    position = lax.broadcasted_iota(jnp.int32, values.shape, 0)
    return jnp.where(position == GROUP - 1, 0.0, rolled)


def sigmoid(values):
    return 0.5 * jnp.tanh(0.5 * values) + 0.5


def repeat_rows(values, rows):
    return jnp.concatenate([values] * (rows // values.shape[0]), axis=0)


STEP = 64
SPLIT = 64
HALO = 24


def mixer_forward_kernel(
    layer, begin, x_ref, gain_ref, wg_ref, wc_ref, kg_ref, kc_ref, bg_ref, bc_ref, wo_ref, keep_ref, init_ref,
    y_ref, p_ref, z_ref, cand_ref, h_ref, final_ref,
    normed, natural, total, proj, local, decay, mask_ref,
):
    step = pl.program_id(0)
    seq = x_ref.shape[0]
    width = wg_ref.shape[1]

    @pl.when(step == 0)
    def _():
        windows_into(keep_ref, mask_ref)
        begin()
        norm_into(x_ref, gain_ref[layer : layer + 1, :], natural)
        to_chunks(natural, normed)
        total[...] = jnp.zeros_like(total)

    def project(index, carry):
        rows = pl.ds(pl.multiple_of(index * BIG, BIG), BIG)
        out_rows = pl.ds(pl.multiple_of(index * BIG + HALO, GROUP), BIG)
        block = normed[rows, :]
        for side, weight in enumerate((wg_ref, wc_ref)):
            lanes = pl.ds(side * width, width)
            piece = dot_nn(block, weight[...])
            proj[out_rows, lanes] = piece
            p_ref[0, rows, lanes] = piece.astype(BF16)
        return carry

    lax.fori_loop(0, seq // BIG, project, 0)
    for offset in range(3):
        last = proj[pl.ds(seq + GROUP * offset, GROUP), :]
        proj[pl.ds(GROUP * offset, GROUP), :] = previous_chunk(last, 0.0)

    def scan_step(index, carry):
        base = pl.multiple_of(index * STEP, STEP)
        rows = pl.ds(base, STEP)
        masks = [None] + [mask_ref[k, rows, :] for k in range(3)]
        updated = []
        for tile in range(width // LANES):
            lanes = pl.ds(tile * LANES, LANES)

            def convolve(shift, taps, bias):
                value = bias[layer : layer + 1, lanes]
                for k in range(4):
                    at = pl.ds(pl.multiple_of(base + HALO - GROUP * k, GROUP), STEP)
                    term = proj[at, pl.ds(shift + tile * LANES, LANES)]
                    if k:
                        term = term * masks[k]
                    value = value + taps[k : k + 1, lanes] * term
                return value

            update = sigmoid(convolve(0, kg_ref, bg_ref))
            candidate = convolve(width, kc_ref, bc_ref)
            z_ref[rows, lanes] = update.astype(BF16)
            cand_ref[rows, lanes] = candidate.astype(BF16)
            retain = (1.0 - update) * masks[1]
            inject = update * candidate
            state, product = carry[tile]
            states, products = [], []
            for g in range(STEP // GROUP):
                here = slice(g * GROUP, (g + 1) * GROUP)
                state = retain[here] * state + inject[here]
                product = retain[here] * product
                states.append(state)
                products.append(product)
            local[rows, lanes] = jnp.concatenate(states, axis=0)
            decay[rows, lanes] = jnp.concatenate(products, axis=0)
            updated.append((state, product))
        return tuple(updated)

    zero = jnp.zeros((GROUP, LANES), F32)
    one = jnp.ones((GROUP, LANES), F32)
    ends = lax.fori_loop(0, seq // STEP, scan_step, ((zero, one),) * (width // LANES))
    entries = []
    for tile, (state, product) in enumerate(ends):
        lanes = pl.ds(tile * LANES, LANES)
        current = init_ref[layer : layer + 1, lanes]
        starts = []
        for g in range(GROUP):
            starts.append(current)
            current = product[g : g + 1] * current + state[g : g + 1]
        final_ref[0:1, lanes] = current
        entries.append(jnp.concatenate(starts, axis=0))
    entry = repeat_rows(jnp.concatenate(entries, axis=1), STEP)

    def fix(index, carry):
        rows = pl.ds(pl.multiple_of(index * STEP, STEP), STEP)
        h_ref[rows, :] = (local[rows, :] + decay[rows, :] * entry).astype(BF16)
        return carry

    lax.fori_loop(0, seq // STEP, fix, 0)

    def output(rows):
        total[rows, :] += dot_nn(h_ref[rows, :], wo_ref[...])

    rows_loop(seq, BIG, output)

    @pl.when(step == pl.num_programs(0) - 1)
    def _():
        to_tokens(total, natural)

        def finish(rows):
            y_ref[rows, :] = (x_ref[rows, :].astype(F32) + get_tiles(natural, rows)).astype(BF16)

        rows_loop(seq, 1024, finish)


def norm_backward(x_ref, g_ref, gain, grad_normed, dx_ref, dgain_ref):

    def at(index, carry):
        rows = pl.ds(pl.multiple_of(index * 1024, 1024), 1024)
        source = x_ref[rows, :].astype(F32)
        upstream = g_ref[rows, :].astype(F32)
        incoming = get_tiles(grad_normed, rows) if len(grad_normed.shape) == 3 else grad_normed[rows, :]
        scale = inverse_rms(source)
        scaled = gain * incoming
        mean = jnp.mean(source * scaled, axis=-1, keepdims=True)
        result = upstream + scale * scaled - source * (scale * scale * scale * mean)
        dx_ref[rows, :] = result.astype(BF16)
        return carry + jnp.sum(incoming * source * scale, axis=0, keepdims=True)

    dgain_ref[...] = lax.fori_loop(0, x_ref.shape[0] // 1024, at, jnp.zeros(gain.shape, F32))


def put_grad(refs, bit_ref, lanes, values):
    if len(refs) == 1:
        refs[0][:, lanes] = values.astype(BF16)
        return
    mine = bit_ref[0] == 1
    for pair in range(values.shape[0] // (2 * SPLIT)):
        low = values[2 * pair * SPLIT : (2 * pair + 1) * SPLIT].astype(BF16)
        high = values[(2 * pair + 1) * SPLIT : (2 * pair + 2) * SPLIT].astype(BF16)
        rows = pl.ds(pair * SPLIT, SPLIT)
        refs[0][rows, lanes] = jnp.where(mine, high, low)
        refs[1][rows, lanes] = jnp.where(mine, low, high)


def mixer_backward_kernel(
    layer, begin, x_ref, g_ref, gain_ref, wg_ref, wc_ref, kg_ref, kc_ref, wo_ref, keep_ref, init_ref,
    p_ref, z_ref, cand_ref, h_ref, bit_ref, *rest,
):
    *dw, dx_ref, small_ref, dgain_ref = rest[:-10]
    (normed_t, upstream, upstream_t, natural, total, local, decay, dconv, dproj, mask_ref) = rest[-10:]
    step = pl.program_id(0)
    seq = x_ref.shape[0]
    width = wg_ref.shape[1]
    tiles = width // LANES

    @pl.when(step == 0)
    def _():
        windows_into(keep_ref, mask_ref)
        begin()
        norm_into(x_ref, gain_ref[layer : layer + 1, :], natural)
        to_chunks(natural, upstream)
        transpose_into(upstream, normed_t)

        def widen(rows):
            put_tiles(natural, rows, g_ref[rows, :].astype(F32))

        rows_loop(seq, 1024, widen)
        to_chunks(natural, upstream)
        transpose_into(upstream, upstream_t)
        total[...] = jnp.zeros_like(total)

    def back_hidden(rows):
        local[rows, :] = dot_nt(upstream[rows, :], wo_ref[...])

    rows_loop(seq, BIG, back_hidden)

    def scan_step(index, carry):
        rows = pl.ds(pl.multiple_of(seq - STEP - index * STEP, STEP), STEP)
        keep = mask_ref[0, rows, :]
        updated = []
        for tile in range(tiles):
            lanes = pl.ds(tile * LANES, LANES)
            retain = (1.0 - z_ref[rows, lanes].astype(F32)) * keep
            grads = local[rows, lanes]
            chain, product = carry[tile]
            chains, products = [], []
            for g in reversed(range(STEP // GROUP)):
                here = slice(g * GROUP, (g + 1) * GROUP)
                value = grads[here] + chain
                chains.append(value)
                products.append(product)
                chain = retain[here] * value
                product = retain[here] * product
            local[rows, lanes] = jnp.concatenate(chains[::-1], axis=0)
            decay[rows, lanes] = jnp.concatenate(products[::-1], axis=0)
            updated.append((chain, product))
        return tuple(updated)

    zero = jnp.zeros((GROUP, LANES), F32)
    one = jnp.ones((GROUP, LANES), F32)
    ends = lax.fori_loop(0, seq // STEP, scan_step, ((zero, one),) * tiles)
    entries = []
    for chain, product in ends:
        current = jnp.zeros((1, LANES), F32)
        starts = [current]
        for g in reversed(range(1, GROUP)):
            current = chain[g : g + 1] + product[g : g + 1] * current
            starts.append(current)
        entries.append(jnp.concatenate(starts[::-1], axis=0))

    last_rows = h_ref[pl.ds(seq - 16, 16), :].astype(F32)[GROUP:]
    before = previous_chunk(last_rows, init_ref[layer : layer + 1, :])

    def gates(index, carry):
        base = pl.multiple_of(index * STEP, STEP)
        rows = pl.ds(base, STEP)
        keep = mask_ref[0, rows, :]
        updated = []
        for tile in range(tiles):
            lanes = pl.ds(tile * LANES, LANES)
            hidden = h_ref[rows, lanes].astype(F32)
            delayed = jnp.concatenate([carry[tile], hidden[: STEP - GROUP]], axis=0)
            error = local[rows, lanes] + decay[rows, lanes] * repeat_rows(entries[tile], STEP)
            update = z_ref[rows, lanes].astype(F32)
            candidate = cand_ref[rows, lanes].astype(F32)
            slope = error * (candidate - keep * delayed)
            dconv[rows, lanes] = slope * (update * (1.0 - update))
            dconv[rows, pl.ds(width + tile * LANES, LANES)] = update * error
            updated.append(hidden[STEP - GROUP :])
        return tuple(updated)

    starting = tuple(before[:, tile * LANES : (tile + 1) * LANES] for tile in range(tiles))
    lax.fori_loop(0, seq // STEP, gates, starting)
    for offset in range(3):
        first = dconv[pl.ds(GROUP * offset, GROUP), :]
        dconv[pl.ds(seq + GROUP * offset, GROUP), :] = following_chunk(first)

    def fold(values):
        result = values[0:GROUP]
        for g in range(1, STEP // GROUP):
            result = result + values[g * GROUP : (g + 1) * GROUP]
        return result

    for side, taps in enumerate((kg_ref, kc_ref)):

        def spread(index, carry):
            base = pl.multiple_of(index * STEP, STEP)
            rows = pl.ds(base, STEP)
            updated = []
            for tile in range(tiles):
                lanes = pl.ds(side * width + tile * LANES, LANES)
                weights = pl.ds(tile * LANES, LANES)
                projected = p_ref[0, rows, lanes].astype(F32)
                sums = carry[tile]
                fresh = []
                value = None
                for k in range(4):
                    at = pl.ds(pl.multiple_of(base + GROUP * k, GROUP), STEP)
                    moved = dconv[at, lanes]
                    if k == 0:
                        bias_sum = sums[4] + fold(moved)
                    else:
                        moved = moved * mask_ref[k - 1, at, :]
                    fresh.append(sums[k] + fold(moved * projected))
                    term = taps[k : k + 1, weights] * moved
                    value = term if value is None else value + term
                fresh.append(bias_sum)
                dproj[rows, lanes] = value.astype(BF16)
                updated.append(tuple(fresh))
            return tuple(updated)

        sums = lax.fori_loop(0, seq // STEP, spread, ((zero,) * 5,) * tiles)
        for tile in range(tiles):
            lanes = pl.ds(side * width + tile * LANES, LANES)
            for k in range(5):
                small_ref[0, k : k + 1, lanes] = jnp.sum(sums[tile][k], axis=0, keepdims=True)
            small_ref[0, 5:8, lanes] = jnp.zeros((3, LANES), F32)

    put_grad(dw, bit_ref, pl.ds(0, 2 * width), dot_nn(normed_t[...], dproj[...]))
    put_grad(dw, bit_ref, pl.ds(2 * width, width), dot_nn(upstream_t[...], h_ref[...]))

    def back_normed(rows):
        total[rows, :] += dot_nt(dproj[rows, pl.ds(0, width)], wg_ref[...]) + dot_nt(
            dproj[rows, pl.ds(width, width)], wc_ref[...]
        )

    rows_loop(seq, BIG, back_normed)

    @pl.when(step == pl.num_programs(0) - 1)
    def _():
        to_tokens(total, natural)
        norm_backward(x_ref, g_ref, gain_ref[layer : layer + 1, :], natural, dx_ref, dgain_ref)


def mlp_forward_kernel(
    layer, begin, x_ref, gain_ref, wu_ref, bu_ref, wd_ref, bd_ref, y_ref, u_ref, normed, total
):
    step = pl.program_id(0)
    seq = x_ref.shape[0]

    @pl.when(step == 0)
    def _():
        begin()
        norm_into(x_ref, gain_ref[layer : layer + 1, :], normed)

        def start(rows):
            total[rows, :] = x_ref[rows, :].astype(F32) + bd_ref[layer : layer + 1, :]

        rows_loop(seq, 1024, start)

    def at(rows):
        pre = dot_nn(normed[rows, :], wu_ref[...]) + bu_ref[layer : layer + 1, :]
        u_ref[rows, :] = pre.astype(BF16)
        inner = ROOT_2_PI * (pre + CUBIC * (pre * pre * pre))
        active = (0.5 * pre * (1.0 + jnp.tanh(inner))).astype(BF16)
        total[rows, :] += dot_nn(active, wd_ref[...])

    rows_loop(seq, BIG, at)

    @pl.when(step == pl.num_programs(0) - 1)
    def _():
        def finish(rows):
            y_ref[rows, :] = total[rows, :].astype(BF16)

        rows_loop(seq, 1024, finish)


def gelu_parts(pre):
    square = pre * pre
    bent = jnp.tanh(pre * (ROOT_2_PI + (ROOT_2_PI * CUBIC) * square))
    half = 0.5 * pre
    slope = 0.5 + 0.5 * bent + half * (1.0 - bent * bent) * (
        ROOT_2_PI + (3.0 * ROOT_2_PI * CUBIC) * square
    )
    return (half + half * bent).astype(BF16), slope


def mlp_backward_kernel(
    layer, begin, x_ref, g_ref, gain_ref, wu_ref, wd_ref, u_ref, bit_ref, *rest,
):
    *dw, dx_ref, dbu_ref, dbd_ref, dgain_ref = rest[:-5]
    normed_t, upstream_t, total, active, dpre = rest[-5:]
    step = pl.program_id(0)
    seq = x_ref.shape[0]
    width = wu_ref.shape[1]

    @pl.when(step == 0)
    def _():
        begin()
        norm_into(x_ref, gain_ref[layer : layer + 1, :], active)
        transpose_into(active, normed_t)
        transpose_into(g_ref, upstream_t)

        def at(index, carry):
            rows = pl.ds(pl.multiple_of(index * 1024, 1024), 1024)
            return carry + jnp.sum(g_ref[rows, :].astype(F32), axis=0, keepdims=True)

        dbd_ref[...] = lax.fori_loop(0, seq // 1024, at, jnp.zeros(dbd_ref.shape, F32))
        total[...] = jnp.zeros_like(total)

    def at(index, carry):
        rows = pl.ds(pl.multiple_of(index * BIG, BIG), BIG)
        pre = u_ref[rows, :].astype(F32)
        active[rows, :], slope = gelu_parts(pre)
        low = (dot_nt(g_ref[rows, :], wd_ref[...]) * slope).astype(BF16)
        dpre[rows, :] = low
        total[rows, :] += dot_nt(low, wu_ref[...])
        return carry + jnp.sum(low.astype(F32), axis=0, keepdims=True)

    dbu_ref[...] = lax.fori_loop(0, seq // BIG, at, jnp.zeros(dbu_ref.shape, F32))

    put_grad(dw, bit_ref, pl.ds(0, width), dot_nn(normed_t[...], dpre[...]))
    put_grad(dw, bit_ref, pl.ds(width, width), dot_nn(upstream_t[...], active[...]))

    @pl.when(step == pl.num_programs(0) - 1)
    def _():
        norm_backward(x_ref, g_ref, gain_ref[layer : layer + 1, :], total, dx_ref, dgain_ref)


def shape(dims, kind):
    return jax.ShapeDtypeStruct(dims, kind)


PARAMS = pltpu.CompilerParams(
    dimension_semantics=("arbitrary",), vmem_limit_bytes=56 * 1024 * 1024
)


SCALAR = pl.BlockSpec(memory_space=pltpu.SMEM)
ANYWHERE = pl.BlockSpec(memory_space=pl.ANY)
MESH = pl.DeviceIdType.MESH
SECTIONS = 4
FAR = 2


def greet_sections(section):
    barrier = pltpu.get_barrier_semaphore()
    for by in range(1, SECTIONS):
        other = (section + by) % SECTIONS
        pl.semaphore_signal(barrier, inc=1, device_id={"section": other}, device_id_type=MESH)


def delivery(jobs, sources, buffers, send_sems, recv_sems, relay_sems=None):
    section = lax.axis_index("section")
    near_bit = section % 2

    def near(number):
        _, source, buffer = jobs[number]
        return pltpu.make_async_remote_copy(
            src_ref=sources[source].at[:, 1 - near_bit],
            dst_ref=buffers[buffer],
            send_sem=send_sems.at[number],
            recv_sem=recv_sems.at[number, 0],
            device_id={"section": section + 1 - 2 * near_bit},
            device_id_type=MESH,
        )

    def relay(number, row):
        _, part, first, count, buffer, _ = jobs[number]
        rows = pl.ds(first, count)
        return pltpu.make_async_remote_copy(
            src_ref=buffers[buffer].at[row, rows],
            dst_ref=buffers[buffer].at[row, rows],
            send_sem=relay_sems.at[0, number, row],
            recv_sem=recv_sems.at[number, row],
            device_id={"section": part},
            device_id_type=MESH,
        )

    def sends(job):
        return functools.reduce(jnp.logical_or, [section == sender for sender in job[5]])

    def copy(number, sender):
        source, part, first, count, buffer, _ = jobs[number]
        rows = pl.ds(first, count)
        return pltpu.make_async_remote_copy(
            src_ref=sources[source].at[rows],
            dst_ref=buffers[buffer].at[sender, rows],
            send_sem=send_sems.at[number],
            recv_sem=recv_sems.at[number, sender],
            device_id={"section": part},
            device_id_type=MESH,
        )

    def start(first=0, last=len(jobs)):
        for number, job in list(enumerate(jobs))[first:last]:
            if job[0] is None:
                near(number).start()
                continue
            if job[0] == "relay":

                @pl.when(section == job[1] + 1)
                def _(number=number, job=job):
                    for row in job[5]:
                        relay(number, row).start()

                continue

            @pl.when(sends(job))
            def _(number=number):
                copy(number, section).start()

    def wait():
        for number, job in enumerate(jobs):
            if job[0] is None:
                near(number).wait()
                continue
            if job[0] == "relay":

                @pl.when(section == job[1] + 1)
                def _(number=number, job=job):
                    for row in job[5]:
                        relay(number, row).wait_send()

                @pl.when(section == job[1])
                def _(number=number, job=job):
                    for row in job[5]:
                        relay(number, row).wait_recv()

                continue

            @pl.when(sends(job))
            def _(number=number):
                copy(number, section).wait_send()

            @pl.when(section == job[1])
            def _(number=number, job=job):
                for sender in job[5]:
                    copy(number, sender).wait_recv()

    return start, wait


def after(value, *others):
    return lax.optimization_barrier((value,) + others)


class Cargo:
    def __init__(self, collective_id, arrays, buffers, jobs, dims):
        self.collective_id = collective_id
        self.arrays = list(arrays)
        self.old = [b for b in buffers if b is not None]
        self.buffers = buffers
        self.jobs = jobs
        self.dims = dims


def call(kernel, cargo, *, grid, in_specs, out_specs, out_shape, scratch_shapes, cost_estimate, name, args, aliases=None):
    aliases = dict(aliases or {})
    if cargo is None:
        return pl.pallas_call(
            functools.partial(kernel, lambda: None), grid=grid, in_specs=in_specs, out_specs=out_specs, out_shape=out_shape,
            scratch_shapes=scratch_shapes, compiler_params=PARAMS, cost_estimate=cost_estimate, name=name,
            input_output_aliases=aliases,
        )(*args)
    n_in, n_out = len(in_specs), len(out_specs)
    n_array, n_old, n_buffer = len(cargo.arrays), len(cargo.old), len(cargo.buffers)

    def carrying(*refs):
        ins, refs = refs[:n_in], refs[n_in:]
        arrays, refs = refs[:n_array], refs[n_array + n_old :]
        outs, refs = refs[:n_out], refs[n_out:]
        buffers, refs = refs[:n_buffer], refs[n_buffer:]
        own, (send_sems, recv_sems, relay_sems) = refs[:-3], refs[-3:]
        start, wait = delivery(cargo.jobs, arrays, buffers, send_sems, recv_sems, relay_sems)
        step = pl.program_id(0)

        @pl.when(step == 0)
        def _():
            greet_sections(lax.axis_index("section"))

        def begin():
            pl.semaphore_wait(pltpu.get_barrier_semaphore(), SECTIONS - 1)
            start()

        kernel(begin, *ins, *outs, *own)

        @pl.when(step == pl.num_programs(0) - 1)
        def _():
            wait()

    old = 0
    for number, buffer in enumerate(cargo.buffers):
        if buffer is not None:
            aliases[n_in + n_array + old] = n_out + number
            old += 1
    jobs = len(cargo.jobs)
    return pl.pallas_call(
        carrying,
        grid=grid,
        in_specs=list(in_specs) + [ANYWHERE] * (n_array + n_old),
        out_specs=list(out_specs) + [ANYWHERE] * n_buffer,
        out_shape=list(out_shape) + (cargo.dims if isinstance(cargo.dims, list) else [shape(cargo.dims, BF16)] * n_buffer),
        scratch_shapes=list(scratch_shapes)
        + [pltpu.SemaphoreType.DMA((jobs,)), pltpu.SemaphoreType.DMA((jobs, SECTIONS))]
        + [pltpu.SemaphoreType.DMA((1, jobs, SECTIONS))],
        compiler_params=pltpu.CompilerParams(
            dimension_semantics=("arbitrary",), vmem_limit_bytes=56 * 1024 * 1024,
            collective_id=cargo.collective_id, has_side_effects=True,
        ),
        cost_estimate=cost_estimate,
        name=name,
        input_output_aliases=aliases,
    )(*args, *cargo.arrays, *cargo.old)


def cost(seq, microseconds):
    return pl.CostEstimate(
        flops=int(microseconds * 1.1e9), bytes_accessed=seq * 4096, transcendentals=0
    )


def whole(dims):
    return pl.BlockSpec(dims, lambda i: (0,) * len(dims))


def mixer_specs(layer, width, hidden, tile):
    count = hidden // tile
    return dict(
        gate=pl.BlockSpec((None, width, tile), lambda i: (layer, 0, i)),
        cand=pl.BlockSpec((None, width, tile), lambda i: (layer, 0, count + i)),
        tap_gate=pl.BlockSpec((None, 4, tile), lambda i: (layer, 0, i)),
        tap_cand=pl.BlockSpec((None, 4, tile), lambda i: (layer, 0, count + i)),
        bias_gate=pl.BlockSpec((2, tile), lambda i: (0, i)),
        bias_cand=pl.BlockSpec((2, tile), lambda i: (0, count + i)),
        out=pl.BlockSpec((None, tile, width), lambda i: (layer, i, 0)),
        gain=whole((2, width)),
        init=pl.BlockSpec((2, tile), lambda i: (0, i)),
    )


def mixer_forward(layer, x, masks, init, gain, weight_in, taps, bias, weight_out, cargo=None):
    seq, width = x.shape
    hidden = init.shape[1]
    tile = TILE_C
    count = hidden // tile
    spec = mixer_specs(layer, width, hidden, tile)
    column = pl.BlockSpec((seq, tile), lambda i: (0, i))
    return call(
        functools.partial(mixer_forward_kernel, layer),
        cargo,
        grid=(count,),
        in_specs=[
            whole(x.shape), spec["gain"], spec["gate"], spec["cand"], spec["tap_gate"], spec["tap_cand"],
            spec["bias_gate"], spec["bias_cand"], spec["out"], whole(masks.shape), spec["init"],
        ],
        out_specs=[
            whole(x.shape), pl.BlockSpec((1, seq, 2 * tile), lambda i: (i, 0, 0)), column, column, column,
            pl.BlockSpec((1, tile), lambda i: (0, i)),
        ],
        out_shape=[
            shape(x.shape, BF16), shape((count, seq, 2 * tile), BF16), shape((seq, hidden), BF16),
            shape((seq, hidden), BF16), shape((seq, hidden), BF16), shape((1, hidden), F32),
        ],
        scratch_shapes=[
            pltpu.VMEM((seq, width), BF16), pltpu.VMEM((width // LANES, seq, LANES), F32), pltpu.VMEM((seq, width), F32),
            pltpu.VMEM((seq + HALO, 2 * tile), F32), pltpu.VMEM((seq, tile), F32), pltpu.VMEM((seq, tile), F32),
            pltpu.VMEM((3, seq + HALO, LANES), F32),
        ],
        cost_estimate=cost(seq, 15),
        name="mixer_forward",
        args=(x, gain, weight_in, weight_in, taps, taps, bias, bias, weight_out, masks, init),
    )


def grad_outputs(width, tile, total, split):
    rows = width // 2 if split else width
    parts = 2 if split else 1
    return (
        [pl.BlockSpec((rows, tile), lambda i: (0, i))] * parts,
        [shape((rows, total), BF16)] * parts,
    )


def mixer_backward(layer, x, g, stash, masks, init, gain, weight_in, taps, weight_out, bit, split, cargo=None):
    seq, width = g.shape
    hidden = init.shape[1]
    tile = TILE_C
    count = hidden // tile
    spec = mixer_specs(layer, width, hidden, tile)
    column = pl.BlockSpec((seq, tile), lambda i: (0, i))
    dw_specs, dw_shapes = grad_outputs(width, 3 * tile, 3 * hidden, split)
    return call(
        functools.partial(mixer_backward_kernel, layer),
        cargo,
        grid=(count,),
        in_specs=[
            whole(x.shape), whole(g.shape), spec["gain"], spec["gate"], spec["cand"], spec["tap_gate"],
            spec["tap_cand"], spec["out"], whole(masks.shape), spec["init"],
            pl.BlockSpec((1, seq, 2 * tile), lambda i: (i, 0, 0)), column, column, column, SCALAR,
        ],
        out_specs=[
            *dw_specs, whole(g.shape), pl.BlockSpec((1, 8, 2 * tile), lambda i: (i, 0, 0)), whole((1, width)),
        ],
        out_shape=[
            *dw_shapes, shape(g.shape, BF16), shape((count, 8, 2 * tile), F32),
            shape((1, width), F32),
        ],
        scratch_shapes=[
            pltpu.VMEM((width, seq), BF16), pltpu.VMEM((seq, width), BF16), pltpu.VMEM((width, seq), BF16),
            pltpu.VMEM((width // LANES, seq, LANES), F32), pltpu.VMEM((seq, width), F32), pltpu.VMEM((seq, tile), F32),
            pltpu.VMEM((seq, tile), F32), pltpu.VMEM((seq + HALO, 2 * tile), F32),
            pltpu.VMEM((seq, 2 * tile), BF16), pltpu.VMEM((3, seq + HALO, LANES), F32),
        ],
        cost_estimate=cost(seq, 30),
        name="mixer_backward",
        args=(x, g, gain, weight_in, weight_in, taps, taps, weight_out, masks, init, *stash, bit),
    )


def mlp_forward(layer, x, gain, weight_up, bias_up, weight_down, bias_down, cargo=None):
    seq, width = x.shape
    inner = weight_up.shape[2]
    tile = 2 * TILE_F
    return call(
        functools.partial(mlp_forward_kernel, layer),
        cargo,
        grid=(inner // tile,),
        in_specs=[
            whole(x.shape), whole(gain.shape),
            pl.BlockSpec((None, width, tile), lambda i: (layer, 0, i)),
            pl.BlockSpec((2, tile), lambda i: (0, i)),
            pl.BlockSpec((None, tile, width), lambda i: (layer, i, 0)),
            whole(bias_down.shape),
        ],
        out_specs=[whole(x.shape), pl.BlockSpec((seq, tile), lambda i: (0, i))],
        out_shape=[shape(x.shape, BF16), shape((seq, inner), BF16)],
        scratch_shapes=[pltpu.VMEM((seq, width), BF16), pltpu.VMEM((seq, width), F32)],
        cost_estimate=cost(seq, 10),
        name="mlp_forward",
        args=(x, gain, weight_up, bias_up, weight_down, bias_down),
    )


def mlp_backward(layer, x, g, pre, gain, weight_up, weight_down, bit, split, cargo=None):
    seq, width = g.shape
    inner = weight_up.shape[2]
    tile = TILE_F
    dw_specs, dw_shapes = grad_outputs(width, 2 * tile, 2 * inner, split)
    return call(
        functools.partial(mlp_backward_kernel, layer),
        cargo,
        grid=(inner // tile,),
        in_specs=[
            whole(x.shape), whole(g.shape), whole(gain.shape),
            pl.BlockSpec((None, width, tile), lambda i: (layer, 0, i)),
            pl.BlockSpec((None, tile, width), lambda i: (layer, i, 0)),
            pl.BlockSpec((seq, tile), lambda i: (0, i)), SCALAR,
        ],
        out_specs=[
            *dw_specs, whole(g.shape), pl.BlockSpec((1, tile), lambda i: (0, i)), whole((1, width)), whole((1, width)),
        ],
        out_shape=[
            *dw_shapes, shape(g.shape, BF16), shape((1, inner), F32),
            shape((1, width), F32), shape((1, width), F32),
        ],
        scratch_shapes=[
            pltpu.VMEM((width, seq), BF16), pltpu.VMEM((width, seq), BF16), pltpu.VMEM((seq, width), F32),
            pltpu.VMEM((seq, tile), BF16), pltpu.VMEM((seq, tile), BF16),
        ],
        cost_estimate=cost(seq, 20),
        name="mlp_backward",
        args=(x, g, gain, weight_up, weight_down, pre, bit),
    )


def chunk_masks(resets):
    seq = resets.shape[0]
    cut = (1 - resets).astype(F32).reshape(GROUP, seq // GROUP).T
    ends = jnp.zeros((3, 1), F32)
    before = jnp.concatenate([ends, cut[-3:, :-1]], axis=1)
    ahead = jnp.concatenate([cut[:3, 1:], ends], axis=1)
    rows = jnp.concatenate([before, cut, ahead]).reshape(seq + 2 * HALO, 1)
    return jnp.broadcast_to(rows, (seq + 2 * HALO, LANES))


def windows_into(keep_ref, mask_ref):
    count = mask_ref.shape[1]
    first = keep_ref[pl.ds(HALO, count), :]
    second = first * keep_ref[pl.ds(HALO - GROUP, count), :]
    mask_ref[0] = first
    mask_ref[1] = second
    mask_ref[2] = second * keep_ref[pl.ds(HALO - 2 * GROUP, count), :]


def permute(x, axis, pairs):
    return lax.ppermute(x, axis, pairs)


def last_kernel(jobs, split, dp, inner, n_array, *refs):
    arrays, refs = refs[:n_array], refs[n_array:]
    keeps, sends, refs = refs[0:3], refs[3:6], refs[6:]
    if inner:
        later, refs = refs[0:2], refs[2:]
    cotangent, wu_any, wd_any, gain_ref, bu_ref, bd_ref, refs = *refs[:6], refs[6:]
    if inner:
        near_any, refs = refs[0], refs[1:]
    buffers, refs = refs[2:4], refs[4:]
    acts, dxs = buffers
    outs, refs = (refs[:5], refs[5:]) if inner else (refs[:3], refs[3:])
    wu, wd, x_own, g_own, normed, total, grad, y_own, d_own, dgain, redo_sems, own_sems = refs[-12:]
    refs = refs[:-12]
    kept, got, parts, landed, refs = refs[0:3], refs[3:6], refs[6:9], refs[9:12], refs[12:]
    if inner:
        level, first, second, third, refs = refs[0:5], refs[5:10], refs[10:15], refs[15:20], refs[20:]
        z_sems, refs = refs[0], refs[1:]
    else:
        sums, refs = refs[0:3], refs[3:]
    send_sems, recv_sems, local_sems, core_sems, part_sems = refs
    section = lax.axis_index("section")
    where = lax.axis_index("dp")
    bit = (where // split) % 2
    partner = where + split * (1 - 2 * bit)
    steps = [step for step in bits_of(dp) if step != split][-2:]
    low_bit, high_bit = (where // steps[0]) % 2, (where // steps[1]) % 2
    mine = low_bit + 2 * high_bit
    near_bit, far_bit = section % 2, section // 2

    def flipped(mask):
        low, high = mask % 2, mask // 2
        new_low = low_bit + low * (1 - 2 * low_bit)
        new_high = high_bit + high * (1 - 2 * high_bit)
        device = where + steps[0] * (new_low - low_bit) + steps[1] * (new_high - high_bit)
        return new_low + 2 * new_high, device

    def near_copy(n):
        return pltpu.make_async_remote_copy(
            src_ref=level[n].at[:, 1 - near_bit], dst_ref=first[n], send_sem=z_sems.at[0, n], recv_sem=z_sems.at[1, n],
            device_id={"section": section + 1 - 2 * near_bit}, device_id_type=MESH,
        )

    def far_copy(n):
        return pltpu.make_async_remote_copy(
            src_ref=second[n].at[1 - far_bit], dst_ref=third[n], send_sem=z_sems.at[2, n], recv_sem=z_sems.at[3, n],
            device_id={"section": section + 2 - 4 * far_bit}, device_id_type=MESH,
        )

    def near_sum(n):
        for half in range(2):
            both = level[n][half, near_bit].astype(F32) + first[n][half].astype(F32)
            second[n][half] = both.astype(second[n].dtype)

    barrier = pltpu.get_barrier_semaphore()
    for by in range(1, SECTIONS):
        other = (section + by) % SECTIONS
        pl.semaphore_signal(barrier, inc=1, device_id={"section": other}, device_id_type=MESH)
    pl.semaphore_signal(barrier, inc=1, device_id={"dp": partner}, device_id_type=MESH)
    for mask in (1, 2, 3):
        pl.semaphore_signal(barrier, inc=1, device_id={"dp": flipped(mask)[1]}, device_id_type=MESH)
    loads = [pltpu.make_async_copy(keeps[n], kept[n], local_sems.at[n]) for n in range(3)]
    if inner:
        loads += [pltpu.make_async_copy(later[n], level[3 + n], local_sems.at[3 + n]) for n in range(2)]
    for load in loads:
        load.start()
    pl.semaphore_wait(barrier, SECTIONS + 3)

    start, wait = delivery(jobs, arrays, buffers, send_sems, recv_sems)
    redoes = (section == SECTIONS - 1) | (section == 1)
    full = section == SECTIONS - 1
    block = section // 2
    base = SECTIONS - 2 - 2 * block

    def own_copies(part):
        return (
            pltpu.make_async_copy(arrays[SECTIONS + part], acts.at[part], own_sems.at[0]),
            pltpu.make_async_copy(arrays[SECTIONS - 1 - part], dxs.at[part], own_sems.at[1]),
        )

    for part in range(SECTIONS):

        @pl.when(section == part)
        def _(part=part):
            for one in own_copies(part):
                one.start()

    def fetch(row):
        return (
            pltpu.make_async_copy(acts.at[base + row], x_own, redo_sems.at[0]),
            pltpu.make_async_copy(cotangent.at[base + row], g_own, redo_sems.at[1]),
        )

    def fetch_weights():
        return (
            pltpu.make_async_copy(wu_any.at[block], wu, redo_sems.at[2]),
            pltpu.make_async_copy(wd_any.at[block], wd, redo_sems.at[3]),
        )

    def put(row):
        return pltpu.make_async_copy(y_own, acts.at[base + row], redo_sems.at[4])

    def put_grad_rows(row):
        return pltpu.make_async_copy(d_own, dxs.at[base + row], redo_sems.at[5])

    @pl.when(redoes)
    def _():
        for one in fetch(0) + fetch_weights():
            one.start()

    def redo(row):
        for one in fetch(row) + (fetch_weights() if row == 0 else (put(row - 1),)):
            one.wait()

        if row:

            @pl.when(full)
            def _():
                put_grad_rows(row - 1).wait()

        gain = gain_ref[pl.ds(block, 1), :]
        norm_into(x_own, gain, normed)

        def begin_total(rows):
            total[rows, :] = x_own[rows, :].astype(F32) + bd_ref[pl.ds(block, 1), :]

        rows_loop(total.shape[0], 128, begin_total)
        grad[...] = jnp.zeros_like(grad)

        def tile(index, carry):
            cut = pl.ds(pl.multiple_of(index * TILE_F, TILE_F), TILE_F)
            up, down = wu[:, cut], wd[cut, :]
            pre = dot_nn(normed[...], up) + bu_ref[pl.ds(block, 1), cut]
            active, slope = gelu_parts(pre)
            total[...] += dot_nn(active, down)

            @pl.when(full)
            def _():
                low = (dot_nt(g_own[...], down) * slope).astype(BF16)
                grad[...] += dot_nt(low, up)

            return carry

        lax.fori_loop(0, wu.shape[1] // TILE_F, tile, 0)

        def end_total(rows):
            y_own[rows, :] = total[rows, :].astype(BF16)

        rows_loop(total.shape[0], 128, end_total)
        put(row).start()

        @pl.when(full)
        def _():
            norm_backward(x_own, g_own, gain, grad, d_own, dgain)
            put_grad_rows(row).start()

        if row + 1 < FAR:
            for one in fetch(row + 1):
                one.start()

    swaps = []
    for n in range(3):
        swap = pltpu.make_async_remote_copy(
            src_ref=sends[n], dst_ref=got[n], send_sem=core_sems.at[0, n], recv_sem=core_sems.at[1, n],
            device_id={"dp": partner}, device_id_type=MESH,
        )
        swap.start()
        swaps.append(swap)
    start(0, -1)
    for load in loads:
        load.wait()
    near = {}
    if inner:
        near[3] = pltpu.make_async_copy(near_any, first[3], local_sems.at[5])
        near[4] = near_copy(4)
        near[3].start()
        near[4].start()
    moves = []
    for n in range(3):
        swaps[n].wait()
        rows = kept[n].shape[0] // 4
        for mask in (1, 2, 3):
            quarter, device = flipped(mask)
            taken = pl.ds(pl.multiple_of(quarter * rows, rows), rows)
            pair = kept[n][taken, :].astype(F32) + got[n][taken, :].astype(F32)
            parts[n][mask - 1] = pair.astype(parts[n].dtype)
            move = pltpu.make_async_remote_copy(
                src_ref=parts[n].at[mask - 1], dst_ref=landed[n].at[mask - 1],
                send_sem=part_sems.at[0, n, mask - 1], recv_sem=part_sems.at[1, n, mask - 1],
                device_id={"dp": device}, device_id_type=MESH,
            )
            move.start()
            moves.append(move)
    pl.when(redoes)(functools.partial(redo, 0))
    for n in range(3):
        rows = kept[n].shape[0] // 4
        taken = pl.ds(pl.multiple_of(mine * rows, rows), rows)
        summed = kept[n][taken, :].astype(F32) + got[n][taken, :].astype(F32)
        for mask in (1, 2, 3):
            moves[3 * n + mask - 1].wait()
            summed = summed + landed[n][mask - 1].astype(F32)
        if inner:
            share = rows // SECTIONS
            for part in range(SECTIONS):
                level[n][part // 2, part % 2] = summed[part * share : (part + 1) * share].astype(level[n].dtype)
            near[n] = near_copy(n)
            near[n].start()
        else:
            sums[n][...] = summed.astype(sums[n].dtype)
            store = pltpu.make_async_copy(sums[n], outs[n], local_sems.at[n])
            store.start()
            store.wait()
    if not inner:
        start(len(jobs) - 1)
    pl.when(redoes)(functools.partial(redo, 1))
    if inner:
        far = {}
        for n in (3, 4, 0, 1, 2):
            near[n].wait()
            near_sum(n)
            far[n] = far_copy(n)
            far[n].start()
        start(len(jobs) - 1)
        for n in (3, 4, 0, 1, 2):
            far[n].wait()
            block = n // 3
            final = second[n][far_bit].astype(F32) + third[n][...].astype(F32)
            if n == 2:
                outs[4][...] = final
            elif n in (1, 4):
                cand = outs[0].shape[2] // 2
                for at in range(0, final.shape[1], 3 * TILE_C):
                    to = at // 3
                    outs[0][block, :, pl.ds(to, TILE_C)] = final[:, at : at + TILE_C]
                    outs[0][block, :, pl.ds(cand + to, TILE_C)] = final[:, at + TILE_C : at + 2 * TILE_C]
                    outs[1][block, :, pl.ds(to, TILE_C)] = final[:, at + 2 * TILE_C : at + 3 * TILE_C]
            else:
                for at in range(0, final.shape[1], 2 * TILE_F):
                    outs[2][block, :, pl.ds(at // 2, TILE_F)] = final[:, at : at + TILE_F]
                    outs[3][block, :, pl.ds(at // 2, TILE_F)] = final[:, at + TILE_F : at + 2 * TILE_F]

    @pl.when(redoes)
    def _():
        put(1).wait()

    @pl.when(full)
    def _():
        put_grad_rows(1).wait()

    for one in own_copies(0):
        one.wait()
    wait()


def finish(cargo, keeps, sends, later, redo, dp, width):
    inner = later is not None
    columns = [k.shape[1] for k in keeps]
    kinds = [k.dtype for k in keeps]
    rows = keeps[0].shape[0] // 4
    share = rows // SECTIONS
    n_array = len(cargo.arrays)
    jobs = len(cargo.jobs)
    lots = list(zip(columns + columns[:2], kinds + kinds[:2]))
    if inner:
        later = [a.reshape(2, 2, share, -1) for a in later]
        wide = columns[1] // 3
        outs = [shape((2, share, c), F32) for c in (2 * wide, wide, columns[0] // 2, columns[0] // 2)]
        outs += [shape((share, columns[2]), F32)]
        out_specs = [pl.BlockSpec(memory_space=pltpu.VMEM)] * 5
        extra = [pltpu.VMEM((2, 2, share, c), kind) for c, kind in lots]
        extra += [pltpu.VMEM((2, share, c), kind) for c, kind in lots] * 2
        extra += [pltpu.VMEM((share, c), kind) for c, kind in lots]
        extra += [pltpu.SemaphoreType.DMA((4, 5))]
    else:
        later = []
        outs = [shape((rows, c), kind) for c, kind in zip(columns, kinds)]
        out_specs = [ANYWHERE] * 3
        extra = [pltpu.VMEM((rows, c), kind) for c, kind in zip(columns, kinds)]
    n_in = n_array + 6 + len(later)
    return pl.pallas_call(
        functools.partial(last_kernel, cargo.jobs, first_step(dp, width), dp, inner, n_array),
        in_specs=[ANYWHERE] * (n_in + 3) + [pl.BlockSpec(memory_space=pltpu.VMEM)] * 3 + [ANYWHERE] * (2 + inner),
        out_specs=[ANYWHERE] * 2 + out_specs,
        out_shape=[shape(cargo.dims, BF16)] * 2 + outs,
        scratch_shapes=[pltpu.VMEM(k.shape, k.dtype) for k in keeps] * 2
        + [pltpu.VMEM((3, rows, c), kind) for c, kind in zip(columns, kinds)] * 2
        + extra
        + [
            pltpu.SemaphoreType.DMA((jobs,)), pltpu.SemaphoreType.DMA((jobs, SECTIONS)),
            pltpu.SemaphoreType.DMA((6,)), pltpu.SemaphoreType.DMA((2, 3)), pltpu.SemaphoreType.DMA((2, 3, 3)),
        ]
        + [pltpu.VMEM(redo[1].shape[1:], BF16), pltpu.VMEM(redo[2].shape[1:], BF16)]
        + [pltpu.VMEM(cargo.dims[1:], BF16)] * 3 + [pltpu.VMEM(cargo.dims[1:], F32)] * 2
        + [pltpu.VMEM(cargo.dims[1:], BF16)] * 2
        + [pltpu.VMEM((1, width), F32), pltpu.SemaphoreType.DMA((6,)), pltpu.SemaphoreType.DMA((2,))],
        compiler_params=pltpu.CompilerParams(
            vmem_limit_bytes=56 * 1024 * 1024, collective_id=cargo.collective_id, has_side_effects=True
        ),
        input_output_aliases={n_in + 6 + inner: 0, n_in + 7 + inner: 1},
        cost_estimate=cost(1024, 100),
        name="finish",
    )(*cargo.arrays, *keeps, *sends, *later, *redo, *cargo.old)


def add_up(pieces):
    return functools.reduce(jnp.add, [piece.astype(F32) for piece in pieces])


def exchange(addends, axis, size, steps):
    where = lax.axis_index(axis)
    own = sum(((where // step) % 2) << k for k, step in enumerate(steps))
    blocks = [a.reshape((1 << len(steps), -1) + a.shape[-1:]) for a in addends]

    def part(which):
        taken = [lax.dynamic_index_in_dim(b, which, 0, keepdims=False) for b in blocks]
        return add_up(taken).astype(addends[0].dtype)

    result = [part(own)]
    for mask in range(1, 1 << len(steps)):
        flip = sum(step for k, step in enumerate(steps) if mask >> k & 1)
        result.append(permute(part(own ^ mask), axis, [(i, i ^ flip) for i in range(size)]))
    return result


def bits_of(size):
    return [1 << k for k in range(size.bit_length() - 1)]


def first_step(dp, width):
    return SPLIT // (width // dp)


def sum_rest(addends, dp, width):
    rest = [step for step in bits_of(dp) if step != first_step(dp, width)][:-2]
    while rest:
        top, rest = rest[-2:], rest[:-2]
        addends = exchange(addends, "dp", dp, top)
    return addends


def sum_section(addends, sections):
    return add_up(exchange(addends, "section", sections, bits_of(sections)))


def body(
    tokens, resets, init_states, cotangent, mix_gain, mix_in, conv_weight, conv_bias, mix_out,
    mlp_gain, mlp_up, up_bias, mlp_down, down_bias,
):
    dp = lax.axis_size("dp")
    sections = lax.axis_size("section")
    section = lax.axis_index("section")
    width = tokens.shape[2]
    bit = ((lax.axis_index("dp") // first_step(dp, width)) % 2).astype(jnp.int32).reshape(1)

    def own(values, axis):
        return lax.dynamic_index_in_dim(values, section, axis, keepdims=False)

    x0 = own(tokens, 0)
    g4 = own(cotangent, 0)
    masks = chunk_masks(own(resets, 0))
    init = own(init_states, 1)
    mixer_weights = (mix_gain, mix_in, conv_weight, conv_bias, mix_out)
    mlp_weights = (mlp_gain, mlp_up, up_bias, mlp_down, down_bias)
    seq = tokens.shape[1]
    dims = (sections, seq, width)
    sent = {}

    def some(source, part, share, buffer=0, senders=None):
        if senders is None:
            senders = tuple(k for k in range(sections) if k != part)
        kind = (buffer, part, senders)
        first = sent.get(kind, 0)
        sent[kind] = first + share
        return (source, part, seq * first // 32, seq * share // 32, buffer, senders)

    distant, close = tuple(range(FAR)), tuple(range(FAR, sections - 1))
    across = tuple(range(FAR, sections))

    def relay(share):
        first = sent.get("relay", 0)
        sent["relay"] = first + share
        return ("relay", 0, seq * first // 32, seq * share // 32, 0, across)

    def early(cross, near, up):
        jobs = []
        if cross:
            jobs.append(some(0, 1, cross, 0, across))
        if near:
            jobs.append(some(0, 0, near, 0, (1,)))
        if up:
            jobs.append(some(1, 1, up, 0, (0,)))
        return jobs

    x1, *stash0, final0 = mixer_forward(0, x0, masks, init, *mixer_weights)
    x2, pre0 = mlp_forward(0, x1, *mlp_weights)
    cargo = Cargo(1, [x1, x2], [None], early(8, 14, 8), dims)
    x3, *stash1, final1, acts = mixer_forward(1, x2, masks, init, *mixer_weights, cargo)
    x4, pre1 = mlp_forward(1, x3, *mlp_weights)

    back_mixer = (mix_gain, mix_in, conv_weight, mix_out, bit)
    back_mlp = (mlp_gain, mlp_up, mlp_down, bit)
    xs = [x1, x2, x3, x4]
    jobs = early(6, 6, 8)
    jobs += [relay(4), some(2, 3, 6, 0, distant), some(2, 2, 4)]
    quarters = jnp.concatenate([final0, final1, jnp.zeros((GROUP - 2, final0.shape[1]), F32)])
    quarters = jnp.split(quarters, sections, axis=1)
    jobs += [some(4 + part, part, 32, 2)[:2] + (0, GROUP, 1) + some(4 + part, part, 32, 3)[5:] for part in range(sections)]
    shapes = [shape(dims, BF16), shape((sections,) + quarters[0].shape, F32)]
    up1, g3, dbu1, dbd1, dgain_mlp1, acts, ends = mlp_backward(
        1, x3, g4, pre1, *back_mlp, False, Cargo(3, xs + quarters, [acts, None], jobs, shapes)
    )
    here = lax.broadcasted_iota(jnp.int32, (sections, 1, 1), 0) == section
    ends = jnp.where(here, lax.dynamic_index_in_dim(jnp.stack(quarters), section, 0), ends)
    final_states = ends[:, :2].transpose(1, 0, 2)
    mlp1 = lax.psum_scatter(up1, "dp", scatter_dimension=0, tiled=True)
    jobs = early(14, 12, 8)
    jobs += [relay(10), some(2, 3, 16, 0, distant), some(3, 3, 6, 0, close)]
    in1, g2, small1, dgain_mix1, acts = mixer_backward(
        1, x2, g3, stash1, masks, init, *back_mixer, False, Cargo(4, xs, [acts], jobs, dims)
    )
    mix1 = lax.psum_scatter(in1, "dp", scatter_dimension=0, tiled=True)
    jobs = early(4, 0, 8)
    jobs += [relay(10), some(2, 3, 10, 0, distant), some(3, 3, 10, 0, close)]
    up0_keep, up0_send, g1, dbu0, dbd0, dgain_mlp0, acts = mlp_backward(
        0, x1, g2, pre0, *back_mlp, True, Cargo(5, xs, [acts], jobs, dims)
    )
    jobs = [relay(8), some(2, 2, 12), some(3, 3, 16, 0, close)]
    jobs += [some(4, 3, 4, 1, close), some(6, 1, 15, 1)]
    inner = dp == 8 and first_step(dp, width) == 1
    share = width // (dp * sections)
    g1, mlp1 = after(g1, mlp1)
    sources, buffers, shapes = xs + [g3, g2, g1], [acts, None], [shape(dims, BF16)] * 2
    if inner:
        halved = (2, share, mlp1.shape[1])
        sources.append(mlp1.reshape((2,) + halved))
        buffers.append(None)
        shapes.append(shape(halved, BF16))
        jobs.append((None, 7, 2))
    in0_keep, in0_send, g0, small0, dgain_mix0, acts, dxs, *near1 = mixer_backward(
        0, x0, g1, stash0, masks, init, *back_mixer, True, Cargo(6, sources, buffers, jobs, shapes)
    )
    jobs = [some(3, 0, 32, 1, (2, 3)), some(3, 0, 16, 1, (1,)), some(2, 1, 17, 1), some(0, 3, 28, 1, close), some(1, 2, 32, 1), some(6, 2, 16)]
    jobs += [some(3, 0, 16, 1, (1,))]
    cargo = Cargo(7, [g3, g2, g1, g0] + xs, [acts, dxs], jobs, dims)
    redo = (cotangent, mlp_up, mlp_down, mlp_gain, up_bias, down_bias)
    devices = dp * sections
    mix_small = jnp.stack([small0, small1])
    count, tile = mix_small.shape[1], mix_small.shape[3] // 2
    mix_small = mix_small.reshape(2, count, 8, 2, tile).transpose(0, 2, 3, 1, 4).reshape(2, 8, -1)
    lines = [
        jnp.stack([dgain_mix0[0], dgain_mix1[0]]),
        jnp.stack([dgain_mlp0[0], dgain_mlp1[0]]),
        jnp.stack([dbd0[0], dbd1[0]]),
        jnp.stack([dbu0[0], dbu1[0]]),
        mix_small[:, :5].reshape(10, -1),
    ]
    packed = jnp.concatenate(
        [a.reshape(a.shape[0], devices, -1).transpose(1, 0, 2).reshape(devices, -1) for a in lines], axis=1
    )
    share = width // devices
    length = packed.shape[1]
    packed = jnp.pad(packed, ((0, 0), (0, share * LANES - length))).reshape(-1, 2, SPLIT, LANES)

    def half(which):
        return lax.dynamic_index_in_dim(packed, which, 1, keepdims=False).reshape(-1, LANES)

    halves = ((up0_keep, in0_keep, half(bit[0])), (up0_send, in0_send, half(1 - bit[0])))
    if inner:
        acts, dxs, mix_in_grad, mix_out_grad, mlp_up_grad, mlp_down_grad, summed = finish(
            cargo, *halves, (mlp1, mix1), redo + tuple(near1), dp, width
        )
    else:
        acts, dxs, mlp0, mix0, summed = finish(cargo, *halves, None, redo, dp, width)
        parts = [sum_rest([part], dp, width) for part in (mlp0, mix0, summed)] + [[mlp1], [mix1]]
        mlp0, mix0, summed, mlp1, mix1 = [
            sum_section([add_up(part).astype(part[0].dtype)], sections) for part in parts
        ]
        mix_big = jnp.stack([mix0, mix1]).reshape(2, share, -1, 3, TILE_C)
        mix_in_grad = mix_big[:, :, :, :2].transpose(0, 1, 3, 2, 4).reshape(2, share, -1)
        mix_out_grad = mix_big[:, :, :, 2].reshape(2, share, -1)
        mlp_big = jnp.stack([mlp0, mlp1]).reshape(2, share, -1, 2, TILE_F)
        mlp_up_grad = mlp_big[:, :, :, 0].reshape(2, share, -1)
        mlp_down_grad = mlp_big[:, :, :, 1].reshape(2, share, -1)
    mix_out_grad = mix_out_grad.transpose(0, 2, 1)
    mlp_down_grad = mlp_down_grad.transpose(0, 2, 1)

    activations, input_grads = acts[None], dxs[None]

    summed = summed.reshape(-1)[:length]
    pieces, at = [], 0
    for a in lines:
        size = a.size // devices
        pieces.append(summed[at : at + size].reshape(a.shape[0], -1))
        at += size
    mix_gain_grad, mlp_gain_grad, down_bias_grad, up_bias_grad, conv = pieces
    conv = conv.reshape(2, 5, -1)

    return (
        activations, input_grads, final_states, mix_gain_grad, mix_in_grad, conv[:, :4], conv[:, 4],
        mix_out_grad, mlp_gain_grad, mlp_up_grad, up_bias_grad, mlp_down_grad, down_bias_grad,
    )


def solution(mesh):
    both = ("dp", "section")
    return jax.shard_map(
        body,
        mesh=mesh,
        in_specs=(
            P("dp", None, None), P("dp", None), P(None, "dp", None), P("dp", None, None),
            P(), P(), P(), P(), P(), P(), P(), P(), P(), P(),
        ),
        out_specs=(
            P("section", "dp", None, None), P("section", "dp", None, None), P(None, "dp", "section"),
            P(None, both), P(None, both, None), P(None, None, both), P(None, both), P(None, None, both),
            P(None, both), P(None, both, None), P(None, both), P(None, None, both), P(None, both),
        ),
        check_vma=False,
    )
```

```python
import functools

import jax
import jax.numpy as jnp
from jax import lax
from jax.experimental import pallas as pl
from jax.experimental.pallas import tpu as pltpu
from jax.sharding import PartitionSpec as P

EPSILON = 1e-06
LANES = 128
GROUP = 8
TILE_C = 512
TILE_F = 512
BIG = 1024
F32 = jnp.float32
BF16 = jnp.bfloat16
ROOT_2_PI = 0.7978845608028654
CUBIC = 0.044715


def dot_nn(left, right):
    return jnp.dot(left, right, preferred_element_type=F32)


def dot_nt(left, right):
    return lax.dot_general(left, right, (((1,), (1,)), ((), ())), preferred_element_type=F32)


def rows_loop(total, step, fn):
    def at(index, carry):
        fn(pl.ds(pl.multiple_of(index * step, step), step))
        return carry

    lax.fori_loop(0, total // step, at, 0)


def to_chunks(natural, target):
    stride = natural.shape[1] // GROUP

    def at(index, carry):
        for tile in range(natural.shape[0]):
            block = jnp.stack(
                [
                    natural[tile, pl.ds(pl.multiple_of(s * stride + index * GROUP, GROUP), GROUP), :]
                    for s in range(GROUP)
                ]
            )
            rows = pl.ds(pl.multiple_of(index * GROUP * GROUP, GROUP * GROUP), GROUP * GROUP)
            mixed = jnp.swapaxes(block, 0, 1).reshape(GROUP * GROUP, LANES)
            target[rows, pl.ds(tile * LANES, LANES)] = mixed.astype(BF16)
        return carry

    lax.fori_loop(0, stride // GROUP, at, 0, unroll=16)


def to_tokens(chunked, natural):
    stride = natural.shape[1] // GROUP

    def at(index, carry):
        for tile in range(natural.shape[0]):
            rows = pl.ds(pl.multiple_of(index * GROUP * GROUP, GROUP * GROUP), GROUP * GROUP)
            block = chunked[rows, pl.ds(tile * LANES, LANES)].reshape(GROUP, GROUP, LANES)
            mixed = jnp.swapaxes(block, 0, 1)
            for s in range(GROUP):
                to = pl.ds(pl.multiple_of(s * stride + index * GROUP, GROUP), GROUP)
                natural[tile, to, :] = mixed[s]
        return carry

    lax.fori_loop(0, stride // GROUP, at, 0, unroll=16)


def transpose_into(source, target):
    def at(index, carry):
        rows = pl.ds(pl.multiple_of(index * LANES, LANES), LANES)
        target[:, rows] = source[rows, :].astype(F32).T.astype(BF16)
        return carry

    lax.fori_loop(0, source.shape[0] // LANES, at, 0, unroll=8)


def inverse_rms(values):
    return lax.rsqrt(jnp.mean(values * values, axis=-1, keepdims=True) + EPSILON)


def put_tiles(natural, rows, values):
    for tile in range(natural.shape[0]):
        natural[tile, rows, :] = values[:, tile * LANES : (tile + 1) * LANES]


def get_tiles(natural, rows):
    return jnp.concatenate([natural[tile, rows, :] for tile in range(natural.shape[0])], axis=1)


def norm_into(x_ref, gain, target):
    def at(rows):
        source = x_ref[rows, :].astype(F32)
        result = source * inverse_rms(source) * gain
        if len(target.shape) == 3:
            put_tiles(target, rows, result)
        else:
            target[rows, :] = result.astype(target.dtype)

    rows_loop(x_ref.shape[0], 1024, at)


def previous_chunk(values, first_row):
    rolled = pltpu.roll(values, 1, 0)
    position = lax.broadcasted_iota(jnp.int32, values.shape, 0)
    return jnp.where(position == 0, first_row, rolled)


def following_chunk(values):
    rolled = pltpu.roll(values, GROUP - 1, 0)
    position = lax.broadcasted_iota(jnp.int32, values.shape, 0)
    return jnp.where(position == GROUP - 1, 0.0, rolled)


def sigmoid(values):
    return 0.5 * jnp.tanh(0.5 * values) + 0.5


def repeat_rows(values, rows):
    return jnp.concatenate([values] * (rows // values.shape[0]), axis=0)


STEP = 64
SPLIT = 64
HALO = 24


def mixer_forward_kernel(
    layer, begin, x_ref, gain_ref, wg_ref, wc_ref, kg_ref, kc_ref, bg_ref, bc_ref, wo_ref, keep_ref, init_ref,
    y_ref, p_ref, z_ref, cand_ref, h_ref, final_ref,
    normed, natural, total, proj, local, decay, mask_ref,
):
    step = pl.program_id(0)
    seq = x_ref.shape[0]
    width = wg_ref.shape[1]

    @pl.when(step == 0)
    def _():
        windows_into(keep_ref, mask_ref)
        begin()
        norm_into(x_ref, gain_ref[layer : layer + 1, :], natural)
        to_chunks(natural, normed)
        total[...] = jnp.zeros_like(total)

    def project(index, carry):
        rows = pl.ds(pl.multiple_of(index * BIG, BIG), BIG)
        out_rows = pl.ds(pl.multiple_of(index * BIG + HALO, GROUP), BIG)
        block = normed[rows, :]
        for side, weight in enumerate((wg_ref, wc_ref)):
            lanes = pl.ds(side * width, width)
            piece = dot_nn(block, weight[...])
            proj[out_rows, lanes] = piece
            p_ref[0, rows, lanes] = piece.astype(BF16)
        return carry

    lax.fori_loop(0, seq // BIG, project, 0)
    for offset in range(3):
        last = proj[pl.ds(seq + GROUP * offset, GROUP), :]
        proj[pl.ds(GROUP * offset, GROUP), :] = previous_chunk(last, 0.0)

    def scan_step(index, carry):
        base = pl.multiple_of(index * STEP, STEP)
        rows = pl.ds(base, STEP)
        masks = [None] + [mask_ref[k, rows, :] for k in range(3)]
        updated = []
        for tile in range(width // LANES):
            lanes = pl.ds(tile * LANES, LANES)

            def convolve(shift, taps, bias):
                value = bias[layer : layer + 1, lanes]
                for k in range(4):
                    at = pl.ds(pl.multiple_of(base + HALO - GROUP * k, GROUP), STEP)
                    term = proj[at, pl.ds(shift + tile * LANES, LANES)]
                    if k:
                        term = term * masks[k]
                    value = value + taps[k : k + 1, lanes] * term
                return value

            update = sigmoid(convolve(0, kg_ref, bg_ref))
            candidate = convolve(width, kc_ref, bc_ref)
            z_ref[rows, lanes] = update.astype(BF16)
            cand_ref[rows, lanes] = candidate.astype(BF16)
            retain = (1.0 - update) * masks[1]
            inject = update * candidate
            state, product = carry[tile]
            states, products = [], []
            for g in range(STEP // GROUP):
                here = slice(g * GROUP, (g + 1) * GROUP)
                state = retain[here] * state + inject[here]
                product = retain[here] * product
                states.append(state)
                products.append(product)
            local[rows, lanes] = jnp.concatenate(states, axis=0)
            decay[rows, lanes] = jnp.concatenate(products, axis=0)
            updated.append((state, product))
        return tuple(updated)

    zero = jnp.zeros((GROUP, LANES), F32)
    one = jnp.ones((GROUP, LANES), F32)
    ends = lax.fori_loop(0, seq // STEP, scan_step, ((zero, one),) * (width // LANES))
    entries = []
    for tile, (state, product) in enumerate(ends):
        lanes = pl.ds(tile * LANES, LANES)
        current = init_ref[layer : layer + 1, lanes]
        starts = []
        for g in range(GROUP):
            starts.append(current)
            current = product[g : g + 1] * current + state[g : g + 1]
        final_ref[0:1, lanes] = current
        entries.append(jnp.concatenate(starts, axis=0))
    entry = repeat_rows(jnp.concatenate(entries, axis=1), STEP)

    def fix(index, carry):
        rows = pl.ds(pl.multiple_of(index * STEP, STEP), STEP)
        h_ref[rows, :] = (local[rows, :] + decay[rows, :] * entry).astype(BF16)
        return carry

    lax.fori_loop(0, seq // STEP, fix, 0)

    def output(rows):
        total[rows, :] += dot_nn(h_ref[rows, :], wo_ref[...])

    rows_loop(seq, BIG, output)

    @pl.when(step == pl.num_programs(0) - 1)
    def _():
        to_tokens(total, natural)

        def finish(rows):
            y_ref[rows, :] = (x_ref[rows, :].astype(F32) + get_tiles(natural, rows)).astype(BF16)

        rows_loop(seq, 1024, finish)


def norm_backward(x_ref, g_ref, gain, grad_normed, dx_ref, dgain_ref):

    def at(index, carry):
        rows = pl.ds(pl.multiple_of(index * 1024, 1024), 1024)
        source = x_ref[rows, :].astype(F32)
        upstream = g_ref[rows, :].astype(F32)
        incoming = get_tiles(grad_normed, rows) if len(grad_normed.shape) == 3 else grad_normed[rows, :]
        scale = inverse_rms(source)
        scaled = gain * incoming
        mean = jnp.mean(source * scaled, axis=-1, keepdims=True)
        result = upstream + scale * scaled - source * (scale * scale * scale * mean)
        dx_ref[rows, :] = result.astype(BF16)
        return carry + jnp.sum(incoming * source * scale, axis=0, keepdims=True)

    dgain_ref[...] = lax.fori_loop(0, x_ref.shape[0] // 1024, at, jnp.zeros(gain.shape, F32))


def put_grad(refs, bit_ref, lanes, values):
    if len(refs) == 1:
        refs[0][:, lanes] = values.astype(BF16)
        return
    mine = bit_ref[0] == 1
    for pair in range(values.shape[0] // (2 * SPLIT)):
        low = values[2 * pair * SPLIT : (2 * pair + 1) * SPLIT].astype(BF16)
        high = values[(2 * pair + 1) * SPLIT : (2 * pair + 2) * SPLIT].astype(BF16)
        rows = pl.ds(pair * SPLIT, SPLIT)
        refs[0][rows, lanes] = jnp.where(mine, high, low)
        refs[1][rows, lanes] = jnp.where(mine, low, high)


def mixer_backward_kernel(
    layer, begin, x_ref, g_ref, gain_ref, wg_ref, wc_ref, kg_ref, kc_ref, wo_ref, keep_ref, init_ref,
    p_ref, z_ref, cand_ref, h_ref, bit_ref, *rest,
):
    *dw, dx_ref, small_ref, dgain_ref = rest[:-10]
    (normed_t, upstream, upstream_t, natural, total, local, decay, dconv, dproj, mask_ref) = rest[-10:]
    step = pl.program_id(0)
    seq = x_ref.shape[0]
    width = wg_ref.shape[1]
    tiles = width // LANES

    @pl.when(step == 0)
    def _():
        windows_into(keep_ref, mask_ref)
        begin()
        norm_into(x_ref, gain_ref[layer : layer + 1, :], natural)
        to_chunks(natural, upstream)
        transpose_into(upstream, normed_t)

        def widen(rows):
            put_tiles(natural, rows, g_ref[rows, :].astype(F32))

        rows_loop(seq, 1024, widen)
        to_chunks(natural, upstream)
        transpose_into(upstream, upstream_t)
        total[...] = jnp.zeros_like(total)

    def back_hidden(rows):
        local[rows, :] = dot_nt(upstream[rows, :], wo_ref[...])

    rows_loop(seq, BIG, back_hidden)

    def scan_step(index, carry):
        rows = pl.ds(pl.multiple_of(seq - STEP - index * STEP, STEP), STEP)
        keep = mask_ref[0, rows, :]
        updated = []
        for tile in range(tiles):
            lanes = pl.ds(tile * LANES, LANES)
            retain = (1.0 - z_ref[rows, lanes].astype(F32)) * keep
            grads = local[rows, lanes]
            chain, product = carry[tile]
            chains, products = [], []
            for g in reversed(range(STEP // GROUP)):
                here = slice(g * GROUP, (g + 1) * GROUP)
                value = grads[here] + chain
                chains.append(value)
                products.append(product)
                chain = retain[here] * value
                product = retain[here] * product
            local[rows, lanes] = jnp.concatenate(chains[::-1], axis=0)
            decay[rows, lanes] = jnp.concatenate(products[::-1], axis=0)
            updated.append((chain, product))
        return tuple(updated)

    zero = jnp.zeros((GROUP, LANES), F32)
    one = jnp.ones((GROUP, LANES), F32)
    ends = lax.fori_loop(0, seq // STEP, scan_step, ((zero, one),) * tiles)
    entries = []
    for chain, product in ends:
        current = jnp.zeros((1, LANES), F32)
        starts = [current]
        for g in reversed(range(1, GROUP)):
            current = chain[g : g + 1] + product[g : g + 1] * current
            starts.append(current)
        entries.append(jnp.concatenate(starts[::-1], axis=0))

    last_rows = h_ref[pl.ds(seq - 16, 16), :].astype(F32)[GROUP:]
    before = previous_chunk(last_rows, init_ref[layer : layer + 1, :])

    def gates(index, carry):
        base = pl.multiple_of(index * STEP, STEP)
        rows = pl.ds(base, STEP)
        keep = mask_ref[0, rows, :]
        updated = []
        for tile in range(tiles):
            lanes = pl.ds(tile * LANES, LANES)
            hidden = h_ref[rows, lanes].astype(F32)
            delayed = jnp.concatenate([carry[tile], hidden[: STEP - GROUP]], axis=0)
            error = local[rows, lanes] + decay[rows, lanes] * repeat_rows(entries[tile], STEP)
            update = z_ref[rows, lanes].astype(F32)
            candidate = cand_ref[rows, lanes].astype(F32)
            slope = error * (candidate - keep * delayed)
            dconv[rows, lanes] = slope * (update * (1.0 - update))
            dconv[rows, pl.ds(width + tile * LANES, LANES)] = update * error
            updated.append(hidden[STEP - GROUP :])
        return tuple(updated)

    starting = tuple(before[:, tile * LANES : (tile + 1) * LANES] for tile in range(tiles))
    lax.fori_loop(0, seq // STEP, gates, starting)
    for offset in range(3):
        first = dconv[pl.ds(GROUP * offset, GROUP), :]
        dconv[pl.ds(seq + GROUP * offset, GROUP), :] = following_chunk(first)

    def fold(values):
        result = values[0:GROUP]
        for g in range(1, STEP // GROUP):
            result = result + values[g * GROUP : (g + 1) * GROUP]
        return result

    for side, taps in enumerate((kg_ref, kc_ref)):

        def spread(index, carry):
            base = pl.multiple_of(index * STEP, STEP)
            rows = pl.ds(base, STEP)
            updated = []
            for tile in range(tiles):
                lanes = pl.ds(side * width + tile * LANES, LANES)
                weights = pl.ds(tile * LANES, LANES)
                projected = p_ref[0, rows, lanes].astype(F32)
                sums = carry[tile]
                fresh = []
                value = None
                for k in range(4):
                    at = pl.ds(pl.multiple_of(base + GROUP * k, GROUP), STEP)
                    moved = dconv[at, lanes]
                    if k == 0:
                        bias_sum = sums[4] + fold(moved)
                    else:
                        moved = moved * mask_ref[k - 1, at, :]
                    fresh.append(sums[k] + fold(moved * projected))
                    term = taps[k : k + 1, weights] * moved
                    value = term if value is None else value + term
                fresh.append(bias_sum)
                dproj[rows, lanes] = value.astype(BF16)
                updated.append(tuple(fresh))
            return tuple(updated)

        sums = lax.fori_loop(0, seq // STEP, spread, ((zero,) * 5,) * tiles)
        for tile in range(tiles):
            lanes = pl.ds(side * width + tile * LANES, LANES)
            for k in range(5):
                small_ref[0, k : k + 1, lanes] = jnp.sum(sums[tile][k], axis=0, keepdims=True)
            small_ref[0, 5:8, lanes] = jnp.zeros((3, LANES), F32)

    put_grad(dw, bit_ref, pl.ds(0, 2 * width), dot_nn(normed_t[...], dproj[...]))
    put_grad(dw, bit_ref, pl.ds(2 * width, width), dot_nn(upstream_t[...], h_ref[...]))

    def back_normed(rows):
        total[rows, :] += dot_nt(dproj[rows, pl.ds(0, width)], wg_ref[...]) + dot_nt(
            dproj[rows, pl.ds(width, width)], wc_ref[...]
        )

    rows_loop(seq, BIG, back_normed)

    @pl.when(step == pl.num_programs(0) - 1)
    def _():
        to_tokens(total, natural)
        norm_backward(x_ref, g_ref, gain_ref[layer : layer + 1, :], natural, dx_ref, dgain_ref)


def mlp_forward_kernel(
    layer, begin, x_ref, gain_ref, wu_ref, bu_ref, wd_ref, bd_ref, y_ref, u_ref, normed, total
):
    step = pl.program_id(0)
    seq = x_ref.shape[0]

    @pl.when(step == 0)
    def _():
        begin()
        norm_into(x_ref, gain_ref[layer : layer + 1, :], normed)

        def start(rows):
            total[rows, :] = x_ref[rows, :].astype(F32) + bd_ref[layer : layer + 1, :]

        rows_loop(seq, 1024, start)

    def at(rows):
        pre = dot_nn(normed[rows, :], wu_ref[...]) + bu_ref[layer : layer + 1, :]
        u_ref[rows, :] = pre.astype(BF16)
        inner = ROOT_2_PI * (pre + CUBIC * (pre * pre * pre))
        active = (0.5 * pre * (1.0 + jnp.tanh(inner))).astype(BF16)
        total[rows, :] += dot_nn(active, wd_ref[...])

    rows_loop(seq, BIG, at)

    @pl.when(step == pl.num_programs(0) - 1)
    def _():
        def finish(rows):
            y_ref[rows, :] = total[rows, :].astype(BF16)

        rows_loop(seq, 1024, finish)


def gelu_parts(pre):
    square = pre * pre
    bent = jnp.tanh(pre * (ROOT_2_PI + (ROOT_2_PI * CUBIC) * square))
    half = 0.5 * pre
    slope = 0.5 + 0.5 * bent + half * (1.0 - bent * bent) * (
        ROOT_2_PI + (3.0 * ROOT_2_PI * CUBIC) * square
    )
    return (half + half * bent).astype(BF16), slope


def mlp_backward_kernel(
    layer, begin, x_ref, g_ref, gain_ref, wu_ref, wd_ref, u_ref, bit_ref, *rest,
):
    *dw, dx_ref, dbu_ref, dbd_ref, dgain_ref = rest[:-5]
    normed_t, upstream_t, total, active, dpre = rest[-5:]
    step = pl.program_id(0)
    seq = x_ref.shape[0]
    width = wu_ref.shape[1]

    @pl.when(step == 0)
    def _():
        begin()
        norm_into(x_ref, gain_ref[layer : layer + 1, :], active)
        transpose_into(active, normed_t)
        transpose_into(g_ref, upstream_t)

        def at(index, carry):
            rows = pl.ds(pl.multiple_of(index * 1024, 1024), 1024)
            return carry + jnp.sum(g_ref[rows, :].astype(F32), axis=0, keepdims=True)

        dbd_ref[...] = lax.fori_loop(0, seq // 1024, at, jnp.zeros(dbd_ref.shape, F32))
        total[...] = jnp.zeros_like(total)

    def at(index, carry):
        rows = pl.ds(pl.multiple_of(index * BIG, BIG), BIG)
        pre = u_ref[rows, :].astype(F32)
        active[rows, :], slope = gelu_parts(pre)
        low = (dot_nt(g_ref[rows, :], wd_ref[...]) * slope).astype(BF16)
        dpre[rows, :] = low
        total[rows, :] += dot_nt(low, wu_ref[...])
        return carry + jnp.sum(low.astype(F32), axis=0, keepdims=True)

    dbu_ref[...] = lax.fori_loop(0, seq // BIG, at, jnp.zeros(dbu_ref.shape, F32))

    put_grad(dw, bit_ref, pl.ds(0, width), dot_nn(normed_t[...], dpre[...]))
    put_grad(dw, bit_ref, pl.ds(width, width), dot_nn(upstream_t[...], active[...]))

    @pl.when(step == pl.num_programs(0) - 1)
    def _():
        norm_backward(x_ref, g_ref, gain_ref[layer : layer + 1, :], total, dx_ref, dgain_ref)


def shape(dims, kind):
    return jax.ShapeDtypeStruct(dims, kind)


PARAMS = pltpu.CompilerParams(
    dimension_semantics=("arbitrary",), vmem_limit_bytes=56 * 1024 * 1024
)


SCALAR = pl.BlockSpec(memory_space=pltpu.SMEM)
ANYWHERE = pl.BlockSpec(memory_space=pl.ANY)
MESH = pl.DeviceIdType.MESH
SECTIONS = 4
FAR = 2


def greet_sections(section):
    barrier = pltpu.get_barrier_semaphore()
    for by in range(1, SECTIONS):
        other = (section + by) % SECTIONS
        pl.semaphore_signal(barrier, inc=1, device_id={"section": other}, device_id_type=MESH)


def delivery(jobs, sources, buffers, send_sems, recv_sems, relay_sems=None):
    section = lax.axis_index("section")
    near_bit = section % 2

    def near(number):
        _, source, buffer = jobs[number]
        return pltpu.make_async_remote_copy(
            src_ref=sources[source].at[:, 1 - near_bit],
            dst_ref=buffers[buffer],
            send_sem=send_sems.at[number],
            recv_sem=recv_sems.at[number, 0],
            device_id={"section": section + 1 - 2 * near_bit},
            device_id_type=MESH,
        )

    def relay(number, row):
        _, part, first, count, buffer, _ = jobs[number]
        rows = pl.ds(first, count)
        return pltpu.make_async_remote_copy(
            src_ref=buffers[buffer].at[row, rows],
            dst_ref=buffers[buffer].at[row, rows],
            send_sem=relay_sems.at[0, number, row],
            recv_sem=recv_sems.at[number, row],
            device_id={"section": part},
            device_id_type=MESH,
        )

    def sends(job):
        return functools.reduce(jnp.logical_or, [section == sender for sender in job[5]])

    def copy(number, sender):
        source, part, first, count, buffer, _ = jobs[number]
        rows = pl.ds(first, count)
        return pltpu.make_async_remote_copy(
            src_ref=sources[source].at[rows],
            dst_ref=buffers[buffer].at[sender, rows],
            send_sem=send_sems.at[number],
            recv_sem=recv_sems.at[number, sender],
            device_id={"section": part},
            device_id_type=MESH,
        )

    def start(first=0, last=len(jobs)):
        for number, job in list(enumerate(jobs))[first:last]:
            if job[0] is None:
                near(number).start()
                continue
            if job[0] == "relay":

                @pl.when(section == job[1] + 1)
                def _(number=number, job=job):
                    for row in job[5]:
                        relay(number, row).start()

                continue

            @pl.when(sends(job))
            def _(number=number):
                copy(number, section).start()

    def wait():
        for number, job in enumerate(jobs):
            if job[0] is None:
                near(number).wait()
                continue
            if job[0] == "relay":

                @pl.when(section == job[1] + 1)
                def _(number=number, job=job):
                    for row in job[5]:
                        relay(number, row).wait_send()

                @pl.when(section == job[1])
                def _(number=number, job=job):
                    for row in job[5]:
                        relay(number, row).wait_recv()

                continue

            @pl.when(sends(job))
            def _(number=number):
                copy(number, section).wait_send()

            @pl.when(section == job[1])
            def _(number=number, job=job):
                for sender in job[5]:
                    copy(number, sender).wait_recv()

    return start, wait


def after(value, *others):
    return lax.optimization_barrier((value,) + others)


class Cargo:
    def __init__(self, collective_id, arrays, buffers, jobs, dims):
        self.collective_id = collective_id
        self.arrays = list(arrays)
        self.old = [b for b in buffers if b is not None]
        self.buffers = buffers
        self.jobs = jobs
        self.dims = dims


def call(kernel, cargo, *, grid, in_specs, out_specs, out_shape, scratch_shapes, cost_estimate, name, args, aliases=None):
    aliases = dict(aliases or {})
    if cargo is None:
        return pl.pallas_call(
            functools.partial(kernel, lambda: None), grid=grid, in_specs=in_specs, out_specs=out_specs, out_shape=out_shape,
            scratch_shapes=scratch_shapes, compiler_params=PARAMS, cost_estimate=cost_estimate, name=name,
            input_output_aliases=aliases,
        )(*args)
    n_in, n_out = len(in_specs), len(out_specs)
    n_array, n_old, n_buffer = len(cargo.arrays), len(cargo.old), len(cargo.buffers)

    def carrying(*refs):
        ins, refs = refs[:n_in], refs[n_in:]
        arrays, refs = refs[:n_array], refs[n_array + n_old :]
        outs, refs = refs[:n_out], refs[n_out:]
        buffers, refs = refs[:n_buffer], refs[n_buffer:]
        own, (send_sems, recv_sems, relay_sems) = refs[:-3], refs[-3:]
        start, wait = delivery(cargo.jobs, arrays, buffers, send_sems, recv_sems, relay_sems)
        step = pl.program_id(0)

        @pl.when(step == 0)
        def _():
            greet_sections(lax.axis_index("section"))

        def begin():
            pl.semaphore_wait(pltpu.get_barrier_semaphore(), SECTIONS - 1)
            start()

        kernel(begin, *ins, *outs, *own)

        @pl.when(step == pl.num_programs(0) - 1)
        def _():
            wait()

    old = 0
    for number, buffer in enumerate(cargo.buffers):
        if buffer is not None:
            aliases[n_in + n_array + old] = n_out + number
            old += 1
    jobs = len(cargo.jobs)
    return pl.pallas_call(
        carrying,
        grid=grid,
        in_specs=list(in_specs) + [ANYWHERE] * (n_array + n_old),
        out_specs=list(out_specs) + [ANYWHERE] * n_buffer,
        out_shape=list(out_shape) + (cargo.dims if isinstance(cargo.dims, list) else [shape(cargo.dims, BF16)] * n_buffer),
        scratch_shapes=list(scratch_shapes)
        + [pltpu.SemaphoreType.DMA((jobs,)), pltpu.SemaphoreType.DMA((jobs, SECTIONS))]
        + [pltpu.SemaphoreType.DMA((1, jobs, SECTIONS))],
        compiler_params=pltpu.CompilerParams(
            dimension_semantics=("arbitrary",), vmem_limit_bytes=56 * 1024 * 1024,
            collective_id=cargo.collective_id, has_side_effects=True,
        ),
        cost_estimate=cost_estimate,
        name=name,
        input_output_aliases=aliases,
    )(*args, *cargo.arrays, *cargo.old)


def cost(seq, microseconds):
    return pl.CostEstimate(
        flops=int(microseconds * 1.1e9), bytes_accessed=seq * 4096, transcendentals=0
    )


def whole(dims):
    return pl.BlockSpec(dims, lambda i: (0,) * len(dims))


def mixer_specs(layer, width, hidden, tile):
    count = hidden // tile
    return dict(
        gate=pl.BlockSpec((None, width, tile), lambda i: (layer, 0, i)),
        cand=pl.BlockSpec((None, width, tile), lambda i: (layer, 0, count + i)),
        tap_gate=pl.BlockSpec((None, 4, tile), lambda i: (layer, 0, i)),
        tap_cand=pl.BlockSpec((None, 4, tile), lambda i: (layer, 0, count + i)),
        bias_gate=pl.BlockSpec((2, tile), lambda i: (0, i)),
        bias_cand=pl.BlockSpec((2, tile), lambda i: (0, count + i)),
        out=pl.BlockSpec((None, tile, width), lambda i: (layer, i, 0)),
        gain=whole((2, width)),
        init=pl.BlockSpec((2, tile), lambda i: (0, i)),
    )


def mixer_forward(layer, x, masks, init, gain, weight_in, taps, bias, weight_out, cargo=None):
    seq, width = x.shape
    hidden = init.shape[1]
    tile = TILE_C
    count = hidden // tile
    spec = mixer_specs(layer, width, hidden, tile)
    column = pl.BlockSpec((seq, tile), lambda i: (0, i))
    return call(
        functools.partial(mixer_forward_kernel, layer),
        cargo,
        grid=(count,),
        in_specs=[
            whole(x.shape), spec["gain"], spec["gate"], spec["cand"], spec["tap_gate"], spec["tap_cand"],
            spec["bias_gate"], spec["bias_cand"], spec["out"], whole(masks.shape), spec["init"],
        ],
        out_specs=[
            whole(x.shape), pl.BlockSpec((1, seq, 2 * tile), lambda i: (i, 0, 0)), column, column, column,
            pl.BlockSpec((1, tile), lambda i: (0, i)),
        ],
        out_shape=[
            shape(x.shape, BF16), shape((count, seq, 2 * tile), BF16), shape((seq, hidden), BF16),
            shape((seq, hidden), BF16), shape((seq, hidden), BF16), shape((1, hidden), F32),
        ],
        scratch_shapes=[
            pltpu.VMEM((seq, width), BF16), pltpu.VMEM((width // LANES, seq, LANES), F32), pltpu.VMEM((seq, width), F32),
            pltpu.VMEM((seq + HALO, 2 * tile), F32), pltpu.VMEM((seq, tile), F32), pltpu.VMEM((seq, tile), F32),
            pltpu.VMEM((3, seq + HALO, LANES), F32),
        ],
        cost_estimate=cost(seq, 15),
        name="mixer_forward",
        args=(x, gain, weight_in, weight_in, taps, taps, bias, bias, weight_out, masks, init),
    )


def grad_outputs(width, tile, total, split):
    rows = width // 2 if split else width
    parts = 2 if split else 1
    return (
        [pl.BlockSpec((rows, tile), lambda i: (0, i))] * parts,
        [shape((rows, total), BF16)] * parts,
    )


def mixer_backward(layer, x, g, stash, masks, init, gain, weight_in, taps, weight_out, bit, split, cargo=None):
    seq, width = g.shape
    hidden = init.shape[1]
    tile = TILE_C
    count = hidden // tile
    spec = mixer_specs(layer, width, hidden, tile)
    column = pl.BlockSpec((seq, tile), lambda i: (0, i))
    dw_specs, dw_shapes = grad_outputs(width, 3 * tile, 3 * hidden, split)
    return call(
        functools.partial(mixer_backward_kernel, layer),
        cargo,
        grid=(count,),
        in_specs=[
            whole(x.shape), whole(g.shape), spec["gain"], spec["gate"], spec["cand"], spec["tap_gate"],
            spec["tap_cand"], spec["out"], whole(masks.shape), spec["init"],
            pl.BlockSpec((1, seq, 2 * tile), lambda i: (i, 0, 0)), column, column, column, SCALAR,
        ],
        out_specs=[
            *dw_specs, whole(g.shape), pl.BlockSpec((1, 8, 2 * tile), lambda i: (i, 0, 0)), whole((1, width)),
        ],
        out_shape=[
            *dw_shapes, shape(g.shape, BF16), shape((count, 8, 2 * tile), F32),
            shape((1, width), F32),
        ],
        scratch_shapes=[
            pltpu.VMEM((width, seq), BF16), pltpu.VMEM((seq, width), BF16), pltpu.VMEM((width, seq), BF16),
            pltpu.VMEM((width // LANES, seq, LANES), F32), pltpu.VMEM((seq, width), F32), pltpu.VMEM((seq, tile), F32),
            pltpu.VMEM((seq, tile), F32), pltpu.VMEM((seq + HALO, 2 * tile), F32),
            pltpu.VMEM((seq, 2 * tile), BF16), pltpu.VMEM((3, seq + HALO, LANES), F32),
        ],
        cost_estimate=cost(seq, 30),
        name="mixer_backward",
        args=(x, g, gain, weight_in, weight_in, taps, taps, weight_out, masks, init, *stash, bit),
    )


def mlp_forward(layer, x, gain, weight_up, bias_up, weight_down, bias_down, cargo=None):
    seq, width = x.shape
    inner = weight_up.shape[2]
    tile = 2 * TILE_F
    return call(
        functools.partial(mlp_forward_kernel, layer),
        cargo,
        grid=(inner // tile,),
        in_specs=[
            whole(x.shape), whole(gain.shape),
            pl.BlockSpec((None, width, tile), lambda i: (layer, 0, i)),
            pl.BlockSpec((2, tile), lambda i: (0, i)),
            pl.BlockSpec((None, tile, width), lambda i: (layer, i, 0)),
            whole(bias_down.shape),
        ],
        out_specs=[whole(x.shape), pl.BlockSpec((seq, tile), lambda i: (0, i))],
        out_shape=[shape(x.shape, BF16), shape((seq, inner), BF16)],
        scratch_shapes=[pltpu.VMEM((seq, width), BF16), pltpu.VMEM((seq, width), F32)],
        cost_estimate=cost(seq, 10),
        name="mlp_forward",
        args=(x, gain, weight_up, bias_up, weight_down, bias_down),
    )


def mlp_backward(layer, x, g, pre, gain, weight_up, weight_down, bit, split, cargo=None):
    seq, width = g.shape
    inner = weight_up.shape[2]
    tile = TILE_F
    dw_specs, dw_shapes = grad_outputs(width, 2 * tile, 2 * inner, split)
    return call(
        functools.partial(mlp_backward_kernel, layer),
        cargo,
        grid=(inner // tile,),
        in_specs=[
            whole(x.shape), whole(g.shape), whole(gain.shape),
            pl.BlockSpec((None, width, tile), lambda i: (layer, 0, i)),
            pl.BlockSpec((None, tile, width), lambda i: (layer, i, 0)),
            pl.BlockSpec((seq, tile), lambda i: (0, i)), SCALAR,
        ],
        out_specs=[
            *dw_specs, whole(g.shape), pl.BlockSpec((1, tile), lambda i: (0, i)), whole((1, width)), whole((1, width)),
        ],
        out_shape=[
            *dw_shapes, shape(g.shape, BF16), shape((1, inner), F32),
            shape((1, width), F32), shape((1, width), F32),
        ],
        scratch_shapes=[
            pltpu.VMEM((width, seq), BF16), pltpu.VMEM((width, seq), BF16), pltpu.VMEM((seq, width), F32),
            pltpu.VMEM((seq, tile), BF16), pltpu.VMEM((seq, tile), BF16),
        ],
        cost_estimate=cost(seq, 20),
        name="mlp_backward",
        args=(x, g, gain, weight_up, weight_down, pre, bit),
    )


def chunk_masks(resets):
    seq = resets.shape[0]
    cut = (1 - resets).astype(F32).reshape(GROUP, seq // GROUP).T
    ends = jnp.zeros((3, 1), F32)
    before = jnp.concatenate([ends, cut[-3:, :-1]], axis=1)
    ahead = jnp.concatenate([cut[:3, 1:], ends], axis=1)
    rows = jnp.concatenate([before, cut, ahead]).reshape(seq + 2 * HALO, 1)
    return jnp.broadcast_to(rows, (seq + 2 * HALO, LANES))


def windows_into(keep_ref, mask_ref):
    count = mask_ref.shape[1]
    first = keep_ref[pl.ds(HALO, count), :]
    second = first * keep_ref[pl.ds(HALO - GROUP, count), :]
    mask_ref[0] = first
    mask_ref[1] = second
    mask_ref[2] = second * keep_ref[pl.ds(HALO - 2 * GROUP, count), :]


def permute(x, axis, pairs):
    return lax.ppermute(x, axis, pairs)


def last_kernel(jobs, split, dp, inner, n_array, *refs):
    arrays, refs = refs[:n_array], refs[n_array:]
    keeps, sends, refs = refs[0:3], refs[3:6], refs[6:]
    if inner:
        later, refs = refs[0:2], refs[2:]
    cotangent, wu_any, wd_any, gain_ref, bu_ref, bd_ref, refs = *refs[:6], refs[6:]
    if inner:
        near_any, refs = refs[0], refs[1:]
    buffers, refs = refs[2:4], refs[4:]
    acts, dxs = buffers
    outs, refs = (refs[:5], refs[5:]) if inner else (refs[:3], refs[3:])
    wu, wd, x_own, g_own, normed, total, grad, y_own, d_own, dgain, redo_sems, own_sems = refs[-12:]
    refs = refs[:-12]
    kept, got, parts, landed, refs = refs[0:3], refs[3:6], refs[6:9], refs[9:12], refs[12:]
    if inner:
        level, first, second, third, refs = refs[0:5], refs[5:10], refs[10:15], refs[15:20], refs[20:]
        z_sems, refs = refs[0], refs[1:]
    else:
        sums, refs = refs[0:3], refs[3:]
    send_sems, recv_sems, local_sems, core_sems, part_sems = refs
    section = lax.axis_index("section")
    where = lax.axis_index("dp")
    bit = (where // split) % 2
    partner = where + split * (1 - 2 * bit)
    steps = [step for step in bits_of(dp) if step != split][-2:]
    low_bit, high_bit = (where // steps[0]) % 2, (where // steps[1]) % 2
    mine = low_bit + 2 * high_bit
    near_bit, far_bit = section % 2, section // 2

    def flipped(mask):
        low, high = mask % 2, mask // 2
        new_low = low_bit + low * (1 - 2 * low_bit)
        new_high = high_bit + high * (1 - 2 * high_bit)
        device = where + steps[0] * (new_low - low_bit) + steps[1] * (new_high - high_bit)
        return new_low + 2 * new_high, device

    def near_copy(n):
        return pltpu.make_async_remote_copy(
            src_ref=level[n].at[:, 1 - near_bit], dst_ref=first[n], send_sem=z_sems.at[0, n], recv_sem=z_sems.at[1, n],
            device_id={"section": section + 1 - 2 * near_bit}, device_id_type=MESH,
        )

    def far_copy(n):
        return pltpu.make_async_remote_copy(
            src_ref=second[n].at[1 - far_bit], dst_ref=third[n], send_sem=z_sems.at[2, n], recv_sem=z_sems.at[3, n],
            device_id={"section": section + 2 - 4 * far_bit}, device_id_type=MESH,
        )

    def near_sum(n):
        for half in range(2):
            both = level[n][half, near_bit].astype(F32) + first[n][half].astype(F32)
            second[n][half] = both.astype(second[n].dtype)

    barrier = pltpu.get_barrier_semaphore()
    for by in range(1, SECTIONS):
        other = (section + by) % SECTIONS
        pl.semaphore_signal(barrier, inc=1, device_id={"section": other}, device_id_type=MESH)
    pl.semaphore_signal(barrier, inc=1, device_id={"dp": partner}, device_id_type=MESH)
    for mask in (1, 2, 3):
        pl.semaphore_signal(barrier, inc=1, device_id={"dp": flipped(mask)[1]}, device_id_type=MESH)
    loads = [pltpu.make_async_copy(keeps[n], kept[n], local_sems.at[n]) for n in range(3)]
    if inner:
        loads += [pltpu.make_async_copy(later[n], level[3 + n], local_sems.at[3 + n]) for n in range(2)]
    for load in loads:
        load.start()
    pl.semaphore_wait(barrier, SECTIONS + 3)

    start, wait = delivery(jobs, arrays, buffers, send_sems, recv_sems)
    redoes = (section == SECTIONS - 1) | (section == 1)
    full = section == SECTIONS - 1
    block = section // 2
    base = SECTIONS - 2 - 2 * block

    def own_copies(part):
        return (
            pltpu.make_async_copy(arrays[SECTIONS + part], acts.at[part], own_sems.at[0]),
            pltpu.make_async_copy(arrays[SECTIONS - 1 - part], dxs.at[part], own_sems.at[1]),
        )

    for part in range(SECTIONS):

        @pl.when(section == part)
        def _(part=part):
            for one in own_copies(part):
                one.start()

    def fetch(row):
        return (
            pltpu.make_async_copy(acts.at[base + row], x_own, redo_sems.at[0]),
            pltpu.make_async_copy(cotangent.at[base + row], g_own, redo_sems.at[1]),
        )

    def fetch_weights():
        return (
            pltpu.make_async_copy(wu_any.at[block], wu, redo_sems.at[2]),
            pltpu.make_async_copy(wd_any.at[block], wd, redo_sems.at[3]),
        )

    def put(row):
        return pltpu.make_async_copy(y_own, acts.at[base + row], redo_sems.at[4])

    def put_grad_rows(row):
        return pltpu.make_async_copy(d_own, dxs.at[base + row], redo_sems.at[5])

    @pl.when(redoes)
    def _():
        for one in fetch(0) + fetch_weights():
            one.start()

    def redo(row):
        for one in fetch(row) + (fetch_weights() if row == 0 else (put(row - 1),)):
            one.wait()

        if row:

            @pl.when(full)
            def _():
                put_grad_rows(row - 1).wait()

        gain = gain_ref[pl.ds(block, 1), :]
        norm_into(x_own, gain, normed)

        def begin_total(rows):
            total[rows, :] = x_own[rows, :].astype(F32) + bd_ref[pl.ds(block, 1), :]

        rows_loop(total.shape[0], 128, begin_total)
        grad[...] = jnp.zeros_like(grad)

        def tile(index, carry):
            cut = pl.ds(pl.multiple_of(index * TILE_F, TILE_F), TILE_F)
            up, down = wu[:, cut], wd[cut, :]
            pre = dot_nn(normed[...], up) + bu_ref[pl.ds(block, 1), cut]
            active, slope = gelu_parts(pre)
            total[...] += dot_nn(active, down)

            @pl.when(full)
            def _():
                low = (dot_nt(g_own[...], down) * slope).astype(BF16)
                grad[...] += dot_nt(low, up)

            return carry

        lax.fori_loop(0, wu.shape[1] // TILE_F, tile, 0)

        def end_total(rows):
            y_own[rows, :] = total[rows, :].astype(BF16)

        rows_loop(total.shape[0], 128, end_total)
        put(row).start()

        @pl.when(full)
        def _():
            norm_backward(x_own, g_own, gain, grad, d_own, dgain)
            put_grad_rows(row).start()

        if row + 1 < FAR:
            for one in fetch(row + 1):
                one.start()

    swaps = []
    for n in range(3):
        swap = pltpu.make_async_remote_copy(
            src_ref=sends[n], dst_ref=got[n], send_sem=core_sems.at[0, n], recv_sem=core_sems.at[1, n],
            device_id={"dp": partner}, device_id_type=MESH,
        )
        swap.start()
        swaps.append(swap)
    start(0, -1)
    for load in loads:
        load.wait()
    near = {}
    if inner:
        near[3] = pltpu.make_async_copy(near_any, first[3], local_sems.at[5])
        near[4] = near_copy(4)
        near[3].start()
        near[4].start()
    moves = []
    for n in range(3):
        swaps[n].wait()
        rows = kept[n].shape[0] // 4
        for mask in (1, 2, 3):
            quarter, device = flipped(mask)
            taken = pl.ds(pl.multiple_of(quarter * rows, rows), rows)
            pair = kept[n][taken, :].astype(F32) + got[n][taken, :].astype(F32)
            parts[n][mask - 1] = pair.astype(parts[n].dtype)
            move = pltpu.make_async_remote_copy(
                src_ref=parts[n].at[mask - 1], dst_ref=landed[n].at[mask - 1],
                send_sem=part_sems.at[0, n, mask - 1], recv_sem=part_sems.at[1, n, mask - 1],
                device_id={"dp": device}, device_id_type=MESH,
            )
            move.start()
            moves.append(move)
    pl.when(redoes)(functools.partial(redo, 0))
    for n in range(3):
        rows = kept[n].shape[0] // 4
        taken = pl.ds(pl.multiple_of(mine * rows, rows), rows)
        summed = kept[n][taken, :].astype(F32) + got[n][taken, :].astype(F32)
        for mask in (1, 2, 3):
            moves[3 * n + mask - 1].wait()
            summed = summed + landed[n][mask - 1].astype(F32)
        if inner:
            share = rows // SECTIONS
            for part in range(SECTIONS):
                level[n][part // 2, part % 2] = summed[part * share : (part + 1) * share].astype(level[n].dtype)
            near[n] = near_copy(n)
            near[n].start()
        else:
            sums[n][...] = summed.astype(sums[n].dtype)
            store = pltpu.make_async_copy(sums[n], outs[n], local_sems.at[n])
            store.start()
            store.wait()
    if not inner:
        start(len(jobs) - 1)
    pl.when(redoes)(functools.partial(redo, 1))
    if inner:
        far = {}
        for n in (3, 4, 0, 1, 2):
            near[n].wait()
            near_sum(n)
            far[n] = far_copy(n)
            far[n].start()
        start(len(jobs) - 1)
        for n in (3, 4, 0, 1, 2):
            far[n].wait()
            block = n // 3
            final = second[n][far_bit].astype(F32) + third[n][...].astype(F32)
            if n == 2:
                outs[4][...] = final
            elif n in (1, 4):
                cand = outs[0].shape[2] // 2
                for at in range(0, final.shape[1], 3 * TILE_C):
                    to = at // 3
                    outs[0][block, :, pl.ds(to, TILE_C)] = final[:, at : at + TILE_C]
                    outs[0][block, :, pl.ds(cand + to, TILE_C)] = final[:, at + TILE_C : at + 2 * TILE_C]
                    outs[1][block, :, pl.ds(to, TILE_C)] = final[:, at + 2 * TILE_C : at + 3 * TILE_C]
            else:
                for at in range(0, final.shape[1], 2 * TILE_F):
                    outs[2][block, :, pl.ds(at // 2, TILE_F)] = final[:, at : at + TILE_F]
                    outs[3][block, :, pl.ds(at // 2, TILE_F)] = final[:, at + TILE_F : at + 2 * TILE_F]

    @pl.when(redoes)
    def _():
        put(1).wait()

    @pl.when(full)
    def _():
        put_grad_rows(1).wait()

    for one in own_copies(0):
        one.wait()
    wait()


def finish(cargo, keeps, sends, later, redo, dp, width):
    inner = later is not None
    columns = [k.shape[1] for k in keeps]
    kinds = [k.dtype for k in keeps]
    rows = keeps[0].shape[0] // 4
    share = rows // SECTIONS
    n_array = len(cargo.arrays)
    jobs = len(cargo.jobs)
    lots = list(zip(columns + columns[:2], kinds + kinds[:2]))
    if inner:
        later = [a.reshape(2, 2, share, -1) for a in later]
        wide = columns[1] // 3
        outs = [shape((2, share, c), F32) for c in (2 * wide, wide, columns[0] // 2, columns[0] // 2)]
        outs += [shape((share, columns[2]), F32)]
        out_specs = [pl.BlockSpec(memory_space=pltpu.VMEM)] * 5
        extra = [pltpu.VMEM((2, 2, share, c), kind) for c, kind in lots]
        extra += [pltpu.VMEM((2, share, c), kind) for c, kind in lots] * 2
        extra += [pltpu.VMEM((share, c), kind) for c, kind in lots]
        extra += [pltpu.SemaphoreType.DMA((4, 5))]
    else:
        later = []
        outs = [shape((rows, c), kind) for c, kind in zip(columns, kinds)]
        out_specs = [ANYWHERE] * 3
        extra = [pltpu.VMEM((rows, c), kind) for c, kind in zip(columns, kinds)]
    n_in = n_array + 6 + len(later)
    return pl.pallas_call(
        functools.partial(last_kernel, cargo.jobs, first_step(dp, width), dp, inner, n_array),
        in_specs=[ANYWHERE] * (n_in + 3) + [pl.BlockSpec(memory_space=pltpu.VMEM)] * 3 + [ANYWHERE] * (2 + inner),
        out_specs=[ANYWHERE] * 2 + out_specs,
        out_shape=[shape(cargo.dims, BF16)] * 2 + outs,
        scratch_shapes=[pltpu.VMEM(k.shape, k.dtype) for k in keeps] * 2
        + [pltpu.VMEM((3, rows, c), kind) for c, kind in zip(columns, kinds)] * 2
        + extra
        + [
            pltpu.SemaphoreType.DMA((jobs,)), pltpu.SemaphoreType.DMA((jobs, SECTIONS)),
            pltpu.SemaphoreType.DMA((6,)), pltpu.SemaphoreType.DMA((2, 3)), pltpu.SemaphoreType.DMA((2, 3, 3)),
        ]
        + [pltpu.VMEM(redo[1].shape[1:], BF16), pltpu.VMEM(redo[2].shape[1:], BF16)]
        + [pltpu.VMEM(cargo.dims[1:], BF16)] * 3 + [pltpu.VMEM(cargo.dims[1:], F32)] * 2
        + [pltpu.VMEM(cargo.dims[1:], BF16)] * 2
        + [pltpu.VMEM((1, width), F32), pltpu.SemaphoreType.DMA((6,)), pltpu.SemaphoreType.DMA((2,))],
        compiler_params=pltpu.CompilerParams(
            vmem_limit_bytes=56 * 1024 * 1024, collective_id=cargo.collective_id, has_side_effects=True
        ),
        input_output_aliases={n_in + 6 + inner: 0, n_in + 7 + inner: 1},
        cost_estimate=cost(1024, 100),
        name="finish",
    )(*cargo.arrays, *keeps, *sends, *later, *redo, *cargo.old)


def hand_out_kernel(counts, summed, up_bias, conv, conv_bias, mix_gain, mlp_gain, down_bias):
    at = 0
    for kind, (rows, columns) in enumerate(counts):
        for row in range(rows):
            piece = summed[at // LANES : at // LANES + 1, at % LANES : at % LANES + columns]
            if kind == 1 and row % 5 == 4:
                conv_bias[row // 5 : row // 5 + 1, :] = piece
            elif kind == 1:
                conv[row // 5, row % 5 : row % 5 + 1, :] = piece
            else:
                (up_bias, None, mix_gain, mlp_gain, down_bias)[kind][row : row + 1, :] = piece
            at += columns


def hand_out(summed, counts):
    wide, narrow = counts[0][1], counts[2][1]
    in_vmem = pl.BlockSpec(memory_space=pltpu.VMEM)
    return pl.pallas_call(
        functools.partial(hand_out_kernel, counts),
        in_specs=[in_vmem],
        out_specs=[in_vmem] * 6,
        out_shape=[
            shape((2, wide), F32), shape((2, 4, wide), F32), shape((2, wide), F32),
            shape((2, narrow), F32), shape((2, narrow), F32), shape((2, narrow), F32),
        ],
        name="hand_out",
    )(summed)


def add_up(pieces):
    return functools.reduce(jnp.add, [piece.astype(F32) for piece in pieces])


def exchange(addends, axis, size, steps):
    where = lax.axis_index(axis)
    own = sum(((where // step) % 2) << k for k, step in enumerate(steps))
    blocks = [a.reshape((1 << len(steps), -1) + a.shape[-1:]) for a in addends]

    def part(which):
        taken = [lax.dynamic_index_in_dim(b, which, 0, keepdims=False) for b in blocks]
        return add_up(taken).astype(addends[0].dtype)

    result = [part(own)]
    for mask in range(1, 1 << len(steps)):
        flip = sum(step for k, step in enumerate(steps) if mask >> k & 1)
        result.append(permute(part(own ^ mask), axis, [(i, i ^ flip) for i in range(size)]))
    return result


def bits_of(size):
    return [1 << k for k in range(size.bit_length() - 1)]


def first_step(dp, width):
    return SPLIT // (width // dp)


def sum_rest(addends, dp, width):
    rest = [step for step in bits_of(dp) if step != first_step(dp, width)][:-2]
    while rest:
        top, rest = rest[-2:], rest[:-2]
        addends = exchange(addends, "dp", dp, top)
    return addends


def sum_section(addends, sections):
    return add_up(exchange(addends, "section", sections, bits_of(sections)))


def body(
    tokens, resets, init_states, cotangent, mix_gain, mix_in, conv_weight, conv_bias, mix_out,
    mlp_gain, mlp_up, up_bias, mlp_down, down_bias,
):
    dp = lax.axis_size("dp")
    sections = lax.axis_size("section")
    section = lax.axis_index("section")
    width = tokens.shape[2]
    bit = ((lax.axis_index("dp") // first_step(dp, width)) % 2).astype(jnp.int32).reshape(1)

    def own(values, axis):
        return lax.dynamic_index_in_dim(values, section, axis, keepdims=False)

    x0 = own(tokens, 0)
    g4 = own(cotangent, 0)
    masks = chunk_masks(own(resets, 0))
    init = own(init_states, 1)
    mixer_weights = (mix_gain, mix_in, conv_weight, conv_bias, mix_out)
    mlp_weights = (mlp_gain, mlp_up, up_bias, mlp_down, down_bias)
    seq = tokens.shape[1]
    dims = (sections, seq, width)
    sent = {}

    def some(source, part, share, buffer=0, senders=None):
        if senders is None:
            senders = tuple(k for k in range(sections) if k != part)
        kind = (buffer, part, senders)
        first = sent.get(kind, 0)
        sent[kind] = first + share
        return (source, part, seq * first // 32, seq * share // 32, buffer, senders)

    distant, close = tuple(range(FAR)), tuple(range(FAR, sections - 1))
    across = tuple(range(FAR, sections))

    def relay(share):
        first = sent.get("relay", 0)
        sent["relay"] = first + share
        return ("relay", 0, seq * first // 32, seq * share // 32, 0, across)

    def early(cross, near, up):
        jobs = []
        if cross:
            jobs.append(some(0, 1, cross, 0, across))
        if near:
            jobs.append(some(0, 0, near, 0, (1,)))
        if up:
            jobs.append(some(1, 1, up, 0, (0,)))
        return jobs

    x1, *stash0, final0 = mixer_forward(0, x0, masks, init, *mixer_weights)
    x2, pre0 = mlp_forward(0, x1, *mlp_weights)
    cargo = Cargo(1, [x1, x2], [None], early(8, 14, 8), dims)
    x3, *stash1, final1, acts = mixer_forward(1, x2, masks, init, *mixer_weights, cargo)
    x4, pre1 = mlp_forward(1, x3, *mlp_weights)

    back_mixer = (mix_gain, mix_in, conv_weight, mix_out, bit)
    back_mlp = (mlp_gain, mlp_up, mlp_down, bit)
    xs = [x1, x2, x3, x4]
    jobs = early(6, 6, 8)
    jobs += [relay(4), some(2, 3, 6, 0, distant), some(2, 2, 4)]
    quarters = jnp.concatenate([final0, final1, jnp.zeros((GROUP - 2, final0.shape[1]), F32)])
    quarters = jnp.split(quarters, sections, axis=1)
    jobs += [some(4 + part, part, 32, 2)[:2] + (0, GROUP, 1) + some(4 + part, part, 32, 3)[5:] for part in range(sections)]
    shapes = [shape(dims, BF16), shape((sections,) + quarters[0].shape, F32)]
    up1, g3, dbu1, dbd1, dgain_mlp1, acts, ends = mlp_backward(
        1, x3, g4, pre1, *back_mlp, False, Cargo(3, xs + quarters, [acts, None], jobs, shapes)
    )
    here = lax.broadcasted_iota(jnp.int32, (sections, 1, 1), 0) == section
    ends = jnp.where(here, lax.dynamic_index_in_dim(jnp.stack(quarters), section, 0), ends)
    final_states = ends[:, :2].transpose(1, 0, 2)
    mlp1 = lax.psum_scatter(up1, "dp", scatter_dimension=0, tiled=True)
    jobs = early(14, 12, 8)
    jobs += [relay(10), some(2, 3, 16, 0, distant), some(3, 3, 6, 0, close)]
    in1, g2, small1, dgain_mix1, acts = mixer_backward(
        1, x2, g3, stash1, masks, init, *back_mixer, False, Cargo(4, xs, [acts], jobs, dims)
    )
    mix1 = lax.psum_scatter(in1, "dp", scatter_dimension=0, tiled=True)
    jobs = early(4, 0, 8)
    jobs += [relay(10), some(2, 3, 10, 0, distant), some(3, 3, 10, 0, close)]
    up0_keep, up0_send, g1, dbu0, dbd0, dgain_mlp0, acts = mlp_backward(
        0, x1, g2, pre0, *back_mlp, True, Cargo(5, xs, [acts], jobs, dims)
    )
    jobs = [relay(8), some(2, 2, 12), some(3, 3, 16, 0, close)]
    jobs += [some(4, 3, 4, 1, close), some(6, 1, 15, 1)]
    inner = dp == 8 and first_step(dp, width) == 1
    share = width // (dp * sections)
    g1, mlp1 = after(g1, mlp1)
    sources, buffers, shapes = xs + [g3, g2, g1], [acts, None], [shape(dims, BF16)] * 2
    if inner:
        halved = (2, share, mlp1.shape[1])
        sources.append(mlp1.reshape((2,) + halved))
        buffers.append(None)
        shapes.append(shape(halved, BF16))
        jobs.append((None, 7, 2))
    in0_keep, in0_send, g0, small0, dgain_mix0, acts, dxs, *near1 = mixer_backward(
        0, x0, g1, stash0, masks, init, *back_mixer, True, Cargo(6, sources, buffers, jobs, shapes)
    )
    jobs = [some(3, 0, 32, 1, (2, 3)), some(3, 0, 16, 1, (1,)), some(2, 1, 17, 1), some(0, 3, 28, 1, close), some(1, 2, 32, 1), some(6, 2, 16)]
    jobs += [some(3, 0, 16, 1, (1,))]
    cargo = Cargo(7, [g3, g2, g1, g0] + xs, [acts, dxs], jobs, dims)
    redo = (cotangent, mlp_up, mlp_down, mlp_gain, up_bias, down_bias)
    devices = dp * sections
    mix_small = jnp.stack([small0, small1])
    count, tile = mix_small.shape[1], mix_small.shape[3] // 2
    mix_small = mix_small.reshape(2, count, 8, 2, tile).transpose(0, 2, 3, 1, 4).reshape(2, 8, -1)
    lines = [
        jnp.stack([dbu0[0], dbu1[0]]),
        mix_small[:, :5].reshape(10, -1),
        jnp.stack([dgain_mix0[0], dgain_mix1[0]]),
        jnp.stack([dgain_mlp0[0], dgain_mlp1[0]]),
        jnp.stack([dbd0[0], dbd1[0]]),
    ]
    packed = jnp.concatenate(
        [a.reshape(a.shape[0], devices, -1).transpose(1, 0, 2).reshape(devices, -1) for a in lines], axis=1
    )
    share = width // devices
    length = packed.shape[1]
    packed = jnp.pad(packed, ((0, 0), (0, share * LANES - length))).reshape(-1, 2, SPLIT, LANES)

    def half(which):
        return lax.dynamic_index_in_dim(packed, which, 1, keepdims=False).reshape(-1, LANES)

    halves = ((up0_keep, in0_keep, half(bit[0])), (up0_send, in0_send, half(1 - bit[0])))
    if inner:
        acts, dxs, mix_in_grad, mix_out_grad, mlp_up_grad, mlp_down_grad, summed = finish(
            cargo, *halves, (mlp1, mix1), redo + tuple(near1), dp, width
        )
    else:
        acts, dxs, mlp0, mix0, summed = finish(cargo, *halves, None, redo, dp, width)
        parts = [sum_rest([part], dp, width) for part in (mlp0, mix0, summed)] + [[mlp1], [mix1]]
        mlp0, mix0, summed, mlp1, mix1 = [
            sum_section([add_up(part).astype(part[0].dtype)], sections) for part in parts
        ]
        mix_big = jnp.stack([mix0, mix1]).reshape(2, share, -1, 3, TILE_C)
        mix_in_grad = mix_big[:, :, :, :2].transpose(0, 1, 3, 2, 4).reshape(2, share, -1)
        mix_out_grad = mix_big[:, :, :, 2].reshape(2, share, -1)
        mlp_big = jnp.stack([mlp0, mlp1]).reshape(2, share, -1, 2, TILE_F)
        mlp_up_grad = mlp_big[:, :, :, 0].reshape(2, share, -1)
        mlp_down_grad = mlp_big[:, :, :, 1].reshape(2, share, -1)
    mix_out_grad = mix_out_grad.transpose(0, 2, 1)
    mlp_down_grad = mlp_down_grad.transpose(0, 2, 1)

    activations, input_grads = acts[None], dxs[None]

    counts = [(a.shape[0], a.shape[1] // devices) for a in lines]
    if all(LANES % columns == 0 for _, columns in counts) and inner:
        up_bias_grad, conv_grad, conv_bias_grad, mix_gain_grad, mlp_gain_grad, down_bias_grad = hand_out(summed, counts)
    else:
        summed = summed.reshape(-1)[:length]
        pieces, at = [], 0
        for rows, columns in counts:
            pieces.append(summed[at : at + rows * columns].reshape(rows, columns))
            at += rows * columns
        up_bias_grad, conv, mix_gain_grad, mlp_gain_grad, down_bias_grad = pieces
        conv = conv.reshape(2, 5, -1)
        conv_grad, conv_bias_grad = conv[:, :4], conv[:, 4]

    return (
        activations, input_grads, final_states, mix_gain_grad, mix_in_grad, conv_grad, conv_bias_grad,
        mix_out_grad, mlp_gain_grad, mlp_up_grad, up_bias_grad, mlp_down_grad, down_bias_grad,
    )


def solution(mesh):
    both = ("dp", "section")
    return jax.shard_map(
        body,
        mesh=mesh,
        in_specs=(
            P("dp", None, None), P("dp", None), P(None, "dp", None), P("dp", None, None),
            P(), P(), P(), P(), P(), P(), P(), P(), P(), P(),
        ),
        out_specs=(
            P("section", "dp", None, None), P("section", "dp", None, None), P(None, "dp", "section"),
            P(None, both), P(None, both, None), P(None, None, both), P(None, both), P(None, None, both),
            P(None, both), P(None, both, None), P(None, both), P(None, None, both), P(None, both),
        ),
        check_vma=False,
    )
```

```python
import functools

import jax
import jax.numpy as jnp
from jax import lax
from jax.experimental import pallas as pl
from jax.experimental.pallas import tpu as pltpu
from jax.sharding import PartitionSpec as P

EPSILON = 1e-06
LANES = 128
GROUP = 8
TILE_C = 512
TILE_F = 512
BIG = 1024
F32 = jnp.float32
BF16 = jnp.bfloat16
ROOT_2_PI = 0.7978845608028654
CUBIC = 0.044715


def dot_nn(left, right):
    return jnp.dot(left, right, preferred_element_type=F32)


def dot_nt(left, right):
    return lax.dot_general(left, right, (((1,), (1,)), ((), ())), preferred_element_type=F32)


def rows_loop(total, step, fn):
    def at(index, carry):
        fn(pl.ds(pl.multiple_of(index * step, step), step))
        return carry

    lax.fori_loop(0, total // step, at, 0)


def to_chunks(natural, target):
    stride = natural.shape[1] // GROUP

    def at(index, carry):
        for tile in range(natural.shape[0]):
            block = jnp.stack(
                [
                    natural[tile, pl.ds(pl.multiple_of(s * stride + index * GROUP, GROUP), GROUP), :]
                    for s in range(GROUP)
                ]
            )
            rows = pl.ds(pl.multiple_of(index * GROUP * GROUP, GROUP * GROUP), GROUP * GROUP)
            mixed = jnp.swapaxes(block, 0, 1).reshape(GROUP * GROUP, LANES)
            target[rows, pl.ds(tile * LANES, LANES)] = mixed.astype(BF16)
        return carry

    lax.fori_loop(0, stride // GROUP, at, 0, unroll=16)


def to_tokens(chunked, natural):
    stride = natural.shape[1] // GROUP

    def at(index, carry):
        for tile in range(natural.shape[0]):
            rows = pl.ds(pl.multiple_of(index * GROUP * GROUP, GROUP * GROUP), GROUP * GROUP)
            block = chunked[rows, pl.ds(tile * LANES, LANES)].reshape(GROUP, GROUP, LANES)
            mixed = jnp.swapaxes(block, 0, 1)
            for s in range(GROUP):
                to = pl.ds(pl.multiple_of(s * stride + index * GROUP, GROUP), GROUP)
                natural[tile, to, :] = mixed[s]
        return carry

    lax.fori_loop(0, stride // GROUP, at, 0, unroll=16)


def transpose_into(source, target):
    def at(index, carry):
        rows = pl.ds(pl.multiple_of(index * LANES, LANES), LANES)
        target[:, rows] = source[rows, :].astype(F32).T.astype(BF16)
        return carry

    lax.fori_loop(0, source.shape[0] // LANES, at, 0, unroll=8)


def inverse_rms(values):
    return lax.rsqrt(jnp.mean(values * values, axis=-1, keepdims=True) + EPSILON)


def put_tiles(natural, rows, values):
    for tile in range(natural.shape[0]):
        natural[tile, rows, :] = values[:, tile * LANES : (tile + 1) * LANES]


def get_tiles(natural, rows):
    return jnp.concatenate([natural[tile, rows, :] for tile in range(natural.shape[0])], axis=1)


def norm_into(x_ref, gain, target):
    def at(rows):
        source = x_ref[rows, :].astype(F32)
        result = source * inverse_rms(source) * gain
        if len(target.shape) == 3:
            put_tiles(target, rows, result)
        else:
            target[rows, :] = result.astype(target.dtype)

    rows_loop(x_ref.shape[0], 1024, at)


def previous_chunk(values, first_row):
    rolled = pltpu.roll(values, 1, 0)
    position = lax.broadcasted_iota(jnp.int32, values.shape, 0)
    return jnp.where(position == 0, first_row, rolled)


def following_chunk(values):
    rolled = pltpu.roll(values, GROUP - 1, 0)
    position = lax.broadcasted_iota(jnp.int32, values.shape, 0)
    return jnp.where(position == GROUP - 1, 0.0, rolled)


def sigmoid(values):
    return 0.5 * jnp.tanh(0.5 * values) + 0.5


def repeat_rows(values, rows):
    return jnp.concatenate([values] * (rows // values.shape[0]), axis=0)


STEP = 64
SPLIT = 64
HALO = 24


def mixer_forward_kernel(
    layer, begin, x_ref, gain_ref, wg_ref, wc_ref, kg_ref, kc_ref, bg_ref, bc_ref, wo_ref, keep_ref, init_ref,
    y_ref, p_ref, z_ref, cand_ref, h_ref, final_ref,
    normed, natural, total, proj, local, decay, mask_ref,
):
    step = pl.program_id(0)
    seq = x_ref.shape[0]
    width = wg_ref.shape[1]

    @pl.when(step == 0)
    def _():
        windows_into(keep_ref, mask_ref)
        begin()
        norm_into(x_ref, gain_ref[layer : layer + 1, :], natural)
        to_chunks(natural, normed)
        total[...] = jnp.zeros_like(total)

    def project(index, carry):
        rows = pl.ds(pl.multiple_of(index * BIG, BIG), BIG)
        out_rows = pl.ds(pl.multiple_of(index * BIG + HALO, GROUP), BIG)
        block = normed[rows, :]
        for side, weight in enumerate((wg_ref, wc_ref)):
            lanes = pl.ds(side * width, width)
            piece = dot_nn(block, weight[...])
            proj[out_rows, lanes] = piece
            p_ref[0, rows, lanes] = piece.astype(BF16)
        return carry

    lax.fori_loop(0, seq // BIG, project, 0)
    for offset in range(3):
        last = proj[pl.ds(seq + GROUP * offset, GROUP), :]
        proj[pl.ds(GROUP * offset, GROUP), :] = previous_chunk(last, 0.0)

    def scan_step(index, carry):
        base = pl.multiple_of(index * STEP, STEP)
        rows = pl.ds(base, STEP)
        masks = [None] + [mask_ref[k, rows, :] for k in range(3)]
        updated = []
        for tile in range(width // LANES):
            lanes = pl.ds(tile * LANES, LANES)

            def convolve(shift, taps, bias):
                value = bias[layer : layer + 1, lanes]
                for k in range(4):
                    at = pl.ds(pl.multiple_of(base + HALO - GROUP * k, GROUP), STEP)
                    term = proj[at, pl.ds(shift + tile * LANES, LANES)]
                    if k:
                        term = term * masks[k]
                    value = value + taps[k : k + 1, lanes] * term
                return value

            update = sigmoid(convolve(0, kg_ref, bg_ref))
            candidate = convolve(width, kc_ref, bc_ref)
            z_ref[rows, lanes] = update.astype(BF16)
            cand_ref[rows, lanes] = candidate.astype(BF16)
            retain = (1.0 - update) * masks[1]
            inject = update * candidate
            state, product = carry[tile]
            states, products = [], []
            for g in range(STEP // GROUP):
                here = slice(g * GROUP, (g + 1) * GROUP)
                state = retain[here] * state + inject[here]
                product = retain[here] * product
                states.append(state)
                products.append(product)
            local[rows, lanes] = jnp.concatenate(states, axis=0)
            decay[rows, lanes] = jnp.concatenate(products, axis=0)
            updated.append((state, product))
        return tuple(updated)

    zero = jnp.zeros((GROUP, LANES), F32)
    one = jnp.ones((GROUP, LANES), F32)
    ends = lax.fori_loop(0, seq // STEP, scan_step, ((zero, one),) * (width // LANES))
    entries = []
    for tile, (state, product) in enumerate(ends):
        lanes = pl.ds(tile * LANES, LANES)
        current = init_ref[layer : layer + 1, lanes]
        starts = []
        for g in range(GROUP):
            starts.append(current)
            current = product[g : g + 1] * current + state[g : g + 1]
        final_ref[0:1, lanes] = current
        entries.append(jnp.concatenate(starts, axis=0))
    entry = repeat_rows(jnp.concatenate(entries, axis=1), STEP)

    def fix(index, carry):
        rows = pl.ds(pl.multiple_of(index * STEP, STEP), STEP)
        h_ref[rows, :] = (local[rows, :] + decay[rows, :] * entry).astype(BF16)
        return carry

    lax.fori_loop(0, seq // STEP, fix, 0)

    def output(rows):
        total[rows, :] += dot_nn(h_ref[rows, :], wo_ref[...])

    rows_loop(seq, BIG, output)

    @pl.when(step == pl.num_programs(0) - 1)
    def _():
        to_tokens(total, natural)

        def finish(rows):
            y_ref[rows, :] = (x_ref[rows, :].astype(F32) + get_tiles(natural, rows)).astype(BF16)

        rows_loop(seq, 1024, finish)


def norm_backward(x_ref, g_ref, gain, grad_normed, dx_ref, dgain_ref):

    def at(index, carry):
        rows = pl.ds(pl.multiple_of(index * 1024, 1024), 1024)
        source = x_ref[rows, :].astype(F32)
        upstream = g_ref[rows, :].astype(F32)
        incoming = get_tiles(grad_normed, rows) if len(grad_normed.shape) == 3 else grad_normed[rows, :]
        scale = inverse_rms(source)
        scaled = gain * incoming
        mean = jnp.mean(source * scaled, axis=-1, keepdims=True)
        result = upstream + scale * scaled - source * (scale * scale * scale * mean)
        dx_ref[rows, :] = result.astype(BF16)
        return carry + jnp.sum(incoming * source * scale, axis=0, keepdims=True)

    dgain_ref[...] = lax.fori_loop(0, x_ref.shape[0] // 1024, at, jnp.zeros(gain.shape, F32))


def put_grad(refs, bit_ref, lanes, values):
    if len(refs) == 1:
        refs[0][:, lanes] = values.astype(BF16)
        return
    mine = bit_ref[0] == 1
    for pair in range(values.shape[0] // (2 * SPLIT)):
        low = values[2 * pair * SPLIT : (2 * pair + 1) * SPLIT].astype(BF16)
        high = values[(2 * pair + 1) * SPLIT : (2 * pair + 2) * SPLIT].astype(BF16)
        rows = pl.ds(pair * SPLIT, SPLIT)
        refs[0][rows, lanes] = jnp.where(mine, high, low)
        refs[1][rows, lanes] = jnp.where(mine, low, high)


def mixer_backward_kernel(
    layer, begin, x_ref, g_ref, gain_ref, wg_ref, wc_ref, kg_ref, kc_ref, wo_ref, keep_ref, init_ref,
    p_ref, z_ref, cand_ref, h_ref, bit_ref, *rest,
):
    *dw, dx_ref, small_ref, dgain_ref = rest[:-10]
    (normed_t, upstream, upstream_t, natural, total, local, decay, dconv, dproj, mask_ref) = rest[-10:]
    step = pl.program_id(0)
    seq = x_ref.shape[0]
    width = wg_ref.shape[1]
    tiles = width // LANES

    @pl.when(step == 0)
    def _():
        windows_into(keep_ref, mask_ref)
        begin()
        norm_into(x_ref, gain_ref[layer : layer + 1, :], natural)
        to_chunks(natural, upstream)
        transpose_into(upstream, normed_t)

        def widen(rows):
            put_tiles(natural, rows, g_ref[rows, :].astype(F32))

        rows_loop(seq, 1024, widen)
        to_chunks(natural, upstream)
        transpose_into(upstream, upstream_t)
        total[...] = jnp.zeros_like(total)

    def back_hidden(rows):
        local[rows, :] = dot_nt(upstream[rows, :], wo_ref[...])

    rows_loop(seq, BIG, back_hidden)

    def scan_step(index, carry):
        rows = pl.ds(pl.multiple_of(seq - STEP - index * STEP, STEP), STEP)
        keep = mask_ref[0, rows, :]
        updated = []
        for tile in range(tiles):
            lanes = pl.ds(tile * LANES, LANES)
            retain = (1.0 - z_ref[rows, lanes].astype(F32)) * keep
            grads = local[rows, lanes]
            chain, product = carry[tile]
            chains, products = [], []
            for g in reversed(range(STEP // GROUP)):
                here = slice(g * GROUP, (g + 1) * GROUP)
                value = grads[here] + chain
                chains.append(value)
                products.append(product)
                chain = retain[here] * value
                product = retain[here] * product
            local[rows, lanes] = jnp.concatenate(chains[::-1], axis=0)
            decay[rows, lanes] = jnp.concatenate(products[::-1], axis=0)
            updated.append((chain, product))
        return tuple(updated)

    zero = jnp.zeros((GROUP, LANES), F32)
    one = jnp.ones((GROUP, LANES), F32)
    ends = lax.fori_loop(0, seq // STEP, scan_step, ((zero, one),) * tiles)
    entries = []
    for chain, product in ends:
        current = jnp.zeros((1, LANES), F32)
        starts = [current]
        for g in reversed(range(1, GROUP)):
            current = chain[g : g + 1] + product[g : g + 1] * current
            starts.append(current)
        entries.append(jnp.concatenate(starts[::-1], axis=0))

    last_rows = h_ref[pl.ds(seq - 16, 16), :].astype(F32)[GROUP:]
    before = previous_chunk(last_rows, init_ref[layer : layer + 1, :])

    def gates(index, carry):
        base = pl.multiple_of(index * STEP, STEP)
        rows = pl.ds(base, STEP)
        keep = mask_ref[0, rows, :]
        updated = []
        for tile in range(tiles):
            lanes = pl.ds(tile * LANES, LANES)
            hidden = h_ref[rows, lanes].astype(F32)
            delayed = jnp.concatenate([carry[tile], hidden[: STEP - GROUP]], axis=0)
            error = local[rows, lanes] + decay[rows, lanes] * repeat_rows(entries[tile], STEP)
            update = z_ref[rows, lanes].astype(F32)
            candidate = cand_ref[rows, lanes].astype(F32)
            slope = error * (candidate - keep * delayed)
            dconv[rows, lanes] = slope * (update * (1.0 - update))
            dconv[rows, pl.ds(width + tile * LANES, LANES)] = update * error
            updated.append(hidden[STEP - GROUP :])
        return tuple(updated)

    starting = tuple(before[:, tile * LANES : (tile + 1) * LANES] for tile in range(tiles))
    lax.fori_loop(0, seq // STEP, gates, starting)
    for offset in range(3):
        first = dconv[pl.ds(GROUP * offset, GROUP), :]
        dconv[pl.ds(seq + GROUP * offset, GROUP), :] = following_chunk(first)

    def fold(values):
        result = values[0:GROUP]
        for g in range(1, STEP // GROUP):
            result = result + values[g * GROUP : (g + 1) * GROUP]
        return result

    for side, taps in enumerate((kg_ref, kc_ref)):

        def spread(index, carry):
            base = pl.multiple_of(index * STEP, STEP)
            rows = pl.ds(base, STEP)
            updated = []
            for tile in range(tiles):
                lanes = pl.ds(side * width + tile * LANES, LANES)
                weights = pl.ds(tile * LANES, LANES)
                projected = p_ref[0, rows, lanes].astype(F32)
                sums = carry[tile]
                fresh = []
                value = None
                for k in range(4):
                    at = pl.ds(pl.multiple_of(base + GROUP * k, GROUP), STEP)
                    moved = dconv[at, lanes]
                    if k == 0:
                        bias_sum = sums[4] + fold(moved)
                    else:
                        moved = moved * mask_ref[k - 1, at, :]
                    fresh.append(sums[k] + fold(moved * projected))
                    term = taps[k : k + 1, weights] * moved
                    value = term if value is None else value + term
                fresh.append(bias_sum)
                dproj[rows, lanes] = value.astype(BF16)
                updated.append(tuple(fresh))
            return tuple(updated)

        sums = lax.fori_loop(0, seq // STEP, spread, ((zero,) * 5,) * tiles)
        for tile in range(tiles):
            lanes = pl.ds(side * width + tile * LANES, LANES)
            for k in range(5):
                small_ref[0, k : k + 1, lanes] = jnp.sum(sums[tile][k], axis=0, keepdims=True)
            small_ref[0, 5:8, lanes] = jnp.zeros((3, LANES), F32)

    put_grad(dw, bit_ref, pl.ds(0, 2 * width), dot_nn(normed_t[...], dproj[...]))
    put_grad(dw, bit_ref, pl.ds(2 * width, width), dot_nn(upstream_t[...], h_ref[...]))

    def back_normed(rows):
        total[rows, :] += dot_nt(dproj[rows, pl.ds(0, width)], wg_ref[...]) + dot_nt(
            dproj[rows, pl.ds(width, width)], wc_ref[...]
        )

    rows_loop(seq, BIG, back_normed)

    @pl.when(step == pl.num_programs(0) - 1)
    def _():
        to_tokens(total, natural)
        norm_backward(x_ref, g_ref, gain_ref[layer : layer + 1, :], natural, dx_ref, dgain_ref)


def mlp_forward_kernel(
    layer, begin, x_ref, gain_ref, wu_ref, bu_ref, wd_ref, bd_ref, y_ref, u_ref, normed, total
):
    step = pl.program_id(0)
    seq = x_ref.shape[0]

    @pl.when(step == 0)
    def _():
        begin()
        norm_into(x_ref, gain_ref[layer : layer + 1, :], normed)

        def start(rows):
            total[rows, :] = x_ref[rows, :].astype(F32) + bd_ref[layer : layer + 1, :]

        rows_loop(seq, 1024, start)

    def at(rows):
        pre = dot_nn(normed[rows, :], wu_ref[...]) + bu_ref[layer : layer + 1, :]
        u_ref[rows, :] = pre.astype(BF16)
        inner = ROOT_2_PI * (pre + CUBIC * (pre * pre * pre))
        active = (0.5 * pre * (1.0 + jnp.tanh(inner))).astype(BF16)
        total[rows, :] += dot_nn(active, wd_ref[...])

    rows_loop(seq, BIG, at)

    @pl.when(step == pl.num_programs(0) - 1)
    def _():
        def finish(rows):
            y_ref[rows, :] = total[rows, :].astype(BF16)

        rows_loop(seq, 1024, finish)


def gelu_parts(pre):
    square = pre * pre
    bent = jnp.tanh(pre * (ROOT_2_PI + (ROOT_2_PI * CUBIC) * square))
    half = 0.5 * pre
    slope = 0.5 + 0.5 * bent + half * (1.0 - bent * bent) * (
        ROOT_2_PI + (3.0 * ROOT_2_PI * CUBIC) * square
    )
    return (half + half * bent).astype(BF16), slope


def mlp_backward_kernel(
    layer, begin, x_ref, g_ref, gain_ref, wu_ref, wd_ref, u_ref, bit_ref, *rest,
):
    *dw, dx_ref, dbu_ref, dbd_ref, dgain_ref = rest[:-5]
    normed_t, upstream_t, total, active, dpre = rest[-5:]
    step = pl.program_id(0)
    seq = x_ref.shape[0]
    width = wu_ref.shape[1]

    @pl.when(step == 0)
    def _():
        begin()
        norm_into(x_ref, gain_ref[layer : layer + 1, :], active)
        transpose_into(active, normed_t)
        transpose_into(g_ref, upstream_t)

        def at(index, carry):
            rows = pl.ds(pl.multiple_of(index * 1024, 1024), 1024)
            return carry + jnp.sum(g_ref[rows, :].astype(F32), axis=0, keepdims=True)

        dbd_ref[...] = lax.fori_loop(0, seq // 1024, at, jnp.zeros(dbd_ref.shape, F32))
        total[...] = jnp.zeros_like(total)

    def at(index, carry):
        rows = pl.ds(pl.multiple_of(index * BIG, BIG), BIG)
        pre = u_ref[rows, :].astype(F32)
        active[rows, :], slope = gelu_parts(pre)
        low = (dot_nt(g_ref[rows, :], wd_ref[...]) * slope).astype(BF16)
        dpre[rows, :] = low
        total[rows, :] += dot_nt(low, wu_ref[...])
        return carry + jnp.sum(low.astype(F32), axis=0, keepdims=True)

    dbu_ref[...] = lax.fori_loop(0, seq // BIG, at, jnp.zeros(dbu_ref.shape, F32))

    put_grad(dw, bit_ref, pl.ds(0, width), dot_nn(normed_t[...], dpre[...]))
    put_grad(dw, bit_ref, pl.ds(width, width), dot_nn(upstream_t[...], active[...]))

    @pl.when(step == pl.num_programs(0) - 1)
    def _():
        norm_backward(x_ref, g_ref, gain_ref[layer : layer + 1, :], total, dx_ref, dgain_ref)


def shape(dims, kind):
    return jax.ShapeDtypeStruct(dims, kind)


PARAMS = pltpu.CompilerParams(
    dimension_semantics=("arbitrary",), vmem_limit_bytes=56 * 1024 * 1024
)


SCALAR = pl.BlockSpec(memory_space=pltpu.SMEM)
ANYWHERE = pl.BlockSpec(memory_space=pl.ANY)
MESH = pl.DeviceIdType.MESH
SECTIONS = 4
FAR = 2


def greet_sections(section):
    barrier = pltpu.get_barrier_semaphore()
    for by in range(1, SECTIONS):
        other = (section + by) % SECTIONS
        pl.semaphore_signal(barrier, inc=1, device_id={"section": other}, device_id_type=MESH)


def delivery(jobs, sources, buffers, send_sems, recv_sems, relay_sems=None):
    section = lax.axis_index("section")
    near_bit = section % 2

    def near(number):
        _, source, buffer = jobs[number]
        return pltpu.make_async_remote_copy(
            src_ref=sources[source].at[:, 1 - near_bit],
            dst_ref=buffers[buffer],
            send_sem=send_sems.at[number],
            recv_sem=recv_sems.at[number, 0],
            device_id={"section": section + 1 - 2 * near_bit},
            device_id_type=MESH,
        )

    def relay(number, row):
        _, part, first, count, buffer, _ = jobs[number]
        rows = pl.ds(first, count)
        return pltpu.make_async_remote_copy(
            src_ref=buffers[buffer].at[row, rows],
            dst_ref=buffers[buffer].at[row, rows],
            send_sem=relay_sems.at[0, number, row],
            recv_sem=recv_sems.at[number, row],
            device_id={"section": part},
            device_id_type=MESH,
        )

    def sends(job):
        return functools.reduce(jnp.logical_or, [section == sender for sender in job[5]])

    def copy(number, sender):
        source, part, first, count, buffer, _ = jobs[number]
        rows = pl.ds(first, count)
        return pltpu.make_async_remote_copy(
            src_ref=sources[source].at[rows],
            dst_ref=buffers[buffer].at[sender, rows],
            send_sem=send_sems.at[number],
            recv_sem=recv_sems.at[number, sender],
            device_id={"section": part},
            device_id_type=MESH,
        )

    def start(first=0, last=len(jobs)):
        for number, job in list(enumerate(jobs))[first:last]:
            if job[0] is None:
                near(number).start()
                continue
            if job[0] == "relay":

                @pl.when(section == job[1] + 1)
                def _(number=number, job=job):
                    for row in job[5]:
                        relay(number, row).start()

                continue

            @pl.when(sends(job))
            def _(number=number):
                copy(number, section).start()

    def wait():
        for number, job in enumerate(jobs):
            if job[0] is None:
                near(number).wait()
                continue
            if job[0] == "relay":

                @pl.when(section == job[1] + 1)
                def _(number=number, job=job):
                    for row in job[5]:
                        relay(number, row).wait_send()

                @pl.when(section == job[1])
                def _(number=number, job=job):
                    for row in job[5]:
                        relay(number, row).wait_recv()

                continue

            @pl.when(sends(job))
            def _(number=number):
                copy(number, section).wait_send()

            @pl.when(section == job[1])
            def _(number=number, job=job):
                for sender in job[5]:
                    copy(number, sender).wait_recv()

    return start, wait


def after(value, *others):
    return lax.optimization_barrier((value,) + others)


class Cargo:
    def __init__(self, collective_id, arrays, buffers, jobs, dims):
        self.collective_id = collective_id
        self.arrays = list(arrays)
        self.old = [b for b in buffers if b is not None]
        self.buffers = buffers
        self.jobs = jobs
        self.dims = dims


def call(kernel, cargo, *, grid, in_specs, out_specs, out_shape, scratch_shapes, cost_estimate, name, args, aliases=None):
    aliases = dict(aliases or {})
    if cargo is None:
        return pl.pallas_call(
            functools.partial(kernel, lambda: None), grid=grid, in_specs=in_specs, out_specs=out_specs, out_shape=out_shape,
            scratch_shapes=scratch_shapes, compiler_params=PARAMS, cost_estimate=cost_estimate, name=name,
            input_output_aliases=aliases,
        )(*args)
    n_in, n_out = len(in_specs), len(out_specs)
    n_array, n_old, n_buffer = len(cargo.arrays), len(cargo.old), len(cargo.buffers)

    def carrying(*refs):
        ins, refs = refs[:n_in], refs[n_in:]
        arrays, refs = refs[:n_array], refs[n_array + n_old :]
        outs, refs = refs[:n_out], refs[n_out:]
        buffers, refs = refs[:n_buffer], refs[n_buffer:]
        own, (send_sems, recv_sems, relay_sems) = refs[:-3], refs[-3:]
        start, wait = delivery(cargo.jobs, arrays, buffers, send_sems, recv_sems, relay_sems)
        step = pl.program_id(0)

        @pl.when(step == 0)
        def _():
            greet_sections(lax.axis_index("section"))

        def begin():
            pl.semaphore_wait(pltpu.get_barrier_semaphore(), SECTIONS - 1)
            start()

        kernel(begin, *ins, *outs, *own)

        @pl.when(step == pl.num_programs(0) - 1)
        def _():
            wait()

    old = 0
    for number, buffer in enumerate(cargo.buffers):
        if buffer is not None:
            aliases[n_in + n_array + old] = n_out + number
            old += 1
    jobs = len(cargo.jobs)
    return pl.pallas_call(
        carrying,
        grid=grid,
        in_specs=list(in_specs) + [ANYWHERE] * (n_array + n_old),
        out_specs=list(out_specs) + [ANYWHERE] * n_buffer,
        out_shape=list(out_shape) + (cargo.dims if isinstance(cargo.dims, list) else [shape(cargo.dims, BF16)] * n_buffer),
        scratch_shapes=list(scratch_shapes)
        + [pltpu.SemaphoreType.DMA((jobs,)), pltpu.SemaphoreType.DMA((jobs, SECTIONS))]
        + [pltpu.SemaphoreType.DMA((1, jobs, SECTIONS))],
        compiler_params=pltpu.CompilerParams(
            dimension_semantics=("arbitrary",), vmem_limit_bytes=56 * 1024 * 1024,
            collective_id=cargo.collective_id, has_side_effects=True,
        ),
        cost_estimate=cost_estimate,
        name=name,
        input_output_aliases=aliases,
    )(*args, *cargo.arrays, *cargo.old)


def cost(seq, microseconds):
    return pl.CostEstimate(
        flops=int(microseconds * 1.1e9), bytes_accessed=seq * 4096, transcendentals=0
    )


def whole(dims):
    return pl.BlockSpec(dims, lambda i: (0,) * len(dims))


def mixer_specs(layer, width, hidden, tile):
    count = hidden // tile
    return dict(
        gate=pl.BlockSpec((None, width, tile), lambda i: (layer, 0, i)),
        cand=pl.BlockSpec((None, width, tile), lambda i: (layer, 0, count + i)),
        tap_gate=pl.BlockSpec((None, 4, tile), lambda i: (layer, 0, i)),
        tap_cand=pl.BlockSpec((None, 4, tile), lambda i: (layer, 0, count + i)),
        bias_gate=pl.BlockSpec((2, tile), lambda i: (0, i)),
        bias_cand=pl.BlockSpec((2, tile), lambda i: (0, count + i)),
        out=pl.BlockSpec((None, tile, width), lambda i: (layer, i, 0)),
        gain=whole((2, width)),
        init=pl.BlockSpec((2, tile), lambda i: (0, i)),
    )


def mixer_forward(layer, x, masks, init, gain, weight_in, taps, bias, weight_out, cargo=None):
    seq, width = x.shape
    hidden = init.shape[1]
    tile = TILE_C
    count = hidden // tile
    spec = mixer_specs(layer, width, hidden, tile)
    column = pl.BlockSpec((seq, tile), lambda i: (0, i))
    return call(
        functools.partial(mixer_forward_kernel, layer),
        cargo,
        grid=(count,),
        in_specs=[
            whole(x.shape), spec["gain"], spec["gate"], spec["cand"], spec["tap_gate"], spec["tap_cand"],
            spec["bias_gate"], spec["bias_cand"], spec["out"], whole(masks.shape), spec["init"],
        ],
        out_specs=[
            whole(x.shape), pl.BlockSpec((1, seq, 2 * tile), lambda i: (i, 0, 0)), column, column, column,
            pl.BlockSpec((1, tile), lambda i: (0, i)),
        ],
        out_shape=[
            shape(x.shape, BF16), shape((count, seq, 2 * tile), BF16), shape((seq, hidden), BF16),
            shape((seq, hidden), BF16), shape((seq, hidden), BF16), shape((1, hidden), F32),
        ],
        scratch_shapes=[
            pltpu.VMEM((seq, width), BF16), pltpu.VMEM((width // LANES, seq, LANES), F32), pltpu.VMEM((seq, width), F32),
            pltpu.VMEM((seq + HALO, 2 * tile), F32), pltpu.VMEM((seq, tile), F32), pltpu.VMEM((seq, tile), F32),
            pltpu.VMEM((3, seq + HALO, LANES), F32),
        ],
        cost_estimate=cost(seq, 15),
        name="mixer_forward",
        args=(x, gain, weight_in, weight_in, taps, taps, bias, bias, weight_out, masks, init),
    )


def grad_outputs(width, tile, total, split):
    rows = width // 2 if split else width
    parts = 2 if split else 1
    return (
        [pl.BlockSpec((rows, tile), lambda i: (0, i))] * parts,
        [shape((rows, total), BF16)] * parts,
    )


def mixer_backward(layer, x, g, stash, masks, init, gain, weight_in, taps, weight_out, bit, split, cargo=None):
    seq, width = g.shape
    hidden = init.shape[1]
    tile = TILE_C
    count = hidden // tile
    spec = mixer_specs(layer, width, hidden, tile)
    column = pl.BlockSpec((seq, tile), lambda i: (0, i))
    dw_specs, dw_shapes = grad_outputs(width, 3 * tile, 3 * hidden, split)
    return call(
        functools.partial(mixer_backward_kernel, layer),
        cargo,
        grid=(count,),
        in_specs=[
            whole(x.shape), whole(g.shape), spec["gain"], spec["gate"], spec["cand"], spec["tap_gate"],
            spec["tap_cand"], spec["out"], whole(masks.shape), spec["init"],
            pl.BlockSpec((1, seq, 2 * tile), lambda i: (i, 0, 0)), column, column, column, SCALAR,
        ],
        out_specs=[
            *dw_specs, whole(g.shape), pl.BlockSpec((1, 8, 2 * tile), lambda i: (i, 0, 0)), whole((1, width)),
        ],
        out_shape=[
            *dw_shapes, shape(g.shape, BF16), shape((count, 8, 2 * tile), F32),
            shape((1, width), F32),
        ],
        scratch_shapes=[
            pltpu.VMEM((width, seq), BF16), pltpu.VMEM((seq, width), BF16), pltpu.VMEM((width, seq), BF16),
            pltpu.VMEM((width // LANES, seq, LANES), F32), pltpu.VMEM((seq, width), F32), pltpu.VMEM((seq, tile), F32),
            pltpu.VMEM((seq, tile), F32), pltpu.VMEM((seq + HALO, 2 * tile), F32),
            pltpu.VMEM((seq, 2 * tile), BF16), pltpu.VMEM((3, seq + HALO, LANES), F32),
        ],
        cost_estimate=cost(seq, 30),
        name="mixer_backward",
        args=(x, g, gain, weight_in, weight_in, taps, taps, weight_out, masks, init, *stash, bit),
    )


def mlp_forward(layer, x, gain, weight_up, bias_up, weight_down, bias_down, cargo=None):
    seq, width = x.shape
    inner = weight_up.shape[2]
    tile = 2 * TILE_F
    return call(
        functools.partial(mlp_forward_kernel, layer),
        cargo,
        grid=(inner // tile,),
        in_specs=[
            whole(x.shape), whole(gain.shape),
            pl.BlockSpec((None, width, tile), lambda i: (layer, 0, i)),
            pl.BlockSpec((2, tile), lambda i: (0, i)),
            pl.BlockSpec((None, tile, width), lambda i: (layer, i, 0)),
            whole(bias_down.shape),
        ],
        out_specs=[whole(x.shape), pl.BlockSpec((seq, tile), lambda i: (0, i))],
        out_shape=[shape(x.shape, BF16), shape((seq, inner), BF16)],
        scratch_shapes=[pltpu.VMEM((seq, width), BF16), pltpu.VMEM((seq, width), F32)],
        cost_estimate=cost(seq, 10),
        name="mlp_forward",
        args=(x, gain, weight_up, bias_up, weight_down, bias_down),
    )


def mlp_backward(layer, x, g, pre, gain, weight_up, weight_down, bit, split, cargo=None):
    seq, width = g.shape
    inner = weight_up.shape[2]
    tile = TILE_F
    dw_specs, dw_shapes = grad_outputs(width, 2 * tile, 2 * inner, split)
    return call(
        functools.partial(mlp_backward_kernel, layer),
        cargo,
        grid=(inner // tile,),
        in_specs=[
            whole(x.shape), whole(g.shape), whole(gain.shape),
            pl.BlockSpec((None, width, tile), lambda i: (layer, 0, i)),
            pl.BlockSpec((None, tile, width), lambda i: (layer, i, 0)),
            pl.BlockSpec((seq, tile), lambda i: (0, i)), SCALAR,
        ],
        out_specs=[
            *dw_specs, whole(g.shape), pl.BlockSpec((1, tile), lambda i: (0, i)), whole((1, width)), whole((1, width)),
        ],
        out_shape=[
            *dw_shapes, shape(g.shape, BF16), shape((1, inner), F32),
            shape((1, width), F32), shape((1, width), F32),
        ],
        scratch_shapes=[
            pltpu.VMEM((width, seq), BF16), pltpu.VMEM((width, seq), BF16), pltpu.VMEM((seq, width), F32),
            pltpu.VMEM((seq, tile), BF16), pltpu.VMEM((seq, tile), BF16),
        ],
        cost_estimate=cost(seq, 20),
        name="mlp_backward",
        args=(x, g, gain, weight_up, weight_down, pre, bit),
    )


def chunk_masks(resets):
    seq = resets.shape[0]
    cut = (1 - resets).astype(F32).reshape(GROUP, seq // GROUP).T
    ends = jnp.zeros((3, 1), F32)
    before = jnp.concatenate([ends, cut[-3:, :-1]], axis=1)
    ahead = jnp.concatenate([cut[:3, 1:], ends], axis=1)
    rows = jnp.concatenate([before, cut, ahead]).reshape(seq + 2 * HALO, 1)
    return jnp.broadcast_to(rows, (seq + 2 * HALO, LANES))


def windows_into(keep_ref, mask_ref):
    count = mask_ref.shape[1]
    first = keep_ref[pl.ds(HALO, count), :]
    second = first * keep_ref[pl.ds(HALO - GROUP, count), :]
    mask_ref[0] = first
    mask_ref[1] = second
    mask_ref[2] = second * keep_ref[pl.ds(HALO - 2 * GROUP, count), :]


def permute(x, axis, pairs):
    return lax.ppermute(x, axis, pairs)


def last_kernel(jobs, split, dp, inner, n_array, *refs):
    arrays, refs = refs[:n_array], refs[n_array:]
    keeps, sends, refs = refs[0:3], refs[3:6], refs[6:]
    if inner:
        later, refs = refs[0:2], refs[2:]
    cotangent, wu_any, wd_any, gain_ref, bu_ref, bd_ref, refs = *refs[:6], refs[6:]
    if inner:
        near_any, refs = refs[0], refs[1:]
    buffers, refs = refs[2:4], refs[4:]
    acts, dxs = buffers
    outs, refs = (refs[:5], refs[5:]) if inner else (refs[:3], refs[3:])
    wu, wd, x_own, g_own, normed, total, grad, y_own, d_own, dgain, redo_sems, own_sems = refs[-12:]
    refs = refs[:-12]
    kept, got, parts, landed, refs = refs[0:3], refs[3:6], refs[6:9], refs[9:12], refs[12:]
    if inner:
        level, first, second, third, refs = refs[0:5], refs[5:10], refs[10:15], refs[15:20], refs[20:]
        z_sems, refs = refs[0], refs[1:]
    else:
        sums, refs = refs[0:3], refs[3:]
    send_sems, recv_sems, local_sems, core_sems, part_sems = refs
    section = lax.axis_index("section")
    where = lax.axis_index("dp")
    bit = (where // split) % 2
    partner = where + split * (1 - 2 * bit)
    steps = [step for step in bits_of(dp) if step != split][-2:]
    low_bit, high_bit = (where // steps[0]) % 2, (where // steps[1]) % 2
    mine = low_bit + 2 * high_bit
    near_bit, far_bit = section % 2, section // 2

    def flipped(mask):
        low, high = mask % 2, mask // 2
        new_low = low_bit + low * (1 - 2 * low_bit)
        new_high = high_bit + high * (1 - 2 * high_bit)
        device = where + steps[0] * (new_low - low_bit) + steps[1] * (new_high - high_bit)
        return new_low + 2 * new_high, device

    def near_copy(n):
        return pltpu.make_async_remote_copy(
            src_ref=level[n].at[:, 1 - near_bit], dst_ref=first[n], send_sem=z_sems.at[0, n], recv_sem=z_sems.at[1, n],
            device_id={"section": section + 1 - 2 * near_bit}, device_id_type=MESH,
        )

    def far_copy(n):
        return pltpu.make_async_remote_copy(
            src_ref=second[n].at[1 - far_bit], dst_ref=third[n], send_sem=z_sems.at[2, n], recv_sem=z_sems.at[3, n],
            device_id={"section": section + 2 - 4 * far_bit}, device_id_type=MESH,
        )

    def near_sum(n):
        for half in range(2):
            both = level[n][half, near_bit].astype(F32) + first[n][half].astype(F32)
            second[n][half] = both.astype(second[n].dtype)

    barrier = pltpu.get_barrier_semaphore()
    for by in range(1, SECTIONS):
        other = (section + by) % SECTIONS
        pl.semaphore_signal(barrier, inc=1, device_id={"section": other}, device_id_type=MESH)
    pl.semaphore_signal(barrier, inc=1, device_id={"dp": partner}, device_id_type=MESH)
    for mask in (1, 2, 3):
        pl.semaphore_signal(barrier, inc=1, device_id={"dp": flipped(mask)[1]}, device_id_type=MESH)
    loads = [pltpu.make_async_copy(keeps[n], kept[n], local_sems.at[n]) for n in range(3)]
    if inner:
        loads += [pltpu.make_async_copy(later[n], level[3 + n], local_sems.at[3 + n]) for n in range(2)]
    for load in loads:
        load.start()
    pl.semaphore_wait(barrier, SECTIONS + 3)

    start, wait = delivery(jobs, arrays, buffers, send_sems, recv_sems)
    redoes = (section == SECTIONS - 1) | (section == 1)
    full = section == SECTIONS - 1
    block = section // 2
    base = SECTIONS - 2 - 2 * block

    def own_copies(part):
        return (
            pltpu.make_async_copy(arrays[SECTIONS + part], acts.at[part], own_sems.at[0]),
            pltpu.make_async_copy(arrays[SECTIONS - 1 - part], dxs.at[part], own_sems.at[1]),
        )

    for part in range(SECTIONS):

        @pl.when(section == part)
        def _(part=part):
            for one in own_copies(part):
                one.start()

    def fetch(row):
        return (
            pltpu.make_async_copy(acts.at[base + row], x_own, redo_sems.at[0]),
            pltpu.make_async_copy(cotangent.at[base + row], g_own, redo_sems.at[1]),
        )

    def fetch_weights():
        return (
            pltpu.make_async_copy(wu_any.at[block], wu, redo_sems.at[2]),
            pltpu.make_async_copy(wd_any.at[block], wd, redo_sems.at[3]),
        )

    def put(row):
        return pltpu.make_async_copy(y_own, acts.at[base + row], redo_sems.at[4])

    def put_grad_rows(row):
        return pltpu.make_async_copy(d_own, dxs.at[base + row], redo_sems.at[5])

    @pl.when(redoes)
    def _():
        for one in fetch(0) + fetch_weights():
            one.start()

    def redo(row):
        for one in fetch(row) + (fetch_weights() if row == 0 else (put(row - 1),)):
            one.wait()

        if row:

            @pl.when(full)
            def _():
                put_grad_rows(row - 1).wait()

        gain = gain_ref[pl.ds(block, 1), :]
        norm_into(x_own, gain, normed)

        def begin_total(rows):
            total[rows, :] = x_own[rows, :].astype(F32) + bd_ref[pl.ds(block, 1), :]

        rows_loop(total.shape[0], 128, begin_total)
        grad[...] = jnp.zeros_like(grad)

        def tile(index, carry):
            cut = pl.ds(pl.multiple_of(index * TILE_F, TILE_F), TILE_F)
            up, down = wu[:, cut], wd[cut, :]
            pre = dot_nn(normed[...], up) + bu_ref[pl.ds(block, 1), cut]
            active, slope = gelu_parts(pre)
            total[...] += dot_nn(active, down)

            @pl.when(full)
            def _():
                low = (dot_nt(g_own[...], down) * slope).astype(BF16)
                grad[...] += dot_nt(low, up)

            return carry

        lax.fori_loop(0, wu.shape[1] // TILE_F, tile, 0)

        def end_total(rows):
            y_own[rows, :] = total[rows, :].astype(BF16)

        rows_loop(total.shape[0], 128, end_total)
        put(row).start()

        @pl.when(full)
        def _():
            norm_backward(x_own, g_own, gain, grad, d_own, dgain)
            put_grad_rows(row).start()

        if row + 1 < FAR:
            for one in fetch(row + 1):
                one.start()

    swaps = []
    for n in range(3):
        swap = pltpu.make_async_remote_copy(
            src_ref=sends[n], dst_ref=got[n], send_sem=core_sems.at[0, n], recv_sem=core_sems.at[1, n],
            device_id={"dp": partner}, device_id_type=MESH,
        )
        swap.start()
        swaps.append(swap)
    start(0, -1)
    for load in loads:
        load.wait()
    near = {}
    if inner:
        near[3] = pltpu.make_async_copy(near_any, first[3], local_sems.at[5])
        near[4] = near_copy(4)
        near[3].start()
        near[4].start()
    moves = []
    for n in range(3):
        swaps[n].wait()
        rows = kept[n].shape[0] // 4
        for mask in (1, 2, 3):
            quarter, device = flipped(mask)
            taken = pl.ds(pl.multiple_of(quarter * rows, rows), rows)
            pair = kept[n][taken, :].astype(F32) + got[n][taken, :].astype(F32)
            parts[n][mask - 1] = pair.astype(parts[n].dtype)
            move = pltpu.make_async_remote_copy(
                src_ref=parts[n].at[mask - 1], dst_ref=landed[n].at[mask - 1],
                send_sem=part_sems.at[0, n, mask - 1], recv_sem=part_sems.at[1, n, mask - 1],
                device_id={"dp": device}, device_id_type=MESH,
            )
            move.start()
            moves.append(move)
    pl.when(redoes)(functools.partial(redo, 0))
    for n in range(3):
        rows = kept[n].shape[0] // 4
        taken = pl.ds(pl.multiple_of(mine * rows, rows), rows)
        summed = kept[n][taken, :].astype(F32) + got[n][taken, :].astype(F32)
        for mask in (1, 2, 3):
            moves[3 * n + mask - 1].wait()
            summed = summed + landed[n][mask - 1].astype(F32)
        if inner:
            share = rows // SECTIONS
            for part in range(SECTIONS):
                level[n][part // 2, part % 2] = summed[part * share : (part + 1) * share].astype(level[n].dtype)
            near[n] = near_copy(n)
            near[n].start()
        else:
            sums[n][...] = summed.astype(sums[n].dtype)
            store = pltpu.make_async_copy(sums[n], outs[n], local_sems.at[n])
            store.start()
            store.wait()
    if not inner:
        start(len(jobs) - 1)
    pl.when(redoes)(functools.partial(redo, 1))
    if inner:
        far = {}
        for n in (3, 4, 0, 1, 2):
            near[n].wait()
            near_sum(n)
            far[n] = far_copy(n)
            far[n].start()
        start(len(jobs) - 1)
        for n in (3, 4, 0, 1, 2):
            far[n].wait()
            block = n // 3
            final = second[n][far_bit].astype(F32) + third[n][...].astype(F32)
            if n == 2:
                outs[4][...] = final
            elif n in (1, 4):
                cand = outs[0].shape[2] // 2
                for at in range(0, final.shape[1], 3 * TILE_C):
                    to = at // 3
                    outs[0][block, :, pl.ds(to, TILE_C)] = final[:, at : at + TILE_C]
                    outs[0][block, :, pl.ds(cand + to, TILE_C)] = final[:, at + TILE_C : at + 2 * TILE_C]
                    outs[1][block, :, pl.ds(to, TILE_C)] = final[:, at + 2 * TILE_C : at + 3 * TILE_C]
            else:
                for at in range(0, final.shape[1], 2 * TILE_F):
                    outs[2][block, :, pl.ds(at // 2, TILE_F)] = final[:, at : at + TILE_F]
                    outs[3][block, :, pl.ds(at // 2, TILE_F)] = final[:, at + TILE_F : at + 2 * TILE_F]

    @pl.when(redoes)
    def _():
        put(1).wait()

    @pl.when(full)
    def _():
        put_grad_rows(1).wait()

    for one in own_copies(0):
        one.wait()
    wait()


def finish(cargo, keeps, sends, later, redo, dp, width):
    inner = later is not None
    columns = [k.shape[1] for k in keeps]
    kinds = [k.dtype for k in keeps]
    rows = keeps[0].shape[0] // 4
    share = rows // SECTIONS
    n_array = len(cargo.arrays)
    jobs = len(cargo.jobs)
    lots = list(zip(columns + columns[:2], kinds + kinds[:2]))
    if inner:
        later = [a.reshape(2, 2, share, -1) for a in later]
        wide = columns[1] // 3
        outs = [shape((2, share, c), F32) for c in (2 * wide, wide, columns[0] // 2, columns[0] // 2)]
        outs += [shape((share, columns[2]), F32)]
        out_specs = [pl.BlockSpec(memory_space=pltpu.VMEM)] * 5
        extra = [pltpu.VMEM((2, 2, share, c), kind) for c, kind in lots]
        extra += [pltpu.VMEM((2, share, c), kind) for c, kind in lots] * 2
        extra += [pltpu.VMEM((share, c), kind) for c, kind in lots]
        extra += [pltpu.SemaphoreType.DMA((4, 5))]
    else:
        later = []
        outs = [shape((rows, c), kind) for c, kind in zip(columns, kinds)]
        out_specs = [ANYWHERE] * 3
        extra = [pltpu.VMEM((rows, c), kind) for c, kind in zip(columns, kinds)]
    n_in = n_array + 6 + len(later)
    return pl.pallas_call(
        functools.partial(last_kernel, cargo.jobs, first_step(dp, width), dp, inner, n_array),
        in_specs=[ANYWHERE] * (n_in + 3) + [pl.BlockSpec(memory_space=pltpu.VMEM)] * 3 + [ANYWHERE] * (2 + inner),
        out_specs=[ANYWHERE] * 2 + out_specs,
        out_shape=[shape(cargo.dims, BF16)] * 2 + outs,
        scratch_shapes=[pltpu.VMEM(k.shape, k.dtype) for k in keeps] * 2
        + [pltpu.VMEM((3, rows, c), kind) for c, kind in zip(columns, kinds)] * 2
        + extra
        + [
            pltpu.SemaphoreType.DMA((jobs,)), pltpu.SemaphoreType.DMA((jobs, SECTIONS)),
            pltpu.SemaphoreType.DMA((6,)), pltpu.SemaphoreType.DMA((2, 3)), pltpu.SemaphoreType.DMA((2, 3, 3)),
        ]
        + [pltpu.VMEM(redo[1].shape[1:], BF16), pltpu.VMEM(redo[2].shape[1:], BF16)]
        + [pltpu.VMEM(cargo.dims[1:], BF16)] * 3 + [pltpu.VMEM(cargo.dims[1:], F32)] * 2
        + [pltpu.VMEM(cargo.dims[1:], BF16)] * 2
        + [pltpu.VMEM((1, width), F32), pltpu.SemaphoreType.DMA((6,)), pltpu.SemaphoreType.DMA((2,))],
        compiler_params=pltpu.CompilerParams(
            vmem_limit_bytes=56 * 1024 * 1024, collective_id=cargo.collective_id, has_side_effects=True
        ),
        input_output_aliases={n_in + 6 + inner: 0, n_in + 7 + inner: 1},
        cost_estimate=cost(1024, 100),
        name="finish",
    )(*cargo.arrays, *keeps, *sends, *later, *redo, *cargo.old)


def hand_out_kernel(counts, summed, up_bias, conv, conv_bias, mix_gain, mlp_gain, down_bias):
    at = 0
    for kind, (rows, columns) in enumerate(counts):
        for row in range(rows):
            piece = summed[at // LANES : at // LANES + 1, at % LANES : at % LANES + columns]
            if kind == 1 and row % 5 == 4:
                conv_bias[row // 5 : row // 5 + 1, :] = piece
            elif kind == 1:
                conv[row // 5, row % 5 : row % 5 + 1, :] = piece
            else:
                (up_bias, None, mix_gain, mlp_gain, down_bias)[kind][row : row + 1, :] = piece
            at += columns


def hand_out(summed, counts):
    wide, narrow = counts[0][1], counts[2][1]
    in_vmem = pl.BlockSpec(memory_space=pltpu.VMEM)
    return pl.pallas_call(
        functools.partial(hand_out_kernel, counts),
        in_specs=[in_vmem],
        out_specs=[in_vmem] * 6,
        out_shape=[
            shape((2, wide), F32), shape((2, 4, wide), F32), shape((2, wide), F32),
            shape((2, narrow), F32), shape((2, narrow), F32), shape((2, narrow), F32),
        ],
        name="hand_out",
    )(summed)


def add_up(pieces):
    return functools.reduce(jnp.add, [piece.astype(F32) for piece in pieces])


def exchange(addends, axis, size, steps):
    where = lax.axis_index(axis)
    own = sum(((where // step) % 2) << k for k, step in enumerate(steps))
    blocks = [a.reshape((1 << len(steps), -1) + a.shape[-1:]) for a in addends]

    def part(which):
        taken = [lax.dynamic_index_in_dim(b, which, 0, keepdims=False) for b in blocks]
        return add_up(taken).astype(addends[0].dtype)

    result = [part(own)]
    for mask in range(1, 1 << len(steps)):
        flip = sum(step for k, step in enumerate(steps) if mask >> k & 1)
        result.append(permute(part(own ^ mask), axis, [(i, i ^ flip) for i in range(size)]))
    return result


def bits_of(size):
    return [1 << k for k in range(size.bit_length() - 1)]


def first_step(dp, width):
    return SPLIT // (width // dp)


def sum_rest(addends, dp, width):
    rest = [step for step in bits_of(dp) if step != first_step(dp, width)][:-2]
    while rest:
        top, rest = rest[-2:], rest[:-2]
        addends = exchange(addends, "dp", dp, top)
    return addends


def sum_section(addends, sections):
    return add_up(exchange(addends, "section", sections, bits_of(sections)))


def body(
    tokens, resets, init_states, cotangent, mix_gain, mix_in, conv_weight, conv_bias, mix_out,
    mlp_gain, mlp_up, up_bias, mlp_down, down_bias,
):
    dp = lax.axis_size("dp")
    sections = lax.axis_size("section")
    section = lax.axis_index("section")
    width = tokens.shape[2]
    bit = ((lax.axis_index("dp") // first_step(dp, width)) % 2).astype(jnp.int32).reshape(1)

    def own(values, axis):
        return lax.dynamic_index_in_dim(values, section, axis, keepdims=False)

    x0 = own(tokens, 0)
    g4 = own(cotangent, 0)
    masks = chunk_masks(own(resets, 0))
    init = own(init_states, 1)
    mixer_weights = (mix_gain, mix_in, conv_weight, conv_bias, mix_out)
    mlp_weights = (mlp_gain, mlp_up, up_bias, mlp_down, down_bias)
    seq = tokens.shape[1]
    dims = (sections, seq, width)
    sent = {}

    def some(source, part, share, buffer=0, senders=None):
        if senders is None:
            senders = tuple(k for k in range(sections) if k != part)
        kind = (buffer, part, senders)
        first = sent.get(kind, 0)
        sent[kind] = first + share
        return (source, part, seq * first // 32, seq * share // 32, buffer, senders)

    distant, close = tuple(range(FAR)), tuple(range(FAR, sections - 1))
    across = tuple(range(FAR, sections))

    def relay(share):
        first = sent.get("relay", 0)
        sent["relay"] = first + share
        return ("relay", 0, seq * first // 32, seq * share // 32, 0, across)

    def early(cross, near, up):
        jobs = []
        if cross:
            jobs.append(some(0, 1, cross, 0, across))
        if near:
            jobs.append(some(0, 0, near, 0, (1,)))
        if up:
            jobs.append(some(1, 1, up, 0, (0,)))
        return jobs

    x1, *stash0, final0 = mixer_forward(0, x0, masks, init, *mixer_weights)
    x2, pre0 = mlp_forward(0, x1, *mlp_weights)
    cargo = Cargo(1, [x1, x2], [None], early(8, 14, 8), dims)
    x3, *stash1, final1, acts = mixer_forward(1, x2, masks, init, *mixer_weights, cargo)
    x4, pre1 = mlp_forward(1, x3, *mlp_weights)

    back_mixer = (mix_gain, mix_in, conv_weight, mix_out, bit)
    back_mlp = (mlp_gain, mlp_up, mlp_down, bit)
    xs = [x1, x2, x3, x4]
    jobs = early(6, 6, 8)
    jobs += [relay(4), some(2, 3, 6, 0, distant), some(2, 2, 4)]
    quarters = jnp.concatenate([final0, final1, jnp.zeros((GROUP - 2, final0.shape[1]), F32)])
    quarters = jnp.split(quarters, sections, axis=1)
    jobs += [some(4 + part, part, 32, 2)[:2] + (0, GROUP, 1) + some(4 + part, part, 32, 3)[5:] for part in range(sections)]
    shapes = [shape(dims, BF16), shape((sections,) + quarters[0].shape, F32)]
    up1, g3, dbu1, dbd1, dgain_mlp1, acts, ends = mlp_backward(
        1, x3, g4, pre1, *back_mlp, False, Cargo(3, xs + quarters, [acts, None], jobs, shapes)
    )
    here = lax.broadcasted_iota(jnp.int32, (sections, 1, 1), 0) == section
    ends = jnp.where(here, lax.dynamic_index_in_dim(jnp.stack(quarters), section, 0), ends)
    final_states = ends[:, :2].transpose(1, 0, 2)
    mlp1 = lax.psum_scatter(up1, "dp", scatter_dimension=0, tiled=True)
    jobs = early(14, 12, 8)
    jobs += [relay(10), some(2, 3, 16, 0, distant), some(3, 3, 6, 0, close)]
    in1, g2, small1, dgain_mix1, acts = mixer_backward(
        1, x2, g3, stash1, masks, init, *back_mixer, False, Cargo(4, xs, [acts], jobs, dims)
    )
    mix1 = lax.psum_scatter(in1, "dp", scatter_dimension=0, tiled=True)
    jobs = early(4, 0, 8)
    jobs += [relay(10), some(2, 3, 10, 0, distant), some(3, 3, 10, 0, close)]
    up0_keep, up0_send, g1, dbu0, dbd0, dgain_mlp0, acts = mlp_backward(
        0, x1, g2, pre0, *back_mlp, True, Cargo(5, xs, [acts], jobs, dims)
    )
    jobs = [relay(8), some(2, 2, 12), some(3, 3, 16, 0, close)]
    jobs += [some(4, 3, 4, 1, close), some(6, 1, 18, 1, across)]
    inner = dp == 8 and first_step(dp, width) == 1
    share = width // (dp * sections)
    g1, mlp1 = after(g1, mlp1)
    sources, buffers, shapes = xs + [g3, g2, g1], [acts, None], [shape(dims, BF16)] * 2
    if inner:
        halved = (2, share, mlp1.shape[1])
        sources.append(mlp1.reshape((2,) + halved))
        buffers.append(None)
        shapes.append(shape(halved, BF16))
        jobs.append((None, 7, 2))
    in0_keep, in0_send, g0, small0, dgain_mix0, acts, dxs, *near1 = mixer_backward(
        0, x0, g1, stash0, masks, init, *back_mixer, True, Cargo(6, sources, buffers, jobs, shapes)
    )
    jobs = [some(3, 0, 32, 1, (2, 3)), some(3, 0, 16, 1, (1,)), some(2, 1, 14, 1, across), some(2, 1, 32, 1, (0,)), some(0, 3, 28, 1, close), some(1, 2, 32, 1), some(6, 2, 16)]
    jobs += [some(3, 0, 16, 1, (1,))]
    cargo = Cargo(7, [g3, g2, g1, g0] + xs, [acts, dxs], jobs, dims)
    redo = (cotangent, mlp_up, mlp_down, mlp_gain, up_bias, down_bias)
    devices = dp * sections
    mix_small = jnp.stack([small0, small1])
    count, tile = mix_small.shape[1], mix_small.shape[3] // 2
    mix_small = mix_small.reshape(2, count, 8, 2, tile).transpose(0, 2, 3, 1, 4).reshape(2, 8, -1)
    lines = [
        jnp.stack([dbu0[0], dbu1[0]]),
        mix_small[:, :5].reshape(10, -1),
        jnp.stack([dgain_mix0[0], dgain_mix1[0]]),
        jnp.stack([dgain_mlp0[0], dgain_mlp1[0]]),
        jnp.stack([dbd0[0], dbd1[0]]),
    ]
    packed = jnp.concatenate(
        [a.reshape(a.shape[0], devices, -1).transpose(1, 0, 2).reshape(devices, -1) for a in lines], axis=1
    )
    share = width // devices
    length = packed.shape[1]
    packed = jnp.pad(packed, ((0, 0), (0, share * LANES - length))).reshape(-1, 2, SPLIT, LANES)

    def half(which):
        return lax.dynamic_index_in_dim(packed, which, 1, keepdims=False).reshape(-1, LANES)

    halves = ((up0_keep, in0_keep, half(bit[0])), (up0_send, in0_send, half(1 - bit[0])))
    if inner:
        acts, dxs, mix_in_grad, mix_out_grad, mlp_up_grad, mlp_down_grad, summed = finish(
            cargo, *halves, (mlp1, mix1), redo + tuple(near1), dp, width
        )
    else:
        acts, dxs, mlp0, mix0, summed = finish(cargo, *halves, None, redo, dp, width)
        parts = [sum_rest([part], dp, width) for part in (mlp0, mix0, summed)] + [[mlp1], [mix1]]
        mlp0, mix0, summed, mlp1, mix1 = [
            sum_section([add_up(part).astype(part[0].dtype)], sections) for part in parts
        ]
        mix_big = jnp.stack([mix0, mix1]).reshape(2, share, -1, 3, TILE_C)
        mix_in_grad = mix_big[:, :, :, :2].transpose(0, 1, 3, 2, 4).reshape(2, share, -1)
        mix_out_grad = mix_big[:, :, :, 2].reshape(2, share, -1)
        mlp_big = jnp.stack([mlp0, mlp1]).reshape(2, share, -1, 2, TILE_F)
        mlp_up_grad = mlp_big[:, :, :, 0].reshape(2, share, -1)
        mlp_down_grad = mlp_big[:, :, :, 1].reshape(2, share, -1)
    mix_out_grad = mix_out_grad.transpose(0, 2, 1)
    mlp_down_grad = mlp_down_grad.transpose(0, 2, 1)

    activations, input_grads = acts[None], dxs[None]

    counts = [(a.shape[0], a.shape[1] // devices) for a in lines]
    if all(LANES % columns == 0 for _, columns in counts) and inner:
        up_bias_grad, conv_grad, conv_bias_grad, mix_gain_grad, mlp_gain_grad, down_bias_grad = hand_out(summed, counts)
    else:
        summed = summed.reshape(-1)[:length]
        pieces, at = [], 0
        for rows, columns in counts:
            pieces.append(summed[at : at + rows * columns].reshape(rows, columns))
            at += rows * columns
        up_bias_grad, conv, mix_gain_grad, mlp_gain_grad, down_bias_grad = pieces
        conv = conv.reshape(2, 5, -1)
        conv_grad, conv_bias_grad = conv[:, :4], conv[:, 4]

    return (
        activations, input_grads, final_states, mix_gain_grad, mix_in_grad, conv_grad, conv_bias_grad,
        mix_out_grad, mlp_gain_grad, mlp_up_grad, up_bias_grad, mlp_down_grad, down_bias_grad,
    )


def solution(mesh):
    both = ("dp", "section")
    return jax.shard_map(
        body,
        mesh=mesh,
        in_specs=(
            P("dp", None, None), P("dp", None), P(None, "dp", None), P("dp", None, None),
            P(), P(), P(), P(), P(), P(), P(), P(), P(), P(),
        ),
        out_specs=(
            P("section", "dp", None, None), P("section", "dp", None, None), P(None, "dp", "section"),
            P(None, both), P(None, both, None), P(None, None, both), P(None, both), P(None, None, both),
            P(None, both), P(None, both, None), P(None, both), P(None, None, both), P(None, both),
        ),
        check_vma=False,
    )
```
